32 devices in a mesh: dp: 2 (over x), fsdp: 16 (over z, y, core).
Axes of the slice: x: 2, y: 2, z: 4, core: 2. Of those that a mesh axis runs over, the one named last changes fastest.
Arguments:
- text_in: bfloat16 [24576, 768], P(('dp', 'fsdp')), may hold values from -6 to 6
- ln_one_gain: bfloat16 [768], P('fsdp'), may hold values from 0.5 to 1.5
- ln_one_bias: bfloat16 [768], P('fsdp'), may hold values from -4 to 4
- qkv_weight: bfloat16 [768, 2304], P('fsdp'), may hold values from -0.21875 to 0.21875
- qv_bias: bfloat16 [1536], P('fsdp'), may hold values from -4 to 4
- out_weight: bfloat16 [768, 768], P('fsdp'), may hold values from -0.875 to 0.875
- out_bias: bfloat16 [768], P('fsdp'), may hold values from -4 to 4
- ln_two_gain: bfloat16 [768], P('fsdp'), may hold values from 0.5 to 1.5
- ln_two_bias: bfloat16 [768], P('fsdp'), may hold values from -4 to 4
- up_weight: bfloat16 [768, 3072], P('fsdp'), may hold values from -0.21875 to 0.21875
- up_bias: bfloat16 [3072], P('fsdp'), may hold values from -4 to 4
- down_weight: bfloat16 [3072, 768], P('fsdp'), may hold values from -0.109375 to 0.109375
- down_bias: bfloat16 [768], P('fsdp'), may hold values from -4 to 4
- image_ln_one_gain: bfloat16 [768], replicated, may hold values from 0.5 to 1.5
- image_ln_one_bias: bfloat16 [768], replicated, may hold values from -4 to 4
- image_qkv_weight: bfloat16 [768, 2304], replicated, may hold values from -0.21875 to 0.21875
- image_qv_bias: bfloat16 [1536], replicated, may hold values from -4 to 4
- image_out_weight: bfloat16 [768, 768], replicated, may hold values from -0.875 to 0.875
- image_out_bias: bfloat16 [768], replicated, may hold values from -4 to 4
- image_ln_two_gain: bfloat16 [768], replicated, may hold values from 0.5 to 1.5
- image_ln_two_bias: bfloat16 [768], replicated, may hold values from -4 to 4
- image_up_weight: bfloat16 [768, 3072], replicated, may hold values from -0.21875 to 0.21875
- image_up_bias: bfloat16 [3072], replicated, may hold values from -4 to 4
- image_down_weight: bfloat16 [3072, 768], replicated, may hold values from -0.109375 to 0.109375
- image_down_bias: bfloat16 [768], replicated, may hold values from -4 to 4
- patches: bfloat16 [1536, 50, 768], P(('dp', 'fsdp')), may hold values from -6 to 6
- targets: bfloat16 [1536, 768], P(('dp', 'fsdp')), may hold values from -6 to 6
- group_ids: int32 [1536], P(('dp', 'fsdp')), may hold values from 0 to 1023
- cap_len: int32 [1536], P(('dp', 'fsdp')), may hold values from 2 to 16, as said below
- slot_counts: int32 [32], P(('dp', 'fsdp')), may hold values from 24 to 48, as said below
Outputs:
- loss: float32 [], replicated
- text_out: bfloat16 [24576, 768], P(('dp', 'fsdp'))
- text_in_grad: float32 [24576, 768], P(('dp', 'fsdp'))
- grad_ln_one_gain: float32 [768], P('fsdp')
- grad_ln_one_bias: float32 [768], P('fsdp')
- grad_qkv_weight: float32 [768, 2304], P('fsdp')
- grad_qv_bias: float32 [1536], P('fsdp')
- grad_out_weight: float32 [768, 768], P('fsdp')
- grad_out_bias: float32 [768], P('fsdp')
- grad_ln_two_gain: float32 [768], P('fsdp')
- grad_ln_two_bias: float32 [768], P('fsdp')
- grad_up_weight: float32 [768, 3072], P('fsdp')
- grad_up_bias: float32 [3072], P('fsdp')
- grad_down_weight: float32 [3072, 768], P('fsdp')
- grad_down_bias: float32 [768], P('fsdp')
The draws below stay inside these ranges and needn't reach their ends.
Inputs may be any that keep to these rules, and one draw needn't show every extreme that they name: `cap_len`: live tokens of each caption; some caption has exactly 16. `slot_counts`: live caption slots of each device come first; some device has all 48 live.
All inputs are finite; a program needn't handle non-finite values.
Results may differ from the reference program's by a relative error of at most 0.0087.
Values may be sent and summed in bfloat16 or wider, within the bound.
A program may use at most 256 MiB of HBM per device.

```python
import math
import jax
import jax.numpy as jnp
import numpy as np
from jax import lax

D = 768
FF = 3072
HEAD = 64
SEQ = 16
PATCHES = 50
CAP_DEV = 48
NGROUPS = 1024
CAPTIONS = 1536
TOKENS = 24576


def draw_cap_len(key, part):
    key = jax.random.fold_in(key, 11)
    first, second = jax.random.split(key)
    lengths = jax.random.randint(first, (CAPTIONS,), 2, SEQ + 1)
    spot = jax.random.randint(second, (), 0, CAPTIONS)
    return jnp.where(jnp.arange(CAPTIONS) == spot, SEQ, lengths).astype(jnp.int32)


def draw_slot_counts(key, part):
    key = jax.random.fold_in(key, 23)
    first, second = jax.random.split(key)
    number = CAPTIONS // CAP_DEV
    counts = jax.random.randint(first, (number,), CAP_DEV // 2, CAP_DEV + 1)
    spot = jax.random.randint(second, (), 0, number)
    return jnp.where(jnp.arange(number) == spot, CAP_DEV, counts).astype(jnp.int32)


def set_ends(result, rng, smallest, high):
    dims = result.shape
    spot = [jax.random.randint(jax.random.fold_in(rng, axis), (), 0, dims[axis]) for axis in range(len(dims))]
    result = result.at[tuple(spot)].set(smallest)
    longest = dims.index(max(dims))
    spot[longest] = (spot[longest] + 1) % dims[longest]
    return result.at[tuple(spot)].set(high)


def block_levels(key, shape, cuts, low, high):
    def one(position, parts):
        heights = jax.random.uniform(jax.random.fold_in(jax.random.fold_in(key, 6), position), (parts,), jnp.float32, low / len(cuts), high / len(cuts))
        return jnp.repeat(jnp.exp(heights), shape[position] // parts).reshape((-1,) + (1,) * (len(shape) - position - 1))

    factor_of = one(*cuts[0])
    for cut in cuts[1:]:
        factor_of = factor_of * one(*cut)
    return factor_of


def cumulative_ranks(amount, slope):
    weights = [(1 << 20) // math.isqrt(standing ** slope) + 1 for standing in range(1, amount + 1)]
    spread = 1 + sum(weights) // (1 << 30)
    return np.cumsum(np.array([max(1, weight // spread) for weight in weights]))


def skewed_ids(rng, shape, amount, skew):
    grid = cumulative_ranks(amount, skew)
    pick = jax.random.randint(jax.random.fold_in(rng, 1), shape, 0, int(grid[amount - 1]))
    standing = jnp.searchsorted(jnp.asarray(grid, jnp.int32), pick, side="right")
    return jax.random.permutation(jax.random.fold_in(rng, 2), amount)[standing].astype(jnp.int32)


def noise(key, dims, deviation, bound, cuts=(), held_as=jnp.bfloat16):
    entries = deviation * jax.random.normal(key, dims, jnp.float32)
    if cuts:
        entries = entries * block_levels(key, dims, cuts, -0.22, 0.18)
    return jnp.clip(entries, -bound, bound).astype(held_as)


def setup_inputs(seed: int = 0) -> dict:
    arg_keys = jax.random.split(jax.random.key(seed), 31)
    text_in = noise(arg_keys[0], (TOKENS, D), 1.0, 6.0, ((0, 32),))
    ln_one_gain = jnp.clip(1.0 + 0.1 * jax.random.normal(arg_keys[1], (D,), jnp.float32), 0.5, 1.5).astype(jnp.bfloat16)
    ln_one_bias = noise(arg_keys[2], (D,), 0.3, 4.0, ((0, 16),))
    qkv_weight = noise(arg_keys[3], (D, 3 * D), D ** -0.5, 0.21875, ((0, 16),))
    qv_bias = noise(arg_keys[4], (2 * D,), 0.3, 4.0, ((0, 16),))
    out_weight = noise(arg_keys[5], (D, D), (D // 16) ** -0.5, 0.875, ((0, 16),))
    out_bias = noise(arg_keys[6], (D,), 0.3, 4.0, ((0, 16),))
    ln_two_gain = jnp.clip(1.0 + 0.1 * jax.random.normal(arg_keys[7], (D,), jnp.float32), 0.5, 1.5).astype(jnp.bfloat16)
    ln_two_bias = noise(arg_keys[8], (D,), 0.3, 4.0, ((0, 16),))
    up_weight = noise(arg_keys[9], (D, FF), D ** -0.5, 0.21875, ((0, 16),))
    up_bias = noise(arg_keys[10], (FF,), 0.3, 4.0, ((0, 16),))
    down_weight = noise(arg_keys[11], (FF, D), FF ** -0.5, 0.109375, ((0, 16),))
    down_bias = noise(arg_keys[12], (D,), 0.3, 4.0, ((0, 16),))
    image_ln_one_gain = jnp.clip(1.0 + 0.1 * jax.random.normal(arg_keys[13], (D,), jnp.float32), 0.5, 1.5).astype(jnp.bfloat16)
    image_ln_one_bias = noise(arg_keys[14], (D,), 0.3, 4.0)
    image_qkv_weight = noise(arg_keys[15], (D, 3 * D), D ** -0.5, 0.21875)
    image_qv_bias = noise(arg_keys[16], (2 * D,), 0.3, 4.0)
    image_out_weight = noise(arg_keys[17], (D, D), (D // 16) ** -0.5, 0.875)
    image_out_bias = noise(arg_keys[18], (D,), 0.3, 4.0)
    image_ln_two_gain = jnp.clip(1.0 + 0.1 * jax.random.normal(arg_keys[19], (D,), jnp.float32), 0.5, 1.5).astype(jnp.bfloat16)
    image_ln_two_bias = noise(arg_keys[20], (D,), 0.3, 4.0)
    image_up_weight = noise(arg_keys[21], (D, FF), D ** -0.5, 0.21875)
    image_up_bias = noise(arg_keys[22], (FF,), 0.3, 4.0)
    image_down_weight = noise(arg_keys[23], (FF, D), FF ** -0.5, 0.109375)
    image_down_bias = noise(arg_keys[24], (D,), 0.3, 4.0)
    patches = noise(arg_keys[25], (CAPTIONS, PATCHES, D), 1.0, 6.0, ((0, 32),))
    targets = noise(arg_keys[26], (CAPTIONS, D), 1.0, 6.0, ((0, 32),))
    group_ids = set_ends(skewed_ids(arg_keys[27], (CAPTIONS,), NGROUPS, 2), jax.random.fold_in(arg_keys[27], 3), 0, NGROUPS - 1).astype(jnp.int32)
    cap_len = draw_cap_len(jax.random.fold_in(arg_keys[30], 71), 0)
    slot_counts = draw_slot_counts(jax.random.fold_in(arg_keys[30], 71), 0)
    return {"text_in": text_in, "ln_one_gain": ln_one_gain, "ln_one_bias": ln_one_bias, "qkv_weight": qkv_weight, "qv_bias": qv_bias, "out_weight": out_weight, "out_bias": out_bias, "ln_two_gain": ln_two_gain, "ln_two_bias": ln_two_bias, "up_weight": up_weight, "up_bias": up_bias, "down_weight": down_weight, "down_bias": down_bias, "image_ln_one_gain": image_ln_one_gain, "image_ln_one_bias": image_ln_one_bias, "image_qkv_weight": image_qkv_weight, "image_qv_bias": image_qv_bias, "image_out_weight": image_out_weight, "image_out_bias": image_out_bias, "image_ln_two_gain": image_ln_two_gain, "image_ln_two_bias": image_ln_two_bias, "image_up_weight": image_up_weight, "image_up_bias": image_up_bias, "image_down_weight": image_down_weight, "image_down_bias": image_down_bias, "patches": patches, "targets": targets, "group_ids": group_ids, "cap_len": cap_len, "slot_counts": slot_counts}


@jax.custom_vjp
def low(v):
    return lax.optimization_barrier(v.astype(jnp.bfloat16)).astype(jnp.float32)

@jax.custom_vjp
def low_back(v):
    return v

def low_keep(v):
    return (low(v), None)

def low_pass(kept, grad):
    return (grad,)

def back_keep(v):
    return (v, None)

def back_low(kept, grad):
    return (low(grad),)
low.defvjp(low_keep, low_pass)
low_back.defvjp(back_keep, back_low)
EPS = 1e-06
ROOT_HALF = 0.7071067811865476
HIGHEST = lax.Precision.HIGHEST

def norm_rows(values):
    centered = values - lax.optimization_barrier(jnp.mean(values, axis=-1, keepdims=True))
    return centered * lax.rsqrt(lax.optimization_barrier(jnp.mean(centered * centered, axis=-1, keepdims=True)) + EPS)

def gelu_exact(values):
    return 0.5 * values * (1.0 + lax.erf(values * ROOT_HALF))

def block_forward(inputs, weights, key_live):
    gain_one, bias_one, w_qkv, b_qv, w_out, b_out, gain_two, bias_two, w_up, b_up, w_down, b_down = weights
    cap, seq, width = inputs.shape
    heads = width // HEAD
    h_one = low(norm_rows(inputs) * gain_one + bias_one)
    filler = jnp.zeros_like(b_out)
    qkv = low(low_back(jnp.matmul(h_one, w_qkv, precision=HIGHEST) + jnp.concatenate([b_qv[:width], filler, b_qv[width:]])))
    qkv = qkv.reshape(cap, seq, 3, heads, HEAD)
    query = qkv[:, :, 0]
    keys = qkv[:, :, 1]
    values = qkv[:, :, 2]
    scores = low_back(jnp.einsum('cqhd,ckhd->chqk', query, keys, precision=HIGHEST) * 0.125)
    scores = jnp.where(key_live[:, None, None, :], scores, -1000000000.0)
    top = lax.optimization_barrier(jnp.max(scores, axis=-1, keepdims=True))
    expo = jnp.exp(scores - top)
    probs = low(expo / lax.optimization_barrier(jnp.sum(expo, axis=-1, keepdims=True)))
    context = low(low_back(jnp.einsum('chqk,ckhd->cqhd', probs, values, precision=HIGHEST))).reshape(cap, seq, width)
    x_one = inputs + low_back(jnp.matmul(context, w_out, precision=HIGHEST) + b_out)
    h_two = low(norm_rows(x_one) * gain_two + bias_two)
    pre = low_back(jnp.matmul(h_two, w_up, precision=HIGHEST) + b_up)
    act = low(gelu_exact(pre))
    return x_one + low_back(jnp.matmul(act, w_down, precision=HIGHEST) + b_down)

def reference(text_in, ln_one_gain, ln_one_bias, qkv_weight, qv_bias, out_weight, out_bias, ln_two_gain, ln_two_bias, up_weight, up_bias, down_weight, down_bias, image_ln_one_gain, image_ln_one_bias, image_qkv_weight, image_qv_bias, image_out_weight, image_out_bias, image_ln_two_gain, image_ln_two_bias, image_up_weight, image_up_bias, image_down_weight, image_down_bias, patches, targets, group_ids, cap_len, slot_counts):
    text_weights = tuple((w.astype(jnp.float32) for w in (ln_one_gain, ln_one_bias, qkv_weight, qv_bias, out_weight, out_bias, ln_two_gain, ln_two_bias, up_weight, up_bias, down_weight, down_bias)))
    image_weights = tuple((w.astype(jnp.float32) for w in (image_ln_one_gain, image_ln_one_bias, image_qkv_weight, image_qv_bias, image_out_weight, image_out_bias, image_ln_two_gain, image_ln_two_bias, image_up_weight, image_up_bias, image_down_weight, image_down_bias)))
    index = jnp.arange(CAPTIONS, dtype=jnp.int32)
    live = index % CAP_DEV < slot_counts[index // CAP_DEV]
    match = group_ids[:, None] == jnp.arange(NGROUPS, dtype=jnp.int32)[None, :]
    group_size = lax.optimization_barrier(jnp.sum(jnp.where(match & live[:, None], 1.0, 0.0).astype(jnp.float32), axis=0))
    members = lax.optimization_barrier(jnp.sum(jnp.where(match, group_size[None, :], 0.0), axis=1))
    weight = jnp.where(live, 1.0 / jnp.maximum(members, 1.0), 0.0).astype(jnp.float32)
    patch_live = jnp.ones((CAP_DEV, PATCHES), dtype=bool)

    def image_block(piece):
        rows = block_forward(piece.astype(jnp.float32), image_weights, patch_live)
        return lax.optimization_barrier(jnp.mean(rows, axis=1))
    image_emb = lax.map(image_block, patches.reshape(CAPTIONS // CAP_DEV, CAP_DEV, PATCHES, D)).reshape(CAPTIONS, D)
    aim = image_emb + targets.astype(jnp.float32)
    key_live = jnp.arange(SEQ, dtype=jnp.int32)[None, :] < cap_len[:, None]
    blocks = CAPTIONS // CAP_DEV
    pieces = (text_in.astype(jnp.float32).reshape(blocks, CAP_DEV, SEQ, D), key_live.reshape(blocks, CAP_DEV, SEQ), weight.reshape(blocks, CAP_DEV), aim.reshape(blocks, CAP_DEV, D))

    def step(carry, piece):
        total, grads = carry
        x_block, live_block, weight_block, aim_block = piece

        def loss_of(weights, inputs):
            rows = block_forward(inputs, weights, live_block)
            live_tokens = live_block.astype(jnp.float32)
            pooled = lax.optimization_barrier(jnp.sum(rows * live_tokens[:, :, None], axis=1)) / lax.optimization_barrier(jnp.sum(live_tokens, axis=1))[:, None]
            error = pooled - aim_block
            return (jnp.sum(weight_block[:, None] * error * error), rows)
        value, pullback, rows = jax.vjp(loss_of, text_weights, x_block, has_aux=True)
        d_weights, d_inputs = pullback(jnp.ones_like(value))
        grads = jax.tree.map(jnp.add, grads, d_weights)
        return ((total + value, grads), (rows.astype(jnp.bfloat16), d_inputs))
    init = (jnp.zeros((), jnp.float32), tuple((jnp.zeros_like(w) for w in text_weights)))
    (loss, grads), (rows, d_inputs) = lax.scan(step, init, pieces)
    return (loss, rows.reshape(TOKENS, D), d_inputs.reshape(TOKENS, D), grads[0], grads[1], grads[2], grads[3], grads[4], grads[5], grads[6], grads[7], grads[8], grads[9], grads[10], grads[11])
```

```python
import functools

import jax
import jax.numpy as jnp
from jax import lax
from jax.experimental import pallas as pl
from jax.experimental.pallas import tpu as pltpu
from jax.sharding import PartitionSpec as P

HEAD = 64
EPS = 1e-06
ROOT_HALF = 0.7071067811865476
INV_ROOT_TAU = 0.3989422804014327
DEAD = -8e9
BF = jnp.bfloat16
F32 = jnp.float32
BLK = 128
TILE = 256
NZ, NY, NC = 4, 2, 2
OWNERS = NZ * NY * NC
MESH = pl.DeviceIdType.MESH
VMEM_LIMIT = 63 * 2**20
LAGS = (-2, 1, 3, 5)
SMALL = ((0, 0), (0, 4), (1, 2), (2, 0), (2, 4))


def norm_rows(values):
    centered = values - jnp.mean(values, axis=-1, keepdims=True)
    inv_std = lax.rsqrt(jnp.mean(centered * centered, axis=-1, keepdims=True) + EPS)
    return centered * inv_std, inv_std


def norm_back(u, n, r):
    return r * (u - jnp.mean(u, axis=-1, keepdims=True) - n * jnp.mean(u * n, axis=-1, keepdims=True))


def gelu_exact(v):
    return 0.5 * v * (1.0 + lax.erf(v * ROOT_HALF))


def dot(a, b):
    return jnp.dot(a, b, preferred_element_type=F32)


def dot_nt(a, b):
    return lax.dot_general(a, b, (((1,), (1,)), ((), ())), preferred_element_type=F32)


def dot_tn(a, b):
    return lax.dot_general(a, b, (((0,), (0,)), ((), ())), preferred_element_type=F32)


def split(v):
    high = v.astype(BF)
    return high, (v - high.astype(F32)).astype(BF)


def row(ref, start=0, size=None):
    size = ref.shape[0] if size is None else size
    return ref[pl.ds(start, size)].astype(F32).reshape(1, size)


def place():
    f = lax.axis_index("fsdp")
    return lax.axis_index("dp"), f // (NY * NC), (f // NC) % NY, f % NC


def device(x, z, y, c):
    return (x, (z * NY + y) * NC + c)


def greet(peers):
    barrier = pltpu.get_barrier_semaphore()
    for peer in peers:
        pl.semaphore_signal(barrier, inc=1, device_id=peer, device_id_type=MESH)
    pl.semaphore_wait(barrier, len(peers))


def remote(src, dst, send, recv, peer):
    return pltpu.make_async_remote_copy(
        src_ref=src, dst_ref=dst, send_sem=send, recv_sem=recv, device_id=peer, device_id_type=MESH
    )


class Gather:
    def __init__(self, g_ref, send, recv):
        self.g, self.send, self.recv = g_ref, send, recv
        self.chunks = g_ref.shape[0]
        half = g_ref.shape[-1] // 2
        self.x, self.z, self.y, self.c = place()
        self.mine = pl.ds(pl.multiple_of(self.x * half, 128), half)
        self.far_z = [device(self.x, (self.z + j) % NZ, self.y, self.c) for j in range(1, NZ)]
        self.near_y = device(self.x, self.z, 1 - self.y, self.c)
        self.near_x = device(1 - self.x, self.z, self.y, self.c)
        self.twin = device(self.x, self.z, self.y, 1 - self.c)
        self.peers = self.far_z + [self.near_y, self.near_x, self.twin]

    def copy(self, k, slot, ref, peer):
        return remote(ref, ref, self.send.at[k, slot], self.recv.at[k, slot], peer)

    def along_z(self, k):
        ref = self.g.at[k, self.z, self.y, self.c, :, self.mine]
        return [self.copy(k, j, ref, peer) for j, peer in enumerate(self.far_z)]

    def first(self, k):
        top, rest = pl.ds(0, 32), pl.ds(32, 16)
        return [self.copy(k, 3, self.g.at[k, :, self.y, self.c, top, self.mine], self.near_y)] + [
            self.copy(k, 4 + j, self.g.at[k, (self.z + 1 + j) % NZ, self.y, self.c, rest, self.mine], self.near_x)
            for j in range(3)
        ]

    def second(self, k):
        top, rest = pl.ds(0, 32), pl.ds(32, 16)
        return (
            [
                self.copy(k, 7 + j, self.g.at[k, (self.z + 1 + j) % NZ, :, self.c, top, self.mine], self.near_x)
                for j in range(3)
            ]
            + [self.copy(k, 10, self.g.at[k, self.z, 1 - self.y, self.c, top, self.mine], self.near_x)]
            + [self.copy(k, 11, self.g.at[k, :, self.y, self.c, rest], self.near_y)]
        )

    def last(self, k):
        return [self.copy(k, 12, self.g.at[k, :, :, self.c], self.twin)]

    def tick(self, t):
        def start(copies):
            for copy in copies:
                copy.start()

        def arrive(copies):
            for copy in copies:
                copy.wait_recv()

        def stage(lag, action):
            @pl.when(jnp.logical_and(t - lag >= 0, t - lag < self.chunks))
            def _():
                action(t - lag)

        def one(k):
            start(self.along_z(k))

        def two(k):
            arrive(self.along_z(k))
            start(self.first(k))

        def three(k):
            arrive(self.first(k))
            start(self.second(k))

        def four(k):
            arrive(self.second(k))
            start(self.last(k))

        stage(LAGS[0], one)
        stage(LAGS[1], two)
        stage(LAGS[2], three)
        stage(LAGS[3], four)

    def finish(self):
        def end(k, _):
            for copy in self.last(k):
                copy.wait()
            for copy in self.along_z(k) + self.first(k) + self.second(k):
                copy.wait_send()
            return 0

        lax.fori_loop(0, self.chunks, end, 0)


def image_body(comm, group, *refs):
    (x_hbm, t_ref, g1, b1, bqv, bout, g2, b2, bup, bdown, wqkv_hbm, wout_hbm, wup_hbm, wdown_hbm), refs = refs[:14], refs[14:]
    if comm:
        (oqkv, oout, oup, odown, ovec, gid, count), refs = refs[:7], refs[7:]
        (aim_ref, gath, vec_ref, wgt_ref), refs = refs[:4], refs[4:]
    else:
        (aim_ref,), refs = refs[:1], refs[1:]
    (x_ref, wqkv, wout, wup, wdown, h_ref, qkv_ref, ctx_ref, act_ref, xm_ref, sems), refs = refs[:11], refs[11:]
    patches, cap, width = x_hbm.shape
    ff = wup.shape[1]
    steps = cap // group
    rows = patches * group
    loads = [
        pltpu.make_async_copy(src, dst, sems.at[i])
        for i, (src, dst) in enumerate(
            [(x_hbm, x_ref), (wqkv_hbm, wqkv), (wout_hbm, wout), (wup_hbm, wup), (wdown_hbm, wdown)]
        )
    ]
    if comm:
        ids, vecs, own_ref, own_sem, g_send, g_recv, s_send, s_recv = refs
        gather = Gather(gath, g_send, g_recv)
        x, z, y, c = gather.x, gather.z, gather.y, gather.c
        own = []
        for k in range(gath.shape[0]):
            if k < 3:
                src = oqkv.at[:, k * width : k * width + width]
            elif k < 4:
                src = oout
            elif k < 8:
                src = oup.at[:, (k - 4) * width : (k - 3) * width]
            else:
                src = odown.at[(k - 8) * oout.shape[0] : (k - 7) * oout.shape[0]]
            own.append((pltpu.make_async_copy(src, own_ref.at[k], own_sem.at[k]), pltpu.make_async_copy(own_ref.at[k], gath.at[k, z, y, c], own_sem.at[k])))
        for copy, _out in own:
            copy.start()
        for load in loads:
            load.start()
        vecs[z, y, c] = ovec[...]
        lane = lax.broadcasted_iota(jnp.int32, (8, 128), 1)
        line = jnp.full((8, 128), -1, jnp.int32)
        for i in range(cap):
            line = jnp.where(lane == i, jnp.where(i < count[0], gid[i], -1), line)
        ids[x, z, y, c] = line
        greet(gather.peers)

        def small(slot, ref, peer):
            return remote(ref, ref, s_send.at[slot], s_recv.at[slot], peer)

        small_z = [small(j, ids.at[x, z, y, c], peer) for j, peer in enumerate(gather.far_z)]
        small_z += [small(3 + j, vecs.at[z, y, c], peer) for j, peer in enumerate(gather.far_z)]
        small_y = [small(6, ids.at[x, :, y, c], gather.near_y), small(7, vecs.at[:, y, c], gather.near_y)]
        small_x = [small(8, ids.at[x, :, :, c], gather.near_x), small(9, vecs.at[:, :, c], gather.twin)]
        small_c = [small(10, ids.at[:, :, :, c], gather.twin)]
        stages = [small_z, small_y, small_x, small_c]
        for copy, out in own:
            copy.wait()
            out.start()
        for _copy, out in own:
            out.wait()
        for k in range(-LAGS[0]):
            for copy in gather.along_z(k):
                copy.start()

        def tick(step, t):
            gather.tick(step * 6 + t)
            for i, (at_step, at) in enumerate(SMALL):
                if at == t:

                    @pl.when(step == at_step)
                    def _():
                        if i > 0:
                            for copy in stages[i - 1]:
                                copy.wait_recv()
                        if i < 4:
                            for copy in stages[i]:
                                copy.start()

    else:
        for load in loads:
            load.start()

        def tick(step, t):
            pass

    lane_q = lax.broadcasted_iota(jnp.int32, (112, 128), 1)
    low_half = lane_q < HEAD
    key = lax.broadcasted_iota(jnp.int32, (224, 128), 1)
    second = lax.broadcasted_iota(jnp.int32, (224, 128), 0) % 112 >= 56
    first_key = jnp.where(second, 64, 0)
    key_ok = (key >= first_key) & (key < first_key + patches)
    ones = jnp.ones((128, 128), BF)
    g1v, b1v, g2v, b2v = row(g1), row(b1), row(g2), row(b2)
    bias = [row(bqv, 0, width), jnp.zeros((1, width), F32), row(bqv, width, width)]
    boutv, bupv, bdownv = row(bout), row(bup), row(bdown)
    xm_ref[...] = jnp.zeros_like(xm_ref)
    for load in loads[:4]:
        load.wait()

    def chunk_step(step, _):
        c0 = pl.multiple_of(step * group, group)
        caps = pl.ds(c0, group)
        tick(step, 0)

        def norm_one(p, _):
            value = x_ref[pl.ds(p * 5, 5), caps, :].astype(F32).reshape(5 * group, width)
            n, _inv = norm_rows(value)
            h_ref[pl.ds(pl.multiple_of(p * 5 * group, 16), 5 * group), :] = (n * g1v + b1v).astype(BF)
            return 0

        lax.fori_loop(0, patches // 5, norm_one, 0)
        for n in range(3 * width // TILE):
            cols = slice(n * TILE, n * TILE + TILE)
            part, off = divmod(n * TILE, width)
            value = dot(h_ref[...], wqkv[:, cols]) + bias[part][:, off : off + TILE]
            qkv_ref[2 * n] = value[:, :128]
            qkv_ref[2 * n + 1] = value[:, 128:]
        tick(step, 1)

        def attend(p, _):
            def load(col, tall):
                parts = []
                for k in range(2):
                    v = qkv_ref[col // 128, pl.ds(2 * p + k, patches, stride=group), :]
                    parts.append(jnp.concatenate([v, jnp.zeros((tall - patches, 128), F32)], axis=0))
                return jnp.concatenate(parts, axis=0).astype(BF)

            for h in range(width // 128):
                q = load(h * 128, 56)
                k = load(width + h * 128, 64)
                v = load(2 * width + h * 128, 64)
                zero = jnp.zeros_like(q)
                q2 = jnp.concatenate([jnp.where(low_half, q, zero), jnp.where(low_half, zero, q)], axis=0)
                s = jnp.where(key_ok, dot_nt(q2, k), DEAD)
                e = jnp.exp((s - jnp.max(s, axis=-1, keepdims=True)) * 0.125).astype(BF)
                o = dot(e, jnp.concatenate([v, ones], axis=1))
                num = jnp.where(low_half, o[:112, :128], o[112:, :128])
                den = jnp.where(low_half, o[:112, 128:], o[112:, 128:])
                out = num / den
                for k in range(2):
                    ctx_ref[h, pl.ds(2 * p + k, patches, stride=group), :] = out[56 * k : 56 * k + patches]
            return 0

        lax.fori_loop(0, group // 4, attend, 0)
        tick(step, 2)
        lax.fori_loop(group // 4, group // 2, attend, 0)
        tick(step, 3)

        def project(p, _):
            span = pl.ds(pl.multiple_of(p * 10 * group, 16), 10 * group)
            ctx = jnp.concatenate([ctx_ref[h, span, :] for h in range(width // 128)], axis=1).astype(BF)
            x1 = x_ref[pl.ds(p * 10, 10), caps, :].astype(F32).reshape(10 * group, width) + dot(ctx, wout[...]) + boutv
            xm_ref[caps, :] += jnp.sum(x1.reshape(10, group, width), axis=0)
            n, _inv = norm_rows(x1)
            h_ref[span, :] = (n * g2v + b2v).astype(BF)
            return 0

        lax.fori_loop(0, patches // 10, project, 0)
        tick(step, 4)
        for n in range(ff // TILE):
            cols = slice(n * TILE, n * TILE + TILE)
            act = gelu_exact(dot(h_ref[...], wup[:, cols]) + bupv[:, cols])
            act_ref[caps, cols] = jnp.sum(act.reshape(patches, group, TILE), axis=0)
            if n == ff // TILE // 2:
                tick(step, 5)
        return 0

    lax.fori_loop(0, steps, chunk_step, 0)
    loads[4].wait()
    both = jnp.concatenate(split(act_ref[...] * (1.0 / patches)), axis=0)
    for n in range(width // TILE):
        cols = slice(n * TILE, n * TILE + TILE)
        o = dot(both, wdown[:, cols])
        aim_ref[:, cols] = (
            o[:cap] + o[cap:] + xm_ref[:, cols] * (1.0 / patches) + bdownv[:, cols] + t_ref[:, cols].astype(F32)
        )
    if comm:
        column = lax.broadcasted_iota(jnp.int32, (cap, 128), 0)
        mine = jnp.zeros((cap, 128), jnp.int32)
        for i in range(cap):
            mine = jnp.where(column == i, gid[i], mine)
        total = jnp.zeros((cap, 128), F32)
        for dx in range(2):
            for o in range(OWNERS):
                line = ids[dx, o // 4, o // 2 % 2, o % 2][0:1]
                total = total + jnp.where(mine == line, 1.0, 0.0)
        members = jnp.sum(total, axis=1, keepdims=True)
        wgt = jnp.where(column < count[0], 1.0 / jnp.maximum(members, 1.0), 0.0)
        wgt_ref[...] = wgt
        vec_ref[...] = vecs[...]
        gather.finish()
        for stage in stages:
            for copy in stage:
                copy.wait_send()


def image_call(patches, targets, weights, extra=(), group=16):
    comm = bool(extra)
    g1, b1, wqkv, bqv, wout, bout, g2, b2, wup, bup, wdown, bdown = weights
    count, cap, width = patches.shape
    ff = wup.shape[1]
    anys = pl.BlockSpec(memory_space=pl.ANY)
    vmem = pl.BlockSpec(memory_space=pltpu.VMEM)
    smem = pl.BlockSpec(memory_space=pltpu.SMEM)
    rows = count * group
    sds = jax.ShapeDtypeStruct
    out_shape = [sds((cap, width), F32)]
    out_specs = [vmem]
    in_specs = [anys] + [vmem] * 9 + [anys] * 4
    scratch = [
        pltpu.VMEM(patches.shape, BF),
        pltpu.VMEM(wqkv.shape, BF),
        pltpu.VMEM(wout.shape, BF),
        pltpu.VMEM(wup.shape, BF),
        pltpu.VMEM(wdown.shape, BF),
        pltpu.VMEM((rows, width), BF),
        pltpu.VMEM((3 * width // 128, rows, 128), F32),
        pltpu.VMEM((width // 128, rows, 128), F32),
        pltpu.VMEM((cap, ff), F32),
        pltpu.VMEM((cap, width), F32),
        pltpu.SemaphoreType.DMA((5,)),
    ]
    params = dict(vmem_limit_bytes=VMEM_LIMIT)
    if comm:
        chunks = 12
        piece = extra[1].shape
        in_specs += [anys] * 4 + [vmem] + [smem] * 2
        out_shape += [
            sds((chunks, NZ, NY, NC) + piece, BF),
            sds((NZ, NY, NC, 16, 128), BF),
            sds((cap, 128), F32),
        ]
        out_specs += [anys, vmem, vmem]
        scratch += [
            pltpu.VMEM((2, NZ, NY, NC, 8, 128), jnp.int32),
            pltpu.VMEM((NZ, NY, NC, 16, 128), BF),
            pltpu.VMEM((chunks,) + piece, BF),
            pltpu.SemaphoreType.DMA((chunks,)),
            pltpu.SemaphoreType.DMA((chunks, 13)),
            pltpu.SemaphoreType.DMA((chunks, 13)),
            pltpu.SemaphoreType.DMA((11,)),
            pltpu.SemaphoreType.DMA((11,)),
        ]
        params.update(collective_id=0, has_side_effects=True)
    return pl.pallas_call(
        functools.partial(image_body, comm, group),
        out_shape=out_shape,
        in_specs=in_specs,
        out_specs=out_specs,
        scratch_shapes=scratch,
        compiler_params=pltpu.CompilerParams(**params),
    )(patches, targets, g1, b1, bqv, bout, g2, b2, bup, bdown, wqkv, wout, wup, wdown, *extra)


class Reduce:
    def __init__(self, half, first_y, first_x, second, third, total, other, sems):
        self.in0, self.in1y, self.in1x, self.in2, self.in3, self.total, self.in4 = (
            half, first_y, first_x, second, third, total, other,
        )
        self.send, self.recv = sems
        self.x, self.z, self.y, self.c = place()
        self.far_z = [device(self.x, (self.z + j) % NZ, self.y, self.c) for j in range(1, NZ)]
        self.near_y = device(self.x, self.z, 1 - self.y, self.c)
        self.near_x = device(1 - self.x, self.z, self.y, self.c)
        self.twin = device(self.x, self.z, self.y, 1 - self.c)
        self.peers = self.far_z + [self.near_y, self.near_x, self.twin]
        self.plans = {}

    def lanes(self, which):
        return pl.ds(pl.multiple_of(which * 384, 128), 384)

    def add(self, k, grad, out, x_first):
        x, z, y, c = self.x, self.z, self.y, self.c
        full = slice(None)
        mine, theirs = self.lanes(x), self.lanes(1 - x)

        def copy(slot, src, dst, peer):
            return remote(src, dst, self.send.at[k, slot], self.recv.at[k, slot], peer)

        c0 = [copy(0, grad(full, full, 1 - c, full), self.in0(k), self.twin)]
        if x_first:
            n = k // 2
            c1 = [copy(1, grad(full, full, c, theirs), self.in1x.at[n], self.near_x)]
            c2 = [copy(2, grad(full, 1 - y, c, mine), self.in2.at[k], self.near_y)]
        else:
            n = k // 2
            c1 = [copy(1, grad(full, 1 - y, c, full), self.in1y.at[n], self.near_y)]
            c2 = [copy(2, grad(full, y, c, theirs), self.in2.at[k], self.near_x)]
        c3 = [
            copy(2 + j, grad((z + j) % NZ, y, c, mine), self.in3.at[k, j - 1], self.far_z[j - 1]) for j in range(1, NZ)
        ]
        c4 = [copy(6, self.total.at[k], self.in4.at[k], self.near_x)]

        def add_into(target, value):
            target[...] = target[...] + value

        def s1():
            c0[0].wait()
            add_into(grad(full, full, c, full), self.in0(k)[...])
            c1[0].start()

        def s2():
            c1[0].wait()
            if x_first:
                add_into(grad(full, full, c, mine), self.in1x[n])
            else:
                add_into(grad(full, y, c, full), self.in1y[n])
            c2[0].start()

        def s3():
            c2[0].wait()
            add_into(grad(full, y, c, mine), self.in2[k])
            for item in c3:
                item.start()

        def s4():
            for item in c3:
                item.wait()
            total = grad(z, y, c, mine)[...].astype(F32)
            for j in range(NZ - 1):
                total = total + self.in3[k, j].astype(F32)
            self.total[k] = total
            out(mine)[...] = total
            c4[0].start()

        def s5():
            c4[0].wait()
            out(theirs)[...] = self.in4[k]

        self.plans[k] = [c0[0].start, s1, s2, s3, s4, s5]

    def run(self, k, stage):
        self.plans[k][stage]()


def text_body(comm, *refs):
    (x_ref, vec_ref, bup_ref, aim_ref, wgt_ref, len_ref, w_hbm), refs = refs[:7], refs[7:]
    if comm:
        (y_hbm, dx_hbm, gvec_ref, gqkv, gout, gup, gdown), refs = refs[:7], refs[7:]
    else:
        (y_hbm, dx_hbm, gvec_ref, grad_hbm), refs = refs[:4], refs[4:]
    (w_ref, wd_ref, h1_ref, qkv_ref, p_ref, ctx_ref, x1_ref, h2_ref, act_ref, slope_ref, asum_ref, lcol_ref, e_ref, et_ref,
     dy_ref, d_ref, da_ref, sems), refs = refs[:18], refs[18:]
    tok, width = x_ref.shape
    cap = aim_ref.shape[0]
    seq = tok // cap
    ff = bup_ref.shape[1]
    blocks = tok // BLK
    pairs = width // 128
    tiles = width // TILE
    piece = w_ref.shape[-2]

    def chunk(k):
        return w_ref.at[k] if k < 8 else wd_ref.at[:, :, :, (k - 8) * piece : (k - 7) * piece]

    loads = [pltpu.make_async_copy(w_hbm.at[k], chunk(k), sems.at[k]) for k in range(12)]
    for load in loads:
        load.start()
    if comm:
        in0_extra, in1y, in1x, in2, in3, totals, in4, vecs, vec_in, vec_z, r_send, r_recv, v_send, v_recv, free = refs
        half = lambda k: slope_half(k)

        def slope_half(k):
            return slope_ref.at[k // 2, k % 2] if k < 8 else in0_extra.at[k - 8]

        red = Reduce(slope_half, in1y, in1x, in2, in3, totals, in4, (r_send, r_recv))
        outs = [gqkv, gqkv, gqkv, gout, gup, gup, gup, gup]

        def view(k):
            if k < 8:
                return lambda a, b, d, lanes: w_ref.at[k, a, b, d, :, lanes]
            rows = slice((k - 8) * piece, (k - 7) * piece)
            return lambda a, b, d, lanes: wd_ref.at[a, b, d, rows, lanes]

        def result(k):
            if k >= 8:
                return lambda lanes: gdown.at[(k - 8) * piece : (k - 7) * piece, lanes]
            base = (k, k, k, 0, 0, 1, 2, 3)[k] if k < 3 else (0 if k == 3 else k - 4)
            return lambda lanes: outs[k].at[:, pl.ds(pl.multiple_of(base * width + lanes.start, 128), lanes.size)]

        for k in range(12):
            red.add(k, view(k), result(k), k % 2 == 1)
        greet(red.peers)
        run = red.run
    else:

        def run(k, stage):
            pass

    vec = lambda i: vec_ref[i : i + 1, :]
    rows_at = lambda b: pl.ds(pl.multiple_of(b * BLK, BLK), BLK)

    for i in range(cap):
        lcol_ref[i : i + 1, :] = jnp.full((1, 128), len_ref[i], jnp.int32)
    lcol = lcol_ref[:, :1]
    t_lane = lax.broadcasted_iota(jnp.int32, (cap, tok), 1)
    c_row = lax.broadcasted_iota(jnp.int32, (cap, tok), 0)
    pool = jnp.where((t_lane // seq == c_row) & (t_lane % seq < lcol), 1.0, 0.0)
    e_ref[...] = pool.astype(BF)
    et_ref[...] = jnp.concatenate([pool, pool, jnp.zeros((128 - 2 * cap, tok), F32)], axis=0).T.astype(BF)
    d_ref[2 * cap :, :] = jnp.zeros_like(d_ref[2 * cap :, :])

    def norm_one(b, _):
        n, _r = norm_rows(x_ref[rows_at(b), :].astype(F32))
        h1_ref[rows_at(b), :] = (n * vec(0) + vec(1)).astype(BF)
        return 0

    lax.fori_loop(0, blocks, norm_one, 0)

    def weight(k, cols):
        return w_ref[k, :, :, :, :, cols].reshape(width, -1)

    for part in range(3):
        loads[part].wait()
        for n in range(tiles):
            cols = slice(n * TILE, n * TILE + TILE)
            value = dot(h1_ref[...], weight(part, cols)) + vec_ref[2 + part : 3 + part, cols]
            qkv_ref[:, part * width + n * TILE : part * width + n * TILE + TILE] = value.astype(BF)

    lane = lax.broadcasted_iota(jnp.int32, (BLK, 128), 1)
    low_half = lane < HEAD
    live_lane = jnp.sum(pool, axis=0, keepdims=True)

    def both_heads(v):
        zero = jnp.zeros_like(v)
        return jnp.concatenate([jnp.where(low_half, v, zero), jnp.where(low_half, zero, v)], axis=0)

    def pick(v):
        return jnp.where(low_half, v[:BLK], v[BLK:])

    same = (lax.broadcasted_iota(jnp.int32, (2 * BLK, BLK), 0) % BLK) // seq == lax.broadcasted_iota(
        jnp.int32, (2 * BLK, BLK), 1
    ) // seq
    for b in range(blocks):
        key_ok = same & (live_lane[:, b * BLK : b * BLK + BLK] > 0.5)
        rows = slice(b * BLK, b * BLK + BLK)
        for h in range(pairs):
            q = qkv_ref[rows, h * 128 : h * 128 + 128]
            k = qkv_ref[rows, width + h * 128 : width + h * 128 + 128]
            v = qkv_ref[rows, 2 * width + h * 128 : 2 * width + h * 128 + 128]
            s = jnp.where(key_ok, dot_nt(both_heads(q), k), DEAD)
            e = jnp.exp((s - jnp.max(s, axis=-1, keepdims=True)) * 0.125)
            p = e / jnp.sum(e, axis=-1, keepdims=True)
            p_ref[b * pairs + h] = p
            ctx_ref[rows, h * 128 : h * 128 + 128] = pick(dot(p.astype(BF), v)).astype(BF)

    loads[3].wait()
    for n in range(tiles):
        cols = slice(n * TILE, n * TILE + TILE)
        x1_ref[:, cols] = x_ref[:, cols].astype(F32) + dot(ctx_ref[...], weight(3, cols)) + vec_ref[5:6, cols]

    def norm_two(b, _):
        n, _r = norm_rows(x1_ref[rows_at(b), :])
        h2_ref[rows_at(b), :] = (n * vec(6) + vec(7)).astype(BF)
        return 0

    lax.fori_loop(0, blocks, norm_two, 0)
    for n in range(ff // TILE):
        k, off = divmod(n * TILE, width)
        if off == 0:
            loads[4 + k].wait()
        cols = slice(n * TILE, n * TILE + TILE)
        inner = slice(off, off + TILE)
        pre = dot(h2_ref[...], weight(4 + k, inner)) + bup_ref[:, cols]
        half_slope = 0.5 * (1.0 + lax.erf(pre * ROOT_HALF))
        act = (pre * half_slope).astype(BF)
        slope = (half_slope + pre * jnp.exp(-0.5 * pre * pre) * INV_ROOT_TAU).astype(BF)
        slope_ref[k, :, :, :, :, inner] = slope.reshape(slope_ref.shape[1:-1] + (TILE,))
        act_ref[:, cols] = act
        hi, lo = split(dot(e_ref[...], act))
        asum_ref[:cap, cols] = hi
        asum_ref[cap:, cols] = lo

    for load in loads[8:]:
        load.wait()
    lens = lcol.astype(F32)
    wgt = wgt_ref[:, :1]
    loss = jnp.zeros((1, TILE), F32)
    for n in range(tiles):
        cols = slice(n * TILE, n * TILE + TILE)
        y = x1_ref[:, cols] + dot(act_ref[...], wd_ref[:, :, :, :, cols].reshape(ff, TILE)) + vec_ref[8:9, cols]
        hi, lo = split(y)
        da_ref[:, cols] = hi
        error = (dot(e_ref[...], hi) + dot(e_ref[...], lo)) / lens - aim_ref[:, cols]
        loss = loss + jnp.sum(wgt * error * error, axis=0, keepdims=True)
        dpool = 2.0 * wgt * error / lens
        dy_hi, dy_lo = split(dpool)
        d_ref[:cap, cols] = dy_hi
        d_ref[cap : 2 * cap, cols] = dy_lo
        gvec_ref[8:9, cols] = jnp.sum(dy_hi.astype(F32) * lens, axis=0, keepdims=True)
    y_out = pltpu.make_async_copy(da_ref, y_hbm, sems.at[12])
    y_out.start()
    gvec_ref[3:4, :] = jnp.zeros((1, width), F32)
    gvec_ref[9:10, :] = jnp.broadcast_to(jnp.sum(loss, axis=1, keepdims=True), (1, width))
    gvec_ref[10:12, :] = jnp.zeros((2, width), F32)

    dm = d_ref[:cap, :]
    span = ff // 8
    for n in range(8):
        cols = slice(n * span, n * span + span)
        hi, lo = split(dot_nt(dm, wd_ref[n // 2, n % 2].reshape(span, width)))
        dmw = dot(et_ref[...], jnp.concatenate([hi, lo, jnp.zeros((128 - 2 * cap, span), BF)], axis=0))
        k, off = divmod(n * span, width)
        slope = slope_ref[k, :, :, :, :, off : off + span].reshape(tok, span)
        dpre = (dmw * slope.astype(F32)).astype(BF)
        gvec_ref[12 + k : 13 + k, off : off + span] = jnp.sum(dpre.astype(F32), axis=0, keepdims=True)
        act_ref[:, cols] = dpre
    if comm:
        pl.semaphore_signal(free, inc=1, device_id=red.twin, device_id_type=MESH)
    dm2 = jnp.concatenate([dm, dm], axis=0)
    per = ff // OWNERS
    for o in range(OWNERS):
        lo, hi = o * per // 128 * 128, (o * per + per + 127) // 128 * 128
        g = dot_tn(asum_ref[:, lo:hi], dm2)
        wd_ref[o // 4, o // 2 % 2, o % 2] = g[o * per - lo : o * per - lo + per].astype(BF)
    for k in range(8, 12):
        run(k, 0)
    for n in range(tiles):
        total = jnp.zeros((tok, TILE), F32)
        for k in range(4):
            w_rows = w_ref[4 + k].reshape(width, width)[n * TILE : n * TILE + TILE]
            total = total + dot_nt(act_ref[:, k * width : k * width + width], w_rows)
        dy_ref[:, n * TILE : n * TILE + TILE] = total
    h2_ref[...] = h2_ref[...].T
    if comm:
        pl.semaphore_wait(free, 1)
    for k in range(4):
        for n in range(tiles):
            cols = slice(n * TILE, n * TILE + TILE)
            g = dot(h2_ref[...], act_ref[:, k * width + n * TILE : k * width + n * TILE + TILE]).astype(BF)
            w_ref[4 + k, :, :, :, :, cols] = g.reshape(w_ref.shape[1:-1] + (TILE,))
        run(4 + k, 0)
        run(8 + k, 1)
    y_out.wait()

    def two_back(b, sums):
        g_gain, g_bias, g_out = sums
        dh = dy_ref[rows_at(b), :]
        n2, r2 = norm_rows(x1_ref[rows_at(b), :])
        dx1 = dot(et_ref[rows_at(b), :], d_ref[...]) + norm_back(dh * vec(6), n2, r2)
        dy_ref[rows_at(b), :] = dx1
        da = dx1.astype(BF)
        da_ref[rows_at(b), :] = da
        return (
            g_gain + jnp.sum(dh * n2, axis=0, keepdims=True),
            g_bias + jnp.sum(dh, axis=0, keepdims=True),
            g_out + jnp.sum(da.astype(F32), axis=0, keepdims=True),
        )

    zero_row = jnp.zeros((1, width), F32)
    sums = lax.fori_loop(0, blocks, two_back, (zero_row,) * 3)
    gvec_ref[6:7, :] = sums[0]
    gvec_ref[7:8, :] = sums[1]
    gvec_ref[5:6, :] = sums[2]
    for k in range(4):
        run(8 + k, 2)
    for n in range(tiles):
        w_rows = w_ref[3].reshape(width, width)[n * TILE : n * TILE + TILE]
        h2_ref[:, n * TILE : n * TILE + TILE] = dot_nt(da_ref[...], w_rows).astype(BF)
    ctx_ref[...] = ctx_ref[...].T
    for n in range(tiles):
        cols = slice(n * TILE, n * TILE + TILE)
        w_ref[3, :, :, :, :, cols] = dot(ctx_ref[...], da_ref[:, cols]).astype(BF).reshape(w_ref.shape[1:-1] + (TILE,))
    run(3, 0)
    for k in range(4):
        run(4 + k, 1)
        run(8 + k, 3)
    for b in range(blocks):
        rows = slice(b * BLK, b * BLK + BLK)
        for h in range(pairs):
            hq = slice(h * 128, h * 128 + 128)
            hk = slice(width + h * 128, width + h * 128 + 128)
            hv = slice(2 * width + h * 128, 2 * width + h * 128 + 128)
            q2 = both_heads(qkv_ref[rows, hq])
            k = qkv_ref[rows, hk]
            v = qkv_ref[rows, hv]
            dc2 = both_heads(h2_ref[rows, hq])
            p = p_ref[b * pairs + h]
            dp = dot_nt(dc2, v)
            ds = (p * (dp - jnp.sum(p * dp, axis=-1, keepdims=True))).astype(BF)
            qkv_ref[rows, hq] = (pick(dot(ds, k)) * 0.125).astype(BF)
            qkv_ref[rows, hk] = (dot_tn(ds, q2) * 0.125).astype(BF)
            qkv_ref[rows, hv] = dot_tn(p.astype(BF), dc2).astype(BF)
    run(3, 1)
    for k in range(4):
        run(4 + k, 2)
        run(8 + k, 4)
    h1_ref[...] = h1_ref[...].T
    for n in range(tiles):
        total = jnp.zeros((tok, TILE), F32)
        for k in range(3):
            w_rows = w_ref[k].reshape(width, width)[n * TILE : n * TILE + TILE]
            total = total + dot_nt(qkv_ref[:, k * width : k * width + width], w_rows)
        x1_ref[:, n * TILE : n * TILE + TILE] = total
    for k in range(3):
        for n in range(tiles):
            cols = slice(n * TILE, n * TILE + TILE)
            d = qkv_ref[:, k * width + n * TILE : k * width + n * TILE + TILE]
            gvec_ref[2 + k : 3 + k, cols] = jnp.sum(d.astype(F32), axis=0, keepdims=True)
            w_ref[k, :, :, :, :, cols] = dot(h1_ref[...], d).astype(BF).reshape(w_ref.shape[1:-1] + (TILE,))
        run(k, 0)

    def one_back(b, sums):
        g_gain, g_bias = sums
        dh = x1_ref[rows_at(b), :]
        n1, r1 = norm_rows(x_ref[rows_at(b), :].astype(F32))
        dy_ref[rows_at(b), :] = dy_ref[rows_at(b), :] + norm_back(dh * vec(0), n1, r1)
        return (g_gain + jnp.sum(dh * n1, axis=0, keepdims=True), g_bias + jnp.sum(dh, axis=0, keepdims=True))

    sums = lax.fori_loop(0, blocks, one_back, (zero_row,) * 2)
    gvec_ref[0:1, :] = sums[0]
    gvec_ref[1:2, :] = sums[1]
    dx_out = pltpu.make_async_copy(dy_ref, dx_hbm, sems.at[13])
    dx_out.start()
    if comm:
        for k in range(3):
            run(k, 1)

        def small(slot, src, dst, peer):
            return remote(src, dst, v_send.at[slot], v_recv.at[slot], peer)

        steps = [
            small(0, vecs.at[0], vec_in.at[0], red.twin),
            small(1, vecs.at[1], vec_in.at[1], red.near_y),
            small(2, vecs.at[2], vec_in.at[2], red.near_x),
        ]
        spread = [small(3 + j, vec_z.at[red.z], vec_z.at[red.z], peer) for j, peer in enumerate(red.far_z)]
        vecs[0] = gvec_ref[...]
        steps[0].start()
        run(3, 2)
        for k in range(4):
            run(4 + k, 3)
            run(8 + k, 5)
        steps[0].wait()
        vecs[1] = vecs[0] + vec_in[0]
        steps[1].start()
        for k in range(3):
            run(k, 2)
        run(3, 3)
        steps[1].wait()
        vecs[2] = vecs[1] + vec_in[1]
        steps[2].start()
        for k in range(4):
            run(4 + k, 4)
        for k in range(3):
            run(k, 3)
        steps[2].wait()
        vec_z[red.z] = vecs[2] + vec_in[2]
        for item in spread:
            item.start()
        run(3, 4)
        for k in range(4):
            run(4 + k, 5)
        for k in range(3):
            run(k, 4)
        for item in spread:
            item.wait()
        gvec_ref[...] = vec_z[0] + vec_z[1] + vec_z[2] + vec_z[3]
        run(3, 5)
        for k in range(3):
            run(k, 5)
    else:
        copies = [pltpu.make_async_copy(chunk(k), grad_hbm.at[k], sems.at[k]) for k in range(12)]
        for copy in copies:
            copy.start()
        for copy in copies:
            copy.wait()
    dx_out.wait()


def text_call(comm, x, vec, bup, aim, wgt, lens, packed):
    tok, width = x.shape
    cap = aim.shape[0]
    ff = bup.shape[1]
    piece = packed.shape[-2]
    anys = pl.BlockSpec(memory_space=pl.ANY)
    vmem = pl.BlockSpec(memory_space=pltpu.VMEM)
    smem = pl.BlockSpec(memory_space=pltpu.SMEM)
    sds = jax.ShapeDtypeStruct
    out_shape = [sds((tok, width), BF), sds((tok, width), F32), sds((16, width), F32)]
    out_specs = [anys, anys, vmem]
    eight = (8, NZ, NY, NC, piece, width)
    scratch = [
        pltpu.VMEM(eight, BF),
        pltpu.VMEM((NZ, NY, NC, 4 * piece, width), BF),
        pltpu.VMEM((tok, width), BF),
        pltpu.VMEM((tok, 3 * width), BF),
        pltpu.VMEM((tok // BLK * (width // 128), 2 * BLK, BLK), F32),
        pltpu.VMEM((tok, width), BF),
        pltpu.VMEM((tok, width), F32),
        pltpu.VMEM((tok, width), BF),
        pltpu.VMEM((tok, ff), BF),
        pltpu.VMEM((ff // width, 2, NZ, NY, tok // 16, width), BF),
        pltpu.VMEM((2 * cap, ff), BF),
        pltpu.VMEM((cap, 128), jnp.int32),
        pltpu.VMEM((cap, tok), BF),
        pltpu.VMEM((tok, 128), BF),
        pltpu.VMEM((tok, width), F32),
        pltpu.VMEM((128, width), BF),
        pltpu.VMEM((tok, width), BF),
        pltpu.SemaphoreType.DMA((14,)),
    ]
    params = dict(vmem_limit_bytes=VMEM_LIMIT)
    if comm:
        out_shape += [
            sds((piece, 3 * width), F32), sds((piece, width), F32), sds((piece, ff), F32), sds((4 * piece, width), F32),
        ]
        out_specs += [vmem] * 4
        scratch += [
            pltpu.VMEM((4, NZ, NY, piece, width), BF),
            pltpu.VMEM((6, NZ, piece, width), BF),
            pltpu.VMEM((6, NZ, NY, piece, width // 2), BF),
            pltpu.VMEM((12, NZ, piece, width // 2), BF),
            pltpu.VMEM((12, NZ - 1, piece, width // 2), BF),
            pltpu.VMEM((12, piece, width // 2), F32),
            pltpu.VMEM((12, piece, width // 2), F32),
            pltpu.VMEM((3, 16, width), F32),
            pltpu.VMEM((3, 16, width), F32),
            pltpu.VMEM((NZ, 16, width), F32),
            pltpu.SemaphoreType.DMA((12, 7)),
            pltpu.SemaphoreType.DMA((12, 7)),
            pltpu.SemaphoreType.DMA((6,)),
            pltpu.SemaphoreType.DMA((6,)),
            pltpu.SemaphoreType.REGULAR,
        ]
        params.update(collective_id=1, has_side_effects=True)
    else:
        out_shape += [sds(packed.shape, BF)]
        out_specs += [anys]
    return pl.pallas_call(
        functools.partial(text_body, comm),
        out_shape=out_shape,
        in_specs=[vmem] * 5 + [smem, anys],
        out_specs=out_specs,
        scratch_shapes=scratch,
        compiler_params=pltpu.CompilerParams(**params),
    )(x, vec, bup, aim, wgt, lens, packed)


def pack(wqkv, wout, wup, wdown):
    width = wout.shape[1]
    parts = [wqkv[:, k * width : (k + 1) * width] for k in range(3)] + [wout]
    parts += [wup[:, k * width : (k + 1) * width] for k in range(4)]
    down = wdown.reshape(OWNERS, 4, width // OWNERS, width)
    parts += [down[:, k].reshape(width, width) for k in range(4)]
    return jnp.stack(parts).reshape(12, NZ, NY, NC, width // OWNERS, width)


def unpack(packed):
    width = packed.shape[-1]
    flat = packed.reshape(12, width, width)
    wqkv = jnp.concatenate([flat[k] for k in range(3)], axis=1)
    wup = jnp.concatenate([flat[4 + k] for k in range(4)], axis=1)
    down = flat[8:].reshape(4, OWNERS, width // OWNERS, width)
    return wqkv, flat[3], wup, jnp.swapaxes(down, 0, 1).reshape(4 * width, width)


def vectors(g1, b1, bqv, bout, g2, b2, bup, bdown):
    width = g1.shape[0]
    zero = jnp.zeros((width,), BF)
    rows = [g1, b1, bqv[:width], zero, bqv[width:], bout, g2, b2, bdown] + [zero] * 7
    return jnp.stack(rows).astype(F32), bup.astype(F32).reshape(1, -1)


def group_weight(group_ids, live):
    match = group_ids[:, None] == jnp.arange(1024, dtype=jnp.int32)[None, :]
    local = jnp.sum(jnp.where(match & live[:, None], 1.0, 0.0).astype(F32), axis=0)
    size = lax.psum(local, ("dp", "fsdp"))
    members = jnp.sum(jnp.where(match, size[None, :], 0.0), axis=1)
    return jnp.where(live, 1.0 / jnp.maximum(members, 1.0), 0.0)


def any_mesh(text, weights, image_weights, patches, targets, group_ids, cap_len, slot_counts):
    cap = targets.shape[0]
    gathered = [lax.all_gather(w, "fsdp", axis=0, tiled=True) for w in weights]
    g1, b1, wqkv, bqv, wout, bout, g2, b2, wup, bup, wdown, bdown = gathered
    live = jnp.arange(cap, dtype=jnp.int32) < slot_counts[0]
    wgt = group_weight(group_ids, live)
    (aim,) = image_call(patches, targets, image_weights)
    vec, bup_row = vectors(g1, b1, bqv, bout, g2, b2, bup, bdown)
    y, dx, gvec, packed = text_call(
        False, text, vec, bup_row, aim, jnp.broadcast_to(wgt[:, None], (cap, 128)), cap_len, pack(wqkv, wout, wup, wdown)
    )
    gqkv, gout, gup, gdown = unpack(packed)
    grads = [
        gvec[0], gvec[1], gqkv, jnp.concatenate([gvec[2], gvec[4]]), gout, gvec[5], gvec[6], gvec[7], gup,
        gvec[12:16].reshape(-1), gdown, gvec[8],
    ]
    owned = [lax.psum_scatter(g.astype(F32), "fsdp", scatter_dimension=0, tiled=True) for g in grads]
    return (lax.psum(gvec[9, 0], ("dp", "fsdp")), y, dx, *[lax.psum(g, "dp") for g in owned])


def block_mesh(text, weights, image_weights, patches, targets, group_ids, cap_len, slot_counts):
    g1, b1, wqkv, bqv, wout, bout, g2, b2, wup, bup, wdown, bdown = weights
    width = wout.shape[1]
    small = jnp.concatenate([g1, b1, bqv, bout, g2, b2, bup, bdown])
    used = small.shape[0]
    small = jnp.pad(small, (0, 2048 - used)).reshape(16, 128)
    aim, packed, all_small, wgt = image_call(
        patches, targets, image_weights, (wqkv, wout, wup, wdown, small, group_ids, slot_counts)
    )
    flat = all_small.reshape(OWNERS, 2048)
    full = []
    start = 0
    for w in (g1, b1, bqv, bout, g2, b2, bup, bdown):
        full.append(flat[:, start : start + w.shape[0]].reshape(-1))
        start += w.shape[0]
    vec, bup_row = vectors(*full)
    y, dx, gvec, gqkv, gout, gup, gdown = text_call(True, text, vec, bup_row, aim, wgt, cap_len, packed)
    me = lax.axis_index("fsdp")
    part = width // OWNERS
    take = lambda v, n: lax.dynamic_slice(v, (me * n,), (n,))
    return (
        gvec[9, 0], y, dx, take(gvec[0], part), take(gvec[1], part), gqkv,
        take(jnp.concatenate([gvec[2], gvec[4]]), 2 * part), gout, take(gvec[5], part), take(gvec[6], part),
        take(gvec[7], part), gup, take(gvec[12:16].reshape(-1), 4 * part), gdown, take(gvec[8], part),
    )


def solution(mesh):
    shape = dict(mesh.shape)
    inner = block_mesh if (shape["dp"], shape["fsdp"]) == (2, OWNERS) else any_mesh

    def per_device(text_in, *rest):
        weights, image_weights = rest[:12], rest[12:24]
        patches, targets, group_ids, cap_len, slot_counts = rest[24:]
        return inner(
            text_in, weights, image_weights, jnp.transpose(patches, (1, 0, 2)), targets, group_ids, cap_len, slot_counts
        )

    both = ("dp", "fsdp")
    owned, table = P("fsdp"), P("fsdp", None)
    text_specs = (owned, owned, table, owned, table, owned, owned, owned, table, owned, table, owned)
    return jax.shard_map(
        per_device,
        mesh=mesh,
        in_specs=(P(both, None), *text_specs, *([P()] * 12), P(both, None, None), P(both, None), P(both), P(both), P(both)),
        out_specs=(P(), P(both, None), P(both, None), *text_specs),
        check_vma=False,
    )
```

```python
import functools

import jax
import jax.numpy as jnp
from jax import lax
from jax.experimental import pallas as pl
from jax.experimental.pallas import tpu as pltpu
from jax.sharding import PartitionSpec as P

HEAD = 64
EPS = 1e-06
ROOT_HALF = 0.7071067811865476
INV_ROOT_TAU = 0.3989422804014327
DEAD = -8e9
BF = jnp.bfloat16
F32 = jnp.float32
BLK = 128
TILE = 256
NZ, NY, NC = 4, 2, 2
OWNERS = NZ * NY * NC
MESH = pl.DeviceIdType.MESH
VMEM_LIMIT = 63 * 2**20
LAGS = (-2, 1, 3, 5)
SPLIT = (0, 3, 4, 6)
WHOLE = (1, 2, 5, 7)
LANDING = {4: 0, 5: 1, 6: 2, 7: 3, 3: 4, 0: 5, 1: 6, 2: 7}
BACK_STEPS = (
    ((3, 1),),
    ((6, 2), (7, 2)),
    ((4, 3),),
    ((5, 3),),
    ((3, 2),),
    ((6, 3), (7, 3)),
)
SMALL = ((0, 0), (0, 4), (1, 2), (2, 0), (2, 4))


def norm_rows(values):
    centered = values - jnp.mean(values, axis=-1, keepdims=True)
    inv_std = lax.rsqrt(jnp.mean(centered * centered, axis=-1, keepdims=True) + EPS)
    return centered * inv_std, inv_std


def norm_back(u, n, r):
    return r * (u - jnp.mean(u, axis=-1, keepdims=True) - n * jnp.mean(u * n, axis=-1, keepdims=True))


def gelu_exact(v):
    return 0.5 * v * (1.0 + lax.erf(v * ROOT_HALF))


def dot(a, b):
    return jnp.dot(a, b, preferred_element_type=F32)


def dot_nt(a, b):
    return lax.dot_general(a, b, (((1,), (1,)), ((), ())), preferred_element_type=F32)


def dot_tn(a, b):
    return lax.dot_general(a, b, (((0,), (0,)), ((), ())), preferred_element_type=F32)


def split(v):
    high = v.astype(BF)
    return high, (v - high.astype(F32)).astype(BF)


def row(ref, start=0, size=None):
    size = ref.shape[0] if size is None else size
    return ref[pl.ds(start, size)].astype(F32).reshape(1, size)


def place():
    f = lax.axis_index("fsdp")
    return lax.axis_index("dp"), f // (NY * NC), (f // NC) % NY, f % NC


def device(x, z, y, c):
    return (x, (z * NY + y) * NC + c)


def greet(peers):
    barrier = pltpu.get_barrier_semaphore()
    for peer in peers:
        pl.semaphore_signal(barrier, inc=1, device_id=peer, device_id_type=MESH)
    pl.semaphore_wait(barrier, len(peers))


def remote(src, dst, send, recv, peer):
    return pltpu.make_async_remote_copy(
        src_ref=src, dst_ref=dst, send_sem=send, recv_sem=recv, device_id=peer, device_id_type=MESH
    )


class Gather:
    def __init__(self, g_ref, send, recv):
        self.g, self.send, self.recv = g_ref, send, recv
        self.chunks = g_ref.shape[0]
        half = g_ref.shape[-1] // 2
        self.x, self.z, self.y, self.c = place()
        self.mine = pl.ds(pl.multiple_of(self.x * half, 128), half)
        self.far_z = [device(self.x, (self.z + j) % NZ, self.y, self.c) for j in range(1, NZ)]
        self.near_y = device(self.x, self.z, 1 - self.y, self.c)
        self.near_x = device(1 - self.x, self.z, self.y, self.c)
        self.twin = device(self.x, self.z, self.y, 1 - self.c)
        self.peers = self.far_z + [self.near_y, self.near_x, self.twin]

    def copy(self, k, slot, ref, peer):
        return remote(ref, ref, self.send.at[k, slot], self.recv.at[k, slot], peer)

    def along_z(self, k):
        ref = self.g.at[k, self.z, self.y, self.c, :, self.mine]
        return [self.copy(k, j, ref, peer) for j, peer in enumerate(self.far_z)]

    def first(self, k):
        top, rest = pl.ds(0, 32), pl.ds(32, 16)
        return [self.copy(k, 3, self.g.at[k, :, self.y, self.c, top, self.mine], self.near_y)] + [
            self.copy(k, 4 + j, self.g.at[k, (self.z + 1 + j) % NZ, self.y, self.c, rest, self.mine], self.near_x)
            for j in range(3)
        ]

    def second(self, k):
        top, rest = pl.ds(0, 32), pl.ds(32, 16)
        return (
            [
                self.copy(k, 7 + j, self.g.at[k, (self.z + 1 + j) % NZ, :, self.c, top, self.mine], self.near_x)
                for j in range(3)
            ]
            + [self.copy(k, 10, self.g.at[k, self.z, 1 - self.y, self.c, top, self.mine], self.near_x)]
            + [self.copy(k, 11, self.g.at[k, :, self.y, self.c, rest], self.near_y)]
        )

    def last(self, k):
        return [self.copy(k, 12, self.g.at[k, :, :, self.c], self.twin)]

    def tick(self, t):
        def start(copies):
            for copy in copies:
                copy.start()

        def arrive(copies):
            for copy in copies:
                copy.wait_recv()

        def stage(lag, action):
            @pl.when(jnp.logical_and(t - lag >= 0, t - lag < self.chunks))
            def _():
                action(t - lag)

        def one(k):
            start(self.along_z(k))

        def two(k):
            arrive(self.along_z(k))
            start(self.first(k))

        def three(k):
            arrive(self.first(k))
            start(self.second(k))

        def four(k):
            arrive(self.second(k))
            start(self.last(k))

        stage(LAGS[0], one)
        stage(LAGS[1], two)
        stage(LAGS[2], three)
        stage(LAGS[3], four)

    def finish(self):
        def end(k, _):
            for copy in self.last(k):
                copy.wait()
            for copy in self.along_z(k) + self.first(k) + self.second(k):
                copy.wait_send()
            return 0

        lax.fori_loop(0, self.chunks, end, 0)


def image_body(comm, group, *refs):
    (x_hbm, t_ref, g1, b1, bqv, bout, g2, b2, bup, bdown, wqkv_hbm, wout_hbm, wup_hbm, wdown_hbm), refs = refs[:14], refs[14:]
    if comm:
        (oqkv, oout, oup, odown, *smalls, gid, count), refs = refs[:14], refs[14:]
        (aim_ref, gath, vec_ref, wgt_ref), refs = refs[:4], refs[4:]
    else:
        (aim_ref,), refs = refs[:1], refs[1:]
    (x_ref, wqkv, wout, wup, wdown, h_ref, qkv_ref, ctx_ref, act_ref, xm_ref, sems), refs = refs[:11], refs[11:]
    patches, cap, width = x_hbm.shape
    ff = wup.shape[1]
    steps = cap // group
    rows = patches * group
    loads = [
        pltpu.make_async_copy(src, dst, sems.at[i])
        for i, (src, dst) in enumerate(
            [(x_hbm, x_ref), (wqkv_hbm, wqkv), (wout_hbm, wout), (wup_hbm, wup), (wdown_hbm, wdown)]
        )
    ]
    if comm:
        ids, vecs, own_ref, own_sem, g_send, g_recv, s_send, s_recv = refs
        gather = Gather(gath, g_send, g_recv)
        x, z, y, c = gather.x, gather.z, gather.y, gather.c
        own = []
        for k in range(gath.shape[0]):
            if k < 3:
                src = oqkv.at[:, k * width : k * width + width]
            elif k < 4:
                src = oout
            elif k < 8:
                src = oup.at[:, (k - 4) * width : (k - 3) * width]
            else:
                src = odown.at[(k - 8) * oout.shape[0] : (k - 7) * oout.shape[0]]
            own.append((pltpu.make_async_copy(src, own_ref.at[k], own_sem.at[k]), pltpu.make_async_copy(own_ref.at[k], gath.at[k, z, y, c], own_sem.at[k])))
        for copy, _out in own:
            copy.start()
        for load in loads:
            load.start()
        lines = []
        for ref in smalls:
            n = ref.shape[0]
            for at in range(0, n, 128):
                take = min(128, n - at)
                line = row(ref)[:, at : at + take]
                lines.append(jnp.concatenate([line, jnp.zeros((1, 128 - take), F32)], axis=1) if take < 128 else line)
        lines.append(jnp.zeros((16 - len(lines), 128), F32))
        vecs[z, y, c] = jnp.concatenate(lines, axis=0).astype(BF)
        lane = lax.broadcasted_iota(jnp.int32, (8, 128), 1)
        line = jnp.full((8, 128), -1, jnp.int32)
        for i in range(cap):
            line = jnp.where(lane == i, jnp.where(i < count[0], gid[i], -1), line)
        ids[x, z, y, c] = line
        greet(gather.peers)

        def small(slot, ref, peer):
            return remote(ref, ref, s_send.at[slot], s_recv.at[slot], peer)

        small_z = [small(j, ids.at[x, z, y, c], peer) for j, peer in enumerate(gather.far_z)]
        small_z += [small(3 + j, vecs.at[z, y, c], peer) for j, peer in enumerate(gather.far_z)]
        small_y = [small(6, ids.at[x, :, y, c], gather.near_y), small(7, vecs.at[:, y, c], gather.near_y)]
        small_x = [small(8, ids.at[x, :, :, c], gather.near_x), small(9, vecs.at[:, :, c], gather.twin)]
        small_c = [small(10, ids.at[:, :, :, c], gather.twin)]
        stages = [small_z, small_y, small_x, small_c]
        for copy, out in own:
            copy.wait()
            out.start()
        for _copy, out in own:
            out.wait()
        for k in range(-LAGS[0]):
            for copy in gather.along_z(k):
                copy.start()

        def tick(step, t):
            gather.tick(step * 6 + t)
            for i, (at_step, at) in enumerate(SMALL):
                if at == t:

                    @pl.when(step == at_step)
                    def _():
                        if i > 0:
                            for copy in stages[i - 1]:
                                copy.wait_recv()
                        if i < 4:
                            for copy in stages[i]:
                                copy.start()

    else:
        for load in loads:
            load.start()

        def tick(step, t):
            pass

    lane_q = lax.broadcasted_iota(jnp.int32, (112, 128), 1)
    low_half = lane_q < HEAD
    key = lax.broadcasted_iota(jnp.int32, (224, 128), 1)
    second = lax.broadcasted_iota(jnp.int32, (224, 128), 0) % 112 >= 56
    first_key = jnp.where(second, 64, 0)
    key_ok = (key >= first_key) & (key < first_key + patches)
    ones = jnp.ones((128, 128), BF)
    g1v, b1v, g2v, b2v = row(g1), row(b1), row(g2), row(b2)
    bias = [row(bqv, 0, width), jnp.zeros((1, width), F32), row(bqv, width, width)]
    boutv, bupv, bdownv = row(bout), row(bup), row(bdown)
    xm_ref[...] = jnp.zeros_like(xm_ref)
    for load in loads[:4]:
        load.wait()

    def chunk_step(step, _):
        c0 = pl.multiple_of(step * group, group)
        caps = pl.ds(c0, group)
        tick(step, 0)

        def norm_one(p, _):
            value = x_ref[pl.ds(p * 5, 5), caps, :].astype(F32).reshape(5 * group, width)
            n, _inv = norm_rows(value)
            h_ref[pl.ds(pl.multiple_of(p * 5 * group, 16), 5 * group), :] = (n * g1v + b1v).astype(BF)
            return 0

        lax.fori_loop(0, patches // 5, norm_one, 0)
        for n in range(3 * width // TILE):
            cols = slice(n * TILE, n * TILE + TILE)
            part, off = divmod(n * TILE, width)
            value = dot(h_ref[...], wqkv[:, cols]) + bias[part][:, off : off + TILE]
            qkv_ref[2 * n] = value[:, :128]
            qkv_ref[2 * n + 1] = value[:, 128:]
        tick(step, 1)

        def attend(p, _):
            def load(col, tall):
                parts = []
                for k in range(2):
                    v = qkv_ref[col // 128, pl.ds(2 * p + k, patches, stride=group), :]
                    parts.append(jnp.concatenate([v, jnp.zeros((tall - patches, 128), F32)], axis=0))
                return jnp.concatenate(parts, axis=0).astype(BF)

            for h in range(width // 128):
                q = load(h * 128, 56)
                k = load(width + h * 128, 64)
                v = load(2 * width + h * 128, 64)
                zero = jnp.zeros_like(q)
                q2 = jnp.concatenate([jnp.where(low_half, q, zero), jnp.where(low_half, zero, q)], axis=0)
                s = jnp.where(key_ok, dot_nt(q2, k), DEAD)
                e = jnp.exp((s - jnp.max(s, axis=-1, keepdims=True)) * 0.125).astype(BF)
                o = dot(e, jnp.concatenate([v, ones], axis=1))
                num = jnp.where(low_half, o[:112, :128], o[112:, :128])
                den = jnp.where(low_half, o[:112, 128:], o[112:, 128:])
                out = num / den
                for k in range(2):
                    ctx_ref[h, pl.ds(2 * p + k, patches, stride=group), :] = out[56 * k : 56 * k + patches]
            return 0

        lax.fori_loop(0, group // 4, attend, 0)
        tick(step, 2)
        lax.fori_loop(group // 4, group // 2, attend, 0)
        tick(step, 3)

        def project(p, _):
            span = pl.ds(pl.multiple_of(p * 10 * group, 16), 10 * group)
            ctx = jnp.concatenate([ctx_ref[h, span, :] for h in range(width // 128)], axis=1).astype(BF)
            x1 = x_ref[pl.ds(p * 10, 10), caps, :].astype(F32).reshape(10 * group, width) + dot(ctx, wout[...]) + boutv
            xm_ref[caps, :] += jnp.sum(x1.reshape(10, group, width), axis=0)
            n, _inv = norm_rows(x1)
            h_ref[span, :] = (n * g2v + b2v).astype(BF)
            return 0

        lax.fori_loop(0, patches // 10, project, 0)
        tick(step, 4)
        for n in range(ff // TILE):
            cols = slice(n * TILE, n * TILE + TILE)
            act = gelu_exact(dot(h_ref[...], wup[:, cols]) + bupv[:, cols])
            act_ref[caps, cols] = jnp.sum(act.reshape(patches, group, TILE), axis=0)
            if n == ff // TILE // 2:
                tick(step, 5)
        return 0

    lax.fori_loop(0, steps, chunk_step, 0)
    loads[4].wait()
    both = jnp.concatenate(split(act_ref[...] * (1.0 / patches)), axis=0)
    for n in range(width // TILE):
        cols = slice(n * TILE, n * TILE + TILE)
        o = dot(both, wdown[:, cols])
        aim_ref[:, cols] = (
            o[:cap] + o[cap:] + xm_ref[:, cols] * (1.0 / patches) + bdownv[:, cols] + t_ref[:, cols].astype(F32)
        )
    if comm:
        column = lax.broadcasted_iota(jnp.int32, (cap, 128), 0)
        mine = jnp.zeros((cap, 128), jnp.int32)
        for i in range(cap):
            mine = jnp.where(column == i, gid[i], mine)
        total = jnp.zeros((cap, 128), F32)
        for dx in range(2):
            for o in range(OWNERS):
                line = ids[dx, o // 4, o // 2 % 2, o % 2][0:1]
                total = total + jnp.where(mine == line, 1.0, 0.0)
        members = jnp.sum(total, axis=1, keepdims=True)
        wgt = jnp.where(column < count[0], 1.0 / jnp.maximum(members, 1.0), 0.0)
        wgt_ref[...] = wgt
        vec_ref[...] = vecs[...]
        gather.finish()
        for stage in stages:
            for copy in stage:
                copy.wait_send()


def image_call(patches, targets, weights, extra=(), group=16):
    comm = bool(extra)
    g1, b1, wqkv, bqv, wout, bout, g2, b2, wup, bup, wdown, bdown = weights
    count, cap, width = patches.shape
    ff = wup.shape[1]
    anys = pl.BlockSpec(memory_space=pl.ANY)
    vmem = pl.BlockSpec(memory_space=pltpu.VMEM)
    smem = pl.BlockSpec(memory_space=pltpu.SMEM)
    rows = count * group
    sds = jax.ShapeDtypeStruct
    out_shape = [sds((cap, width), F32)]
    out_specs = [vmem]
    in_specs = [anys] + [vmem] * 9 + [anys] * 4
    scratch = [
        pltpu.VMEM(patches.shape, BF),
        pltpu.VMEM(wqkv.shape, BF),
        pltpu.VMEM(wout.shape, BF),
        pltpu.VMEM(wup.shape, BF),
        pltpu.VMEM(wdown.shape, BF),
        pltpu.VMEM((rows, width), BF),
        pltpu.VMEM((3 * width // 128, rows, 128), F32),
        pltpu.VMEM((width // 128, rows, 128), F32),
        pltpu.VMEM((cap, ff), F32),
        pltpu.VMEM((cap, width), F32),
        pltpu.SemaphoreType.DMA((5,)),
    ]
    params = dict(vmem_limit_bytes=VMEM_LIMIT)
    if comm:
        chunks = 12
        piece = extra[1].shape
        in_specs += [anys] * 4 + [vmem] * 8 + [smem] * 2
        out_shape += [
            sds((chunks, NZ, NY, NC) + piece, BF),
            sds((NZ, NY, NC, 16, 128), BF),
            sds((cap, 128), F32),
        ]
        out_specs += [anys, vmem, vmem]
        scratch += [
            pltpu.VMEM((2, NZ, NY, NC, 8, 128), jnp.int32),
            pltpu.VMEM((NZ, NY, NC, 16, 128), BF),
            pltpu.VMEM((chunks,) + piece, BF),
            pltpu.SemaphoreType.DMA((chunks,)),
            pltpu.SemaphoreType.DMA((chunks, 13)),
            pltpu.SemaphoreType.DMA((chunks, 13)),
            pltpu.SemaphoreType.DMA((11,)),
            pltpu.SemaphoreType.DMA((11,)),
        ]
        params.update(collective_id=0, has_side_effects=True)
    return pl.pallas_call(
        functools.partial(image_body, comm, group),
        out_shape=out_shape,
        in_specs=in_specs,
        out_specs=out_specs,
        scratch_shapes=scratch,
        compiler_params=pltpu.CompilerParams(**params),
    )(patches, targets, g1, b1, bqv, bout, g2, b2, bup, bdown, wqkv, wout, wup, wdown, *extra)


class Reduce:
    def __init__(self, landing, split_bufs, whole_bufs, sems):
        self.landing, self.split_bufs, self.whole_bufs = landing, split_bufs, whole_bufs
        self.send, self.recv = sems
        self.x, self.z, self.y, self.c = place()
        self.far_z = [device(self.x, (self.z + j) % NZ, self.y, self.c) for j in range(1, NZ)]
        self.near_y = device(self.x, self.z, 1 - self.y, self.c)
        self.near_x = device(1 - self.x, self.z, self.y, self.c)
        self.twin = device(self.x, self.z, self.y, 1 - self.c)
        self.peers = self.far_z + [self.near_y, self.near_x, self.twin]
        self.plans = {}

    def add(self, k, grad, out):
        z, y, c = self.z, self.y, self.c
        full = slice(None)

        def copy(slot, src, dst, peer):
            return remote(src, dst, self.send.at[k, slot], self.recv.at[k, slot], peer)

        def start(items):
            for item in items:
                item.start()

        def wait(items):
            for item in items:
                item.wait()

        def add_into(target, value):
            target[...] = target[...] + value

        landed = self.landing(k)
        c0 = [copy(0, grad(full, full, 1 - c, full), landed, self.twin)]
        if k in WHOLE:
            n = WHOLE.index(k)
            in_y, in_z, mine, other = (buf.at[n] for buf in self.whole_bufs)
            c1 = [copy(1, grad(full, 1 - y, c, full), in_y, self.near_y)]
            c2 = [
                copy(1 + j, grad((z + j) % NZ, y, c, full), in_z.at[j - 1], self.far_z[j - 1]) for j in range(1, NZ)
            ]
            c3 = [copy(5, mine, other, self.near_x)]

            def s1():
                wait(c0)
                add_into(grad(full, full, c, full), landed[...])
                start(c1)

            def s2():
                wait(c1)
                add_into(grad(full, y, c, full), in_y[...])
                start(c2)

            def s3():
                wait(c2)
                total = grad(z, y, c, full)[...].astype(F32)
                for j in range(NZ - 1):
                    total = total + in_z[j].astype(F32)
                mine[...] = total.astype(BF)
                start(c3)

            def s4():
                wait(c3)
                out(pl.ds(0, mine.shape[-1]))[...] = mine[...].astype(F32) + other[...].astype(F32)

            self.plans[k] = [lambda: start(c0), s1, s2, s3, s4]
            return
        n = SPLIT.index(k)
        in_x, in_y, in_z, sum_x, other = (buf.at[n] for buf in self.split_bufs)
        half = sum_x.shape[-1]
        mine = pl.ds(pl.multiple_of(self.x * half, 128), half)
        theirs = pl.ds(pl.multiple_of((1 - self.x) * half, 128), half)
        c1 = [copy(1, grad(full, full, c, theirs), in_x, self.near_x)]
        c2 = [copy(2, grad(full, 1 - y, c, mine), in_y, self.near_y)]
        c3 = [copy(2 + j, grad((z + j) % NZ, y, c, mine), in_z.at[j - 1], self.far_z[j - 1]) for j in range(1, NZ)]
        c4 = [copy(6, sum_x, other, self.near_x)]

        def s1():
            wait(c0)
            add_into(grad(full, full, c, full), landed[...])
            start(c1)

        def s2():
            wait(c1)
            add_into(grad(full, full, c, mine), in_x[...])
            start(c2)

        def s3():
            wait(c2)
            add_into(grad(full, y, c, mine), in_y[...])
            start(c3)

        def s4():
            wait(c3)
            total = grad(z, y, c, mine)[...].astype(F32)
            for j in range(NZ - 1):
                total = total + in_z[j].astype(F32)
            rounded = total.astype(BF)
            sum_x[...] = rounded
            out(mine)[...] = rounded.astype(F32)
            start(c4)

        def s5():
            wait(c4)
            out(theirs)[...] = other[...].astype(F32)

        self.plans[k] = [lambda: start(c0), s1, s2, s3, s4, s5]

    def run(self, k, stage):
        self.plans[k][stage]()


def one_hot(rows, start, width, limit):
    i = lax.broadcasted_iota(jnp.int32, (rows, width), 0)
    j = lax.broadcasted_iota(jnp.int32, (rows, width), 1)
    return jnp.where((j == i + start) & (i < limit), 1.0, 0.0).astype(BF)


def spread_rows(all_small, vec_ref, bup_ref):
    width = vec_ref.shape[1]
    part = width // OWNERS
    tile = lambda o: all_small[o // 4, o // 2 % 2, o % 2]
    plain = jnp.zeros((16, width), F32)
    for o in range(OWNERS):
        plain = plain + dot(tile(o), one_hot(128, o * part, width, part))
    halves = []
    for h in range(2):
        total = jnp.zeros((16, width), F32)
        for m in range(8):
            total = total + dot(tile(8 * h + m), one_hot(128, 2 * m * part, width, 2 * part))
        halves.append(total[2:3])
    zero = jnp.zeros((1, width), F32)
    order = [plain[0:1], plain[1:2], halves[0], zero, halves[1], plain[3:4], plain[4:5], plain[5:6], plain[8:9]]
    vec_ref[...] = jnp.concatenate(order + [jnp.zeros((7, width), F32)], axis=0)
    first = [one_hot(128, 4 * m * part, width, 128) for m in range(4)]
    rest = [one_hot(128, 4 * m * part + 128, width, 4 * part - 128) for m in range(4)]
    for q in range(4):
        total = jnp.zeros((1, width), F32)
        for m in range(4):
            t = tile(4 * q + m)
            total = total + dot(t, first[m])[6:7] + dot(t, rest[m])[7:8]
        bup_ref[:, q * width : (q + 1) * width] = total


def own_rows(gvec, own_ref):
    width = gvec.shape[1]
    part = width // OWNERS
    me = lax.axis_index("fsdp")
    high = gvec.astype(BF)
    left = gvec - high.astype(F32)
    mid = left.astype(BF)
    low = (left - mid.astype(F32)).astype(BF)

    def pick(start, lanes):
        i = lax.broadcasted_iota(jnp.int32, (width, lanes), 0)
        j = lax.broadcasted_iota(jnp.int32, (width, lanes), 1)
        hot = jnp.where(i == j + start, 1.0, 0.0).astype(BF)
        return dot(high, hot) + dot(mid, hot) + dot(low, hot)

    plain = pick(me * part, 256)
    pair = pick(me % 8 * (2 * part), 256)
    four = pick(me % 4 * (4 * part), 256)
    qv = jnp.where(me < 8, pair[2:3], pair[4:5])
    q = me // 4
    bup = jnp.where(q == 0, four[12:13], jnp.where(q == 1, four[13:14], jnp.where(q == 2, four[14:15], four[15:16])))
    loss = jnp.broadcast_to(gvec[9:10, :1], (1, 256))
    rows = [plain[0:1], plain[1:2], qv, plain[5:6], plain[6:7], plain[7:8], plain[8:9], loss, bup]
    own_ref[...] = jnp.concatenate(rows + [jnp.zeros((7, 256), F32)], axis=0)


def text_body(comm, *refs):
    if comm:
        (x_ref, all_small, aim_ref, wgt_ref, len_ref, w_hbm), refs = refs[:6], refs[6:]
    else:
        (x_ref, vec_ref, bup_ref, aim_ref, wgt_ref, len_ref, w_hbm), refs = refs[:7], refs[7:]
    if comm:
        (y_hbm, dx_hbm, own_out, gqkv, gout, gup, gdown), refs = refs[:7], refs[7:]
    else:
        (y_hbm, dx_hbm, gvec_ref, grad_hbm), refs = refs[:4], refs[4:]
    (w_ref, wd_ref, h1_ref, qkv_ref, p_ref, ctx_ref, x1_ref, h2_ref, act_ref, slope_ref, asum_ref, lcol_ref, e_ref, et_ref,
     dy_ref, d_ref, da_ref, dmw_ref, sems), refs = refs[:19], refs[19:]
    tok, width = x_ref.shape
    cap = aim_ref.shape[0]
    seq = tok // cap
    ff = 4 * width
    blocks = tok // BLK
    pairs = width // 128
    tiles = width // TILE
    piece = w_ref.shape[-2]

    def chunk(k):
        return w_ref.at[k] if k < 8 else wd_ref.at[:, :, :, (k - 8) * piece : (k - 7) * piece]

    loads = [pltpu.make_async_copy(w_hbm.at[k], chunk(k), sems.at[k]) for k in range(12)]
    for load in loads:
        load.start()
    if comm:
        vec_ref, bup_ref, gvec_ref, *bufs, vecs, vec_in, vec_z, as0, as1, as2, as3, dms, down_mine, down_in, r_send, r_recv, v_send, v_recv, f_send, f_recv, free = refs
        split_bufs, whole_bufs = bufs[:5], bufs[5:]
        red = Reduce(
            lambda k: slope_ref.at[LANDING[k] // 2, LANDING[k] % 2], split_bufs, whole_bufs, (r_send, r_recv)
        )
        outs = [gqkv, gqkv, gqkv, gout, gup, gup, gup, gup]

        def view(k):
            if k >= 4:
                rows = slice((k - 4) * piece, (k - 3) * piece)
                return lambda a, b, d, lanes: wd_ref.at[a, b, d, rows, lanes]
            n = 3 if k == 3 else 4 + k
            return lambda a, b, d, lanes: w_ref.at[n, a, b, d, :, lanes]

        def result(k):
            base = (0, 1, 2, 0, 0, 1, 2, 3)[k] * width
            return lambda lanes: outs[k].at[:, pl.ds(pl.multiple_of(base + lanes.start, 128), lanes.size)]

        for k in range(8):
            red.add(k, view(k), result(k))
        z, y_at, c = red.z, red.y, red.c

        def side(slot, src, dst, peer):
            return remote(src, dst, f_send.at[slot], f_recv.at[slot], peer)

        to_twin = [side(0, as0.at[:, :, 1 - c], as1.at[:, :, c], red.twin)]
        to_y = [side(1, as1.at[:, 1 - y_at], as2.at[:, y_at], red.near_y)]
        to_z = [side(2 + j, as2.at[(z + 1 + j) % NZ], as3.at[z], peer) for j, peer in enumerate(red.far_z)]
        dm_z = [side(5 + j, dms.at[z, y_at, c], dms.at[z, y_at, c], peer) for j, peer in enumerate(red.far_z)]
        dm_y = [side(8, dms.at[:, y_at, c], dms.at[:, y_at, c], red.near_y)]
        dm_twin = [side(9, dms.at[:, :, c], dms.at[:, :, c], red.twin)]
        down_x = [side(10, down_mine, down_in, red.near_x)]

        def begin(copies):
            for item in copies:
                item.start()

        def end(copies):
            for item in copies:
                item.wait()

        greet(red.peers)
        run = red.run
        spread_rows(all_small, vec_ref, bup_ref)
    else:

        def run(k, stage):
            pass

    vec = lambda i: vec_ref[i : i + 1, :]
    rows_at = lambda b: pl.ds(pl.multiple_of(b * BLK, BLK), BLK)

    for i in range(cap):
        lcol_ref[i : i + 1, :] = jnp.full((1, 128), len_ref[i], jnp.int32)
    lcol = lcol_ref[:, :1]
    t_lane = lax.broadcasted_iota(jnp.int32, (cap, tok), 1)
    c_row = lax.broadcasted_iota(jnp.int32, (cap, tok), 0)
    pool = jnp.where((t_lane // seq == c_row) & (t_lane % seq < lcol), 1.0, 0.0)
    e_ref[...] = pool.astype(BF)
    et_ref[...] = jnp.concatenate([pool, pool, jnp.zeros((128 - 2 * cap, tok), F32)], axis=0).T.astype(BF)
    d_ref[2 * cap :, :] = jnp.zeros_like(d_ref[2 * cap :, :])

    def norm_one(b, _):
        n, _r = norm_rows(x_ref[rows_at(b), :].astype(F32))
        h1_ref[rows_at(b), :] = (n * vec(0) + vec(1)).astype(BF)
        return 0

    lax.fori_loop(0, blocks, norm_one, 0)

    def weight(k, cols):
        return w_ref[k, :, :, :, :, cols].reshape(width, -1)

    for part in range(3):
        loads[part].wait()
        for n in range(tiles):
            cols = slice(n * TILE, n * TILE + TILE)
            value = dot(h1_ref[...], weight(part, cols)) + vec_ref[2 + part : 3 + part, cols]
            qkv_ref[:, part * width + n * TILE : part * width + n * TILE + TILE] = value.astype(BF)

    lane = lax.broadcasted_iota(jnp.int32, (BLK, 128), 1)
    low_half = lane < HEAD
    live_lane = jnp.sum(pool, axis=0, keepdims=True)

    def both_heads(v):
        zero = jnp.zeros_like(v)
        return jnp.concatenate([jnp.where(low_half, v, zero), jnp.where(low_half, zero, v)], axis=0)

    def pick(v):
        return jnp.where(low_half, v[:BLK], v[BLK:])

    same = (lax.broadcasted_iota(jnp.int32, (2 * BLK, BLK), 0) % BLK) // seq == lax.broadcasted_iota(
        jnp.int32, (2 * BLK, BLK), 1
    ) // seq
    for b in range(blocks):
        key_ok = same & (live_lane[:, b * BLK : b * BLK + BLK] > 0.5)
        rows = slice(b * BLK, b * BLK + BLK)
        for h in range(pairs):
            q = qkv_ref[rows, h * 128 : h * 128 + 128]
            k = qkv_ref[rows, width + h * 128 : width + h * 128 + 128]
            v = qkv_ref[rows, 2 * width + h * 128 : 2 * width + h * 128 + 128]
            s = jnp.where(key_ok, dot_nt(both_heads(q), k), DEAD)
            e = jnp.exp((s - jnp.max(s, axis=-1, keepdims=True)) * 0.125)
            p = e / jnp.sum(e, axis=-1, keepdims=True)
            p_ref[b * pairs + h] = p
            ctx_ref[rows, h * 128 : h * 128 + 128] = pick(dot(p.astype(BF), v)).astype(BF)

    loads[3].wait()
    for n in range(tiles):
        cols = slice(n * TILE, n * TILE + TILE)
        x1_ref[:, cols] = x_ref[:, cols].astype(F32) + dot(ctx_ref[...], weight(3, cols)) + vec_ref[5:6, cols]

    def norm_two(b, _):
        n, _r = norm_rows(x1_ref[rows_at(b), :])
        h2_ref[rows_at(b), :] = (n * vec(6) + vec(7)).astype(BF)
        return 0

    lax.fori_loop(0, blocks, norm_two, 0)
    for n in range(ff // TILE):
        k, off = divmod(n * TILE, width)
        if off == 0:
            loads[4 + k].wait()
        cols = slice(n * TILE, n * TILE + TILE)
        inner = slice(off, off + TILE)
        pre = dot(h2_ref[...], weight(4 + k, inner)) + bup_ref[:, cols]
        half_slope = 0.5 * (1.0 + lax.erf(pre * ROOT_HALF))
        act = (pre * half_slope).astype(BF)
        slope = (half_slope + pre * jnp.exp(-0.5 * pre * pre) * INV_ROOT_TAU).astype(BF)
        slope_ref[k, :, :, :, :, inner] = slope.reshape(slope_ref.shape[1:-1] + (TILE,))
        act_ref[:, cols] = act

    for k in range(4):
        total = dot(e_ref[...], act_ref[:, k * width : (k + 1) * width])
        if comm:
            for o in range(4):
                own = total[:, o * 4 * piece : (o + 1) * 4 * piece]
                own = jnp.concatenate([own, jnp.zeros((cap, 256 - 4 * piece), F32)], axis=1)
                as0[k, o // 2, o % 2] = own.astype(BF)
        else:
            hi, lo = split(total)
            asum_ref[:cap, k * width : (k + 1) * width] = hi
            asum_ref[cap:, k * width : (k + 1) * width] = lo
    if comm:
        begin(to_twin)
        as1[:, :, c] = as0[:, :, c]
    h2_ref[...] = h2_ref[...].T
    for load in loads[8:]:
        load.wait()
    lens = lcol.astype(F32)
    wgt = wgt_ref[:, :1]
    loss = jnp.zeros((1, TILE), F32)
    for n in range(tiles):
        cols = slice(n * TILE, n * TILE + TILE)
        y = x1_ref[:, cols] + vec_ref[8:9, cols]
        for k in range(NZ):
            y = y + dot(act_ref[:, k * width : k * width + width], wd_ref[k, :, :, :, cols].reshape(width, TILE))
        hi, lo = split(y)
        da_ref[:, cols] = hi
        error = (dot(e_ref[...], hi) + dot(e_ref[...], lo)) / lens - aim_ref[:, cols]
        loss = loss + jnp.sum(wgt * error * error, axis=0, keepdims=True)
        dpool = 2.0 * wgt * error / lens
        dy_hi, dy_lo = split(dpool)
        d_ref[:cap, cols] = dy_hi
        d_ref[cap : 2 * cap, cols] = dy_lo
        gvec_ref[8:9, cols] = jnp.sum(dy_hi.astype(F32) * lens, axis=0, keepdims=True)
        if comm:
            dms[z, y_at, c, :, cols] = dy_hi
            if n == 1:
                end(to_twin)
                begin(to_y)
                as2[:, y_at] = as1[:, y_at]
            elif n == tiles - 1:
                begin(dm_z)
    y_out = pltpu.make_async_copy(da_ref, y_hbm, sems.at[12])
    y_out.start()
    gvec_ref[3:4, :] = jnp.zeros((1, width), F32)
    gvec_ref[9:10, :] = jnp.broadcast_to(jnp.sum(loss, axis=1, keepdims=True), (1, width))
    gvec_ref[10:12, :] = jnp.zeros((2, width), F32)

    dm = d_ref[:cap, :]
    span = ff // 8
    pad = jnp.zeros((128 - 2 * cap, span), BF)
    for n in range(8):
        hi, lo = split(dot_nt(dm, wd_ref[n // 2, n % 2].reshape(span, width)))
        dmw_ref[:cap, n * span : (n + 1) * span] = hi
        dmw_ref[cap : 2 * cap, n * span : (n + 1) * span] = lo
        dmw_ref[2 * cap :, n * span : (n + 1) * span] = pad
    for k in range(4):
        for n in range(tiles):
            at = k * width + n * TILE
            cols = slice(n * TILE, n * TILE + TILE)
            slope = slope_ref[k, :, :, :, :, cols].reshape(tok, TILE)
            dpre = (dot(et_ref[...], dmw_ref[:, at : at + TILE]) * slope.astype(F32)).astype(BF)
            gvec_ref[12 + k : 13 + k, cols] = jnp.sum(dpre.astype(F32), axis=0, keepdims=True)
            act_ref[:, at : at + TILE] = dpre
            wd_ref[:, :, :, k * piece : (k + 1) * piece, cols] = (
                dot(h2_ref[...], dpre).astype(BF).reshape(NZ, NY, NC, piece, TILE)
            )
        if comm:
            pl.semaphore_signal(free, inc=1, device_id=red.twin, device_id_type=MESH)
            if k == 0:
                end(to_y)
                begin(to_z)
                as3[z] = as2[z]
            if k == 1:
                end(dm_z)
                begin(dm_y)
            if k % 2 == 0:
                pl.semaphore_wait(free, 1)
        run(4 + k, 0)
        if k > 0:
            run(3 + k, 1)
    for n in range(tiles):
        total = jnp.zeros((tok, TILE), F32)
        for k in range(4):
            w_rows = w_ref[4 + k].reshape(width, width)[n * TILE : n * TILE + TILE]
            total = total + dot_nt(act_ref[:, k * width : k * width + width], w_rows)
        dy_ref[:, n * TILE : n * TILE + TILE] = total
        if n == 0:
            run(7, 1)
        elif n == 2:
            run(4, 2)
    if not comm:
        dm2 = jnp.concatenate([dm, dm], axis=0)
        per = ff // OWNERS
        for o in range(OWNERS):
            lo, hi = o * per // 128 * 128, (o * per + per + 127) // 128 * 128
            g = dot_tn(asum_ref[:, lo:hi], dm2)[o * per - lo : o * per - lo + per].astype(BF)
            for k in range(4):
                slope_ref[k, o % 2, o // 4, o // 2 % 2] = g[k * piece : (k + 1) * piece]
    y_out.wait()

    def two_back(b, sums):
        g_gain, g_bias, g_out = sums
        dh = dy_ref[rows_at(b), :]
        n2, r2 = norm_rows(x1_ref[rows_at(b), :])
        dx1 = dot(et_ref[rows_at(b), :], d_ref[...]) + norm_back(dh * vec(6), n2, r2)
        dy_ref[rows_at(b), :] = dx1
        da = dx1.astype(BF)
        da_ref[rows_at(b), :] = da
        return (
            g_gain + jnp.sum(dh * n2, axis=0, keepdims=True),
            g_bias + jnp.sum(dh, axis=0, keepdims=True),
            g_out + jnp.sum(da.astype(F32), axis=0, keepdims=True),
        )

    zero_row = jnp.zeros((1, width), F32)
    sums = lax.fori_loop(0, blocks, two_back, (zero_row,) * 3)
    gvec_ref[6:7, :] = sums[0]
    gvec_ref[7:8, :] = sums[1]
    gvec_ref[5:6, :] = sums[2]
    run(5, 2)
    if comm:
        end(dm_y)
        begin(dm_twin)
    for n in range(tiles):
        w_rows = w_ref[3].reshape(width, width)[n * TILE : n * TILE + TILE]
        h2_ref[:, n * TILE : n * TILE + TILE] = dot_nt(da_ref[...], w_rows).astype(BF)
    ctx_ref[...] = ctx_ref[...].T
    for n in range(tiles):
        cols = slice(n * TILE, n * TILE + TILE)
        w_ref[3, :, :, :, :, cols] = dot(ctx_ref[...], da_ref[:, cols]).astype(BF).reshape(w_ref.shape[1:-1] + (TILE,))
    if comm:
        pl.semaphore_wait(free, 1)
    run(3, 0)
    for b in range(blocks):
        rows = slice(b * BLK, b * BLK + BLK)
        for h in range(pairs):
            hq = slice(h * 128, h * 128 + 128)
            hk = slice(width + h * 128, width + h * 128 + 128)
            hv = slice(2 * width + h * 128, 2 * width + h * 128 + 128)
            q2 = both_heads(qkv_ref[rows, hq])
            k = qkv_ref[rows, hk]
            v = qkv_ref[rows, hv]
            dc2 = both_heads(h2_ref[rows, hq])
            p = p_ref[b * pairs + h]
            dp = dot_nt(dc2, v)
            ds = (p * (dp - jnp.sum(p * dp, axis=-1, keepdims=True))).astype(BF)
            qkv_ref[rows, hq] = (pick(dot(ds, k)) * 0.125).astype(BF)
            qkv_ref[rows, hk] = (dot_tn(ds, q2) * 0.125).astype(BF)
            qkv_ref[rows, hv] = dot_tn(p.astype(BF), dc2).astype(BF)
        for k, stage in BACK_STEPS[b]:
            run(k, stage)
        if comm and b == 2:
            end(dm_twin)
            end(to_z)
            g = dot_tn(as3[...].reshape(OWNERS * cap, 256), dms[...].reshape(OWNERS * cap, width))
            down_mine[...] = g[: 4 * piece].astype(BF)
            begin(down_x)
    h1_ref[...] = h1_ref[...].T
    for k in range(3):
        for n in range(tiles):
            cols = slice(n * TILE, n * TILE + TILE)
            d = qkv_ref[:, k * width + n * TILE : k * width + n * TILE + TILE]
            gvec_ref[2 + k : 3 + k, cols] = jnp.sum(d.astype(F32), axis=0, keepdims=True)
            w_ref[4 + k, :, :, :, :, cols] = dot(h1_ref[...], d).astype(BF).reshape(w_ref.shape[1:-1] + (TILE,))
        if comm and k == 1:
            pl.semaphore_wait(free, 1)
        run(k, 0)
        if k > 0:
            run(k - 1, 1)
    for n in range(tiles):
        total = jnp.zeros((tok, TILE), F32)
        for k in range(3):
            w_rows = w_ref[k].reshape(width, width)[n * TILE : n * TILE + TILE]
            total = total + dot_nt(qkv_ref[:, k * width : k * width + width], w_rows)
        x1_ref[:, n * TILE : n * TILE + TILE] = total
        for k, stage in (((2, 1),), ((3, 3), (4, 4)), ((5, 4), (6, 4)))[n]:
            run(k, stage)

    def one_back(b, sums):
        g_gain, g_bias = sums
        dh = x1_ref[rows_at(b), :]
        n1, r1 = norm_rows(x_ref[rows_at(b), :].astype(F32))
        dy_ref[rows_at(b), :] = dy_ref[rows_at(b), :] + norm_back(dh * vec(0), n1, r1)
        return (g_gain + jnp.sum(dh * n1, axis=0, keepdims=True), g_bias + jnp.sum(dh, axis=0, keepdims=True))

    sums = lax.fori_loop(0, blocks, one_back, (zero_row,) * 2)
    gvec_ref[0:1, :] = sums[0]
    gvec_ref[1:2, :] = sums[1]
    dx_out = pltpu.make_async_copy(dy_ref, dx_hbm, sems.at[13])
    dx_out.start()
    if comm:

        def small(slot, src, dst, peer):
            return remote(src, dst, v_send.at[slot], v_recv.at[slot], peer)

        steps = [
            small(0, vecs.at[0], vec_in.at[0], red.twin),
            small(1, vecs.at[1], vec_in.at[1], red.near_y),
            small(2, vecs.at[2], vec_in.at[2], red.near_x),
        ]
        spread = [small(3 + j, vec_z.at[red.z], vec_z.at[red.z], peer) for j, peer in enumerate(red.far_z)]
        vecs[0] = gvec_ref[...]
        steps[0].start()
        run(0, 2)
        run(1, 2)
        steps[0].wait()
        vecs[1] = vecs[0] + vec_in[0]
        steps[1].start()
        for k, stage in ((3, 4), (7, 4), (4, 5), (6, 5), (2, 2)):
            run(k, stage)
        steps[1].wait()
        vecs[2] = vecs[1] + vec_in[1]
        steps[2].start()
        run(0, 3)
        run(1, 3)
        end(down_x)
        gdown[...] = down_mine[...].astype(F32) + down_in[...].astype(F32)
        steps[2].wait()
        vec_z[red.z] = vecs[2] + vec_in[2]
        for item in spread:
            item.start()
        run(2, 3)
        run(3, 5)
        run(1, 4)
        run(0, 4)
        for item in spread:
            item.wait()
        own_rows(vec_z[0] + vec_z[1] + vec_z[2] + vec_z[3], own_out)
        run(2, 4)
        run(0, 5)
    else:
        copies = [pltpu.make_async_copy(w_ref.at[3 if k == 3 else 4 + k], grad_hbm.at[k], sems.at[k]) for k in range(4)]
        for k in range(4):
            rows = slice(k * piece, (k + 1) * piece)
            copies.append(pltpu.make_async_copy(wd_ref.at[:, :, :, rows], grad_hbm.at[4 + k], sems.at[4 + k]))
            for c in range(NC):
                copies.append(
                    pltpu.make_async_copy(slope_ref.at[k, c], grad_hbm.at[8 + k, :, :, c], sems.at[14 + 2 * k + c])
                )
        for copy in copies:
            copy.start()
        for copy in copies:
            copy.wait()
    dx_out.wait()


def text_call(comm, x, smalls, aim, wgt, lens, packed):
    tok, width = x.shape
    cap = aim.shape[0]
    ff = 4 * width
    piece = packed.shape[-2]
    anys = pl.BlockSpec(memory_space=pl.ANY)
    vmem = pl.BlockSpec(memory_space=pltpu.VMEM)
    smem = pl.BlockSpec(memory_space=pltpu.SMEM)
    sds = jax.ShapeDtypeStruct
    out_shape = [sds((tok, width), BF), sds((tok, width), F32), sds((16, 256 if comm else width), F32)]
    out_specs = [anys, anys, vmem]
    eight = (8, NZ, NY, NC, piece, width)
    scratch = [
        pltpu.VMEM(eight, BF),
        pltpu.VMEM((NZ, NY, NC, 4 * piece, width), BF),
        pltpu.VMEM((tok, width), BF),
        pltpu.VMEM((tok, 3 * width), BF),
        pltpu.VMEM((tok // BLK * (width // 128), 2 * BLK, BLK), F32),
        pltpu.VMEM((tok, width), BF),
        pltpu.VMEM((tok, width), F32),
        pltpu.VMEM((tok, width), BF),
        pltpu.VMEM((tok, ff), BF),
        pltpu.VMEM((ff // width, 2, NZ, NY, tok // 16, width), BF),
        pltpu.VMEM((2 * cap, ff), BF),
        pltpu.VMEM((cap, 128), jnp.int32),
        pltpu.VMEM((cap, tok), BF),
        pltpu.VMEM((tok, 128), BF),
        pltpu.VMEM((tok, width), F32),
        pltpu.VMEM((128, width), BF),
        pltpu.VMEM((tok, width), BF),
        pltpu.VMEM((128, ff), BF),
        pltpu.SemaphoreType.DMA((22,)),
    ]
    params = dict(vmem_limit_bytes=VMEM_LIMIT)
    if comm:
        out_shape += [
            sds((piece, 3 * width), F32), sds((piece, width), F32), sds((piece, ff), F32), sds((4 * piece, width), F32),
        ]
        out_specs += [vmem] * 4
        scratch += [
            pltpu.VMEM((16, width), F32),
            pltpu.VMEM((1, ff), F32),
            pltpu.VMEM((16, width), F32),
            pltpu.VMEM((4, NZ, NY, piece, width // 2), BF),
            pltpu.VMEM((4, NZ, piece, width // 2), BF),
            pltpu.VMEM((4, NZ - 1, piece, width // 2), BF),
            pltpu.VMEM((4, piece, width // 2), BF),
            pltpu.VMEM((4, piece, width // 2), BF),
            pltpu.VMEM((4, NZ, piece, width), BF),
            pltpu.VMEM((4, NZ - 1, piece, width), BF),
            pltpu.VMEM((4, piece, width), BF),
            pltpu.VMEM((4, piece, width), BF),
            pltpu.VMEM((3, 16, width), F32),
            pltpu.VMEM((3, 16, width), F32),
            pltpu.VMEM((NZ, 16, width), F32),
            *[pltpu.VMEM((NZ, NY, NC, cap, 256), BF)] * 4,
            pltpu.VMEM((NZ, NY, NC, cap, width), BF),
            pltpu.VMEM((4 * piece, width), BF),
            pltpu.VMEM((4 * piece, width), BF),
            pltpu.SemaphoreType.DMA((8, 7)),
            pltpu.SemaphoreType.DMA((8, 7)),
            pltpu.SemaphoreType.DMA((6,)),
            pltpu.SemaphoreType.DMA((6,)),
            pltpu.SemaphoreType.DMA((11,)),
            pltpu.SemaphoreType.DMA((11,)),
            pltpu.SemaphoreType.REGULAR,
        ]
        params.update(collective_id=1, has_side_effects=True)
    else:
        out_shape += [sds(packed.shape, BF)]
        out_specs += [anys]
    return pl.pallas_call(
        functools.partial(text_body, comm),
        out_shape=out_shape,
        in_specs=[vmem] * (3 + len(smalls)) + [smem, anys],
        out_specs=out_specs,
        scratch_shapes=scratch,
        compiler_params=pltpu.CompilerParams(**params),
    )(x, *smalls, aim, wgt, lens, packed)


def pack(wqkv, wout, wup, wdown):
    width = wout.shape[1]
    parts = [wqkv[:, k * width : (k + 1) * width] for k in range(3)] + [wout]
    parts += [wup[:, k * width : (k + 1) * width] for k in range(4)]
    down = wdown.reshape(OWNERS, 4, width // OWNERS, width)
    parts += [down[:, k].reshape(width, width) for k in range(4)]
    return jnp.stack(parts).reshape(12, NZ, NY, NC, width // OWNERS, width)


def unpack(packed):
    width = packed.shape[-1]
    flat = packed.reshape(12, width, width)
    wqkv = jnp.concatenate([flat[k] for k in range(3)], axis=1)
    wup = jnp.concatenate([flat[4 + k] for k in range(4)], axis=1)
    down = flat[8:].reshape(4, OWNERS, width // OWNERS, width)
    return wqkv, flat[3], wup, jnp.swapaxes(down, 0, 1).reshape(4 * width, width)


def vectors(g1, b1, bqv, bout, g2, b2, bup, bdown):
    width = g1.shape[0]
    zero = jnp.zeros((width,), BF)
    rows = [g1, b1, bqv[:width], zero, bqv[width:], bout, g2, b2, bdown] + [zero] * 7
    return jnp.stack(rows).astype(F32), bup.astype(F32).reshape(1, -1)


def hand_out_body(part, *refs):
    big, own, outs, bufs, sem_in, sem_out = refs[:6], refs[6], refs[7:22], refs[22:28], refs[28], refs[29]
    loss, y, dx, g1, b1, gqkv, qv, gout, bout, g2, b2, gup, bup, gdown, bdown = outs
    pairs = list(zip(big, bufs, (y, dx, gqkv, gout, gup, gdown)))
    ins, backs = [], []
    for i, (src, buf, dst) in enumerate(pairs):
        pieces = 4 if i < 2 else 1
        n = src.shape[0] // pieces
        for p in range(pieces):
            rows = pl.ds(p * n, n)
            slot = 4 * i + p
            ins.append(pltpu.make_async_copy(src.at[rows], buf.at[rows], sem_in.at[slot]))
            backs.append(pltpu.make_async_copy(buf.at[rows], dst.at[rows], sem_out.at[slot]))
    for copy in ins:
        copy.start()
    for ref, at, lanes in (
        (g1, 0, part), (b1, 1, part), (qv, 2, 2 * part), (bout, 3, part), (g2, 4, part), (b2, 5, part), (bdown, 6, part),
        (bup, 8, 4 * part),
    ):
        ref[...] = own[at : at + 1, :lanes].reshape(lanes)
    loss[...] = own[7:8, :1]
    for copy, back in zip(ins, backs):
        copy.wait()
        back.start()
    for back in backs:
        back.wait()


def hand_out(big, own, part):
    sds = jax.ShapeDtypeStruct
    anys = pl.BlockSpec(memory_space=pl.ANY)
    vmem = pl.BlockSpec(memory_space=pltpu.VMEM)
    like = lambda v: sds(v.shape, v.dtype)
    line = lambda n: sds((n * part,), F32)
    y, dx, gqkv, gout, gup, gdown = big
    return pl.pallas_call(
        functools.partial(hand_out_body, part),
        out_shape=[
            sds((1, 1), F32), like(y), like(dx), line(1), line(1), like(gqkv), line(2), like(gout), line(1), line(1),
            line(1), like(gup), line(4), like(gdown), line(1),
        ],
        in_specs=[anys] * 6 + [vmem],
        out_specs=[vmem, anys, anys, vmem, vmem, anys, vmem, anys, vmem, vmem, vmem, anys, vmem, anys, vmem],
        scratch_shapes=[pltpu.VMEM(v.shape, v.dtype) for v in big]
        + [pltpu.SemaphoreType.DMA((24,)), pltpu.SemaphoreType.DMA((24,))],
        compiler_params=pltpu.CompilerParams(vmem_limit_bytes=VMEM_LIMIT),
    )(*big, own)


def group_weight(group_ids, live):
    match = group_ids[:, None] == jnp.arange(1024, dtype=jnp.int32)[None, :]
    local = jnp.sum(jnp.where(match & live[:, None], 1.0, 0.0).astype(F32), axis=0)
    size = lax.psum(local, ("dp", "fsdp"))
    members = jnp.sum(jnp.where(match, size[None, :], 0.0), axis=1)
    return jnp.where(live, 1.0 / jnp.maximum(members, 1.0), 0.0)


def any_mesh(text, weights, image_weights, patches, targets, group_ids, cap_len, slot_counts):
    cap = targets.shape[0]
    gathered = [lax.all_gather(w, "fsdp", axis=0, tiled=True) for w in weights]
    g1, b1, wqkv, bqv, wout, bout, g2, b2, wup, bup, wdown, bdown = gathered
    live = jnp.arange(cap, dtype=jnp.int32) < slot_counts[0]
    wgt = group_weight(group_ids, live)
    (aim,) = image_call(patches, targets, image_weights)
    vec, bup_row = vectors(g1, b1, bqv, bout, g2, b2, bup, bdown)
    y, dx, gvec, packed = text_call(
        False, text, (vec, bup_row), aim, jnp.broadcast_to(wgt[:, None], (cap, 128)), cap_len, pack(wqkv, wout, wup, wdown)
    )
    gqkv, gout, gup, gdown = unpack(packed)
    grads = [
        gvec[0], gvec[1], gqkv, jnp.concatenate([gvec[2], gvec[4]]), gout, gvec[5], gvec[6], gvec[7], gup,
        gvec[12:16].reshape(-1), gdown, gvec[8],
    ]
    owned = [lax.psum_scatter(g.astype(F32), "fsdp", scatter_dimension=0, tiled=True) for g in grads]
    return (lax.psum(gvec[9, 0], ("dp", "fsdp")), y, dx, *[lax.psum(g, "dp") for g in owned])


def block_mesh(text, weights, image_weights, patches, targets, group_ids, cap_len, slot_counts):
    g1, b1, wqkv, bqv, wout, bout, g2, b2, wup, bup, wdown, bdown = weights
    width = wout.shape[1]
    aim, packed, all_small, wgt = image_call(
        patches, targets, image_weights, (wqkv, wout, wup, wdown, g1, b1, bqv, bout, g2, b2, bup, bdown, group_ids, slot_counts)
    )
    y, dx, gvec, gqkv, gout, gup, gdown = text_call(True, text, (all_small,), aim, wgt, cap_len, packed)
    part = width // OWNERS
    loss, y, dx, g1, b1, gqkv, qv, gout, bout, g2, b2, gup, bup, gdown, bdown = hand_out(
        (y, dx, gqkv, gout, gup, gdown), gvec, part
    )
    return loss[0, 0], y, dx, g1, b1, gqkv, qv, gout, bout, g2, b2, gup, bup, gdown, bdown


def solution(mesh):
    shape = dict(mesh.shape)
    inner = block_mesh if (shape["dp"], shape["fsdp"]) == (2, OWNERS) else any_mesh

    def per_device(text_in, *rest):
        weights, image_weights = rest[:12], rest[12:24]
        patches, targets, group_ids, cap_len, slot_counts = rest[24:]
        return inner(
            text_in, weights, image_weights, jnp.transpose(patches, (1, 0, 2)), targets, group_ids, cap_len, slot_counts
        )

    both = ("dp", "fsdp")
    owned, table = P("fsdp"), P("fsdp", None)
    text_specs = (owned, owned, table, owned, table, owned, owned, owned, table, owned, table, owned)
    return jax.shard_map(
        per_device,
        mesh=mesh,
        in_specs=(P(both, None), *text_specs, *([P()] * 12), P(both, None, None), P(both, None), P(both), P(both), P(both)),
        out_specs=(P(), P(both, None), P(both, None), *text_specs),
        check_vma=False,
    )
```

```python
import functools

import jax
import jax.numpy as jnp
from jax import lax
from jax.experimental import pallas as pl
from jax.experimental.pallas import tpu as pltpu
from jax.sharding import PartitionSpec as P

HEAD = 64
EPS = 1e-06
ROOT_HALF = 0.7071067811865476
INV_ROOT_TAU = 0.3989422804014327
DEAD = -8e9
BF = jnp.bfloat16
F32 = jnp.float32
BLK = 128
TILE = 256
NZ, NY, NC = 4, 2, 2
OWNERS = NZ * NY * NC
MESH = pl.DeviceIdType.MESH
VMEM_LIMIT = 63 * 2**20
LAGS = (-2, 1, 3, 5)
SPLIT = (0, 3, 4, 6)
WHOLE = (1, 2, 5, 7)
LANDING = {4: 0, 5: 1, 6: 2, 7: 3, 3: 4, 0: 5, 1: 6, 2: 7}
BACK_STEPS = (
    ((3, 1),),
    ((6, 2), (7, 2)),
    ((4, 3),),
    ((5, 3),),
    ((3, 2),),
    ((6, 3), (7, 3)),
)
SMALL = ((0, 0), (0, 4), (1, 2), (2, 0), (2, 4))


def norm_rows(values):
    centered = values - jnp.mean(values, axis=-1, keepdims=True)
    inv_std = lax.rsqrt(jnp.mean(centered * centered, axis=-1, keepdims=True) + EPS)
    return centered * inv_std, inv_std


def norm_back(u, n, r):
    return r * (u - jnp.mean(u, axis=-1, keepdims=True) - n * jnp.mean(u * n, axis=-1, keepdims=True))


def gelu_exact(v):
    return 0.5 * v * (1.0 + lax.erf(v * ROOT_HALF))


def dot(a, b):
    return jnp.dot(a, b, preferred_element_type=F32)


def dot_nt(a, b):
    return lax.dot_general(a, b, (((1,), (1,)), ((), ())), preferred_element_type=F32)


def dot_tn(a, b):
    return lax.dot_general(a, b, (((0,), (0,)), ((), ())), preferred_element_type=F32)


def split(v):
    high = v.astype(BF)
    return high, (v - high.astype(F32)).astype(BF)


def row(ref, start=0, size=None):
    size = ref.shape[0] if size is None else size
    return ref[pl.ds(start, size)].astype(F32).reshape(1, size)


def place():
    f = lax.axis_index("fsdp")
    return lax.axis_index("dp"), f // (NY * NC), (f // NC) % NY, f % NC


def device(x, z, y, c):
    return (x, (z * NY + y) * NC + c)


def greet(peers):
    barrier = pltpu.get_barrier_semaphore()
    for peer in peers:
        pl.semaphore_signal(barrier, inc=1, device_id=peer, device_id_type=MESH)
    pl.semaphore_wait(barrier, len(peers))


def remote(src, dst, send, recv, peer):
    return pltpu.make_async_remote_copy(
        src_ref=src, dst_ref=dst, send_sem=send, recv_sem=recv, device_id=peer, device_id_type=MESH
    )


class Gather:
    def __init__(self, g_ref, send, recv):
        self.g, self.send, self.recv = g_ref, send, recv
        self.chunks = g_ref.shape[0]
        half = g_ref.shape[-1] // 2
        self.x, self.z, self.y, self.c = place()
        self.mine = pl.ds(pl.multiple_of(self.x * half, 128), half)
        self.far_z = [device(self.x, (self.z + j) % NZ, self.y, self.c) for j in range(1, NZ)]
        self.near_y = device(self.x, self.z, 1 - self.y, self.c)
        self.near_x = device(1 - self.x, self.z, self.y, self.c)
        self.twin = device(self.x, self.z, self.y, 1 - self.c)
        self.peers = self.far_z + [self.near_y, self.near_x, self.twin]

    def copy(self, k, slot, ref, peer):
        return remote(ref, ref, self.send.at[k, slot], self.recv.at[k, slot], peer)

    def along_z(self, k):
        ref = self.g.at[k, self.z, self.y, self.c, :, self.mine]
        return [self.copy(k, j, ref, peer) for j, peer in enumerate(self.far_z)]

    def first(self, k):
        top, rest = pl.ds(0, 32), pl.ds(32, 16)
        return [self.copy(k, 3, self.g.at[k, :, self.y, self.c, top, self.mine], self.near_y)] + [
            self.copy(k, 4 + j, self.g.at[k, (self.z + 1 + j) % NZ, self.y, self.c, rest, self.mine], self.near_x)
            for j in range(3)
        ]

    def second(self, k):
        top, rest = pl.ds(0, 32), pl.ds(32, 16)
        return (
            [
                self.copy(k, 7 + j, self.g.at[k, (self.z + 1 + j) % NZ, :, self.c, top, self.mine], self.near_x)
                for j in range(3)
            ]
            + [self.copy(k, 10, self.g.at[k, self.z, 1 - self.y, self.c, top, self.mine], self.near_x)]
            + [self.copy(k, 11, self.g.at[k, :, self.y, self.c, rest], self.near_y)]
        )

    def last(self, k):
        return [self.copy(k, 12, self.g.at[k, :, :, self.c], self.twin)]

    def tick(self, t):
        def start(copies):
            for copy in copies:
                copy.start()

        def arrive(copies):
            for copy in copies:
                copy.wait_recv()

        def stage(lag, action):
            @pl.when(jnp.logical_and(t - lag >= 0, t - lag < self.chunks))
            def _():
                action(t - lag)

        def one(k):
            start(self.along_z(k))

        def two(k):
            arrive(self.along_z(k))
            start(self.first(k))

        def three(k):
            arrive(self.first(k))
            start(self.second(k))

        def four(k):
            arrive(self.second(k))
            start(self.last(k))

        stage(LAGS[0], one)
        stage(LAGS[1], two)
        stage(LAGS[2], three)
        stage(LAGS[3], four)

    def finish(self):
        def end(k, _):
            for copy in self.last(k):
                copy.wait()
            for copy in self.along_z(k) + self.first(k) + self.second(k):
                copy.wait_send()
            return 0

        lax.fori_loop(0, self.chunks, end, 0)


def image_body(comm, group, *refs):
    (x_hbm, t_ref, g1, b1, bqv, bout, g2, b2, bup, bdown, wqkv_hbm, wout_hbm, wup_hbm, wdown_hbm), refs = refs[:14], refs[14:]
    if comm:
        (oqkv, oout, oup, odown, *smalls, gid, count), refs = refs[:14], refs[14:]
        (aim_ref, gath, vec_ref, wgt_ref), refs = refs[:4], refs[4:]
    else:
        (aim_ref,), refs = refs[:1], refs[1:]
    (x_ref, wqkv, wout, wup, wdown, h_ref, qkv_ref, ctx_ref, act_ref, xm_ref, sems), refs = refs[:11], refs[11:]
    patches, cap, width = x_hbm.shape
    ff = wup.shape[1]
    steps = cap // group
    rows = patches * group
    loads = [
        pltpu.make_async_copy(src, dst, sems.at[i])
        for i, (src, dst) in enumerate(
            [(x_hbm, x_ref), (wqkv_hbm, wqkv), (wout_hbm, wout), (wup_hbm, wup), (wdown_hbm, wdown)]
        )
    ]
    if comm:
        ids, vecs, own_ref, own_sem, g_send, g_recv, s_send, s_recv = refs
        gather = Gather(gath, g_send, g_recv)
        x, z, y, c = gather.x, gather.z, gather.y, gather.c
        own = []
        for k in range(gath.shape[0]):
            if k < 3:
                src = oqkv.at[:, k * width : k * width + width]
            elif k < 4:
                src = oout
            elif k < 8:
                src = oup.at[:, (k - 4) * width : (k - 3) * width]
            else:
                src = odown.at[(k - 8) * oout.shape[0] : (k - 7) * oout.shape[0]]
            own.append((pltpu.make_async_copy(src, own_ref.at[k], own_sem.at[k]), pltpu.make_async_copy(own_ref.at[k], gath.at[k, z, y, c], own_sem.at[k])))
        for copy, _out in own:
            copy.start()
        for load in loads:
            load.start()
        lines = []
        for ref in smalls:
            n = ref.shape[0]
            for at in range(0, n, 128):
                take = min(128, n - at)
                line = row(ref)[:, at : at + take]
                lines.append(jnp.concatenate([line, jnp.zeros((1, 128 - take), F32)], axis=1) if take < 128 else line)
        lines.append(jnp.zeros((16 - len(lines), 128), F32))
        vecs[z, y, c] = jnp.concatenate(lines, axis=0).astype(BF)
        lane = lax.broadcasted_iota(jnp.int32, (8, 128), 1)
        line = jnp.full((8, 128), -1, jnp.int32)
        for i in range(cap):
            line = jnp.where(lane == i, jnp.where(i < count[0], gid[i], -1), line)
        ids[x, z, y, c] = line
        greet(gather.peers)

        def small(slot, ref, peer):
            return remote(ref, ref, s_send.at[slot], s_recv.at[slot], peer)

        small_z = [small(j, ids.at[x, z, y, c], peer) for j, peer in enumerate(gather.far_z)]
        small_z += [small(3 + j, vecs.at[z, y, c], peer) for j, peer in enumerate(gather.far_z)]
        small_y = [small(6, ids.at[x, :, y, c], gather.near_y), small(7, vecs.at[:, y, c], gather.near_y)]
        small_x = [small(8, ids.at[x, :, :, c], gather.near_x), small(9, vecs.at[:, :, c], gather.twin)]
        small_c = [small(10, ids.at[:, :, :, c], gather.twin)]
        stages = [small_z, small_y, small_x, small_c]
        for copy, out in own:
            copy.wait()
            out.start()
        for _copy, out in own:
            out.wait()
        for k in range(-LAGS[0]):
            for copy in gather.along_z(k):
                copy.start()

        def tick(step, t):
            gather.tick(step * 6 + t)
            for i, (at_step, at) in enumerate(SMALL):
                if at == t:

                    @pl.when(step == at_step)
                    def _():
                        if i > 0:
                            for copy in stages[i - 1]:
                                copy.wait_recv()
                        if i < 4:
                            for copy in stages[i]:
                                copy.start()

    else:
        for load in loads:
            load.start()

        def tick(step, t):
            pass

    lane_q = lax.broadcasted_iota(jnp.int32, (112, 128), 1)
    low_half = lane_q < HEAD
    key = lax.broadcasted_iota(jnp.int32, (224, 128), 1)
    second = lax.broadcasted_iota(jnp.int32, (224, 128), 0) % 112 >= 56
    first_key = jnp.where(second, 64, 0)
    key_ok = (key >= first_key) & (key < first_key + patches)
    ones = jnp.ones((128, 128), BF)
    g1v, b1v, g2v, b2v = row(g1), row(b1), row(g2), row(b2)
    bias = [row(bqv, 0, width), jnp.zeros((1, width), F32), row(bqv, width, width)]
    boutv, bupv, bdownv = row(bout), row(bup), row(bdown)
    xm_ref[...] = jnp.zeros_like(xm_ref)
    for load in loads[:4]:
        load.wait()

    def chunk_step(step, _):
        c0 = pl.multiple_of(step * group, group)
        caps = pl.ds(c0, group)
        tick(step, 0)

        def norm_one(p, _):
            value = x_ref[pl.ds(p * 5, 5), caps, :].astype(F32).reshape(5 * group, width)
            n, _inv = norm_rows(value)
            h_ref[pl.ds(pl.multiple_of(p * 5 * group, 16), 5 * group), :] = (n * g1v + b1v).astype(BF)
            return 0

        lax.fori_loop(0, patches // 5, norm_one, 0)
        for n in range(3 * width // TILE):
            cols = slice(n * TILE, n * TILE + TILE)
            part, off = divmod(n * TILE, width)
            value = dot(h_ref[...], wqkv[:, cols]) + bias[part][:, off : off + TILE]
            qkv_ref[2 * n] = value[:, :128]
            qkv_ref[2 * n + 1] = value[:, 128:]
        tick(step, 1)

        def attend(p, _):
            def load(col, tall):
                parts = []
                for k in range(2):
                    v = qkv_ref[col // 128, pl.ds(2 * p + k, patches, stride=group), :]
                    parts.append(jnp.concatenate([v, jnp.zeros((tall - patches, 128), F32)], axis=0))
                return jnp.concatenate(parts, axis=0).astype(BF)

            def scores(h):
                q = load(h * 128, 56)
                zero = jnp.zeros_like(q)
                q2 = jnp.concatenate([jnp.where(low_half, q, zero), jnp.where(low_half, zero, q)], axis=0)
                return jnp.where(key_ok, dot_nt(q2, load(width + h * 128, 64)), DEAD)

            for first in range(0, width // 128, 6):
                heads = range(first, first + 6)
                ss = [scores(h) for h in heads]
                tops = [jnp.max(s, axis=-1, keepdims=True) for s in ss]
                es = [jnp.exp((s - top) * 0.125).astype(BF) for s, top in zip(ss, tops)]
                os = [dot(e, jnp.concatenate([load(2 * width + h * 128, 64), ones], axis=1)) for e, h in zip(es, heads)]
                for o, h in zip(os, heads):
                    num = jnp.where(low_half, o[:112, :128], o[112:, :128])
                    den = jnp.where(low_half, o[:112, 128:], o[112:, 128:])
                    out = num / den
                    for k in range(2):
                        ctx_ref[h, pl.ds(2 * p + k, patches, stride=group), :] = out[56 * k : 56 * k + patches]
            return 0

        lax.fori_loop(0, group // 4, attend, 0)
        tick(step, 2)
        lax.fori_loop(group // 4, group // 2, attend, 0)
        tick(step, 3)

        def project(p, _):
            span = pl.ds(pl.multiple_of(p * 10 * group, 16), 10 * group)
            ctx = jnp.concatenate([ctx_ref[h, span, :] for h in range(width // 128)], axis=1).astype(BF)
            x1 = x_ref[pl.ds(p * 10, 10), caps, :].astype(F32).reshape(10 * group, width) + dot(ctx, wout[...]) + boutv
            xm_ref[caps, :] += jnp.sum(x1.reshape(10, group, width), axis=0)
            n, _inv = norm_rows(x1)
            h_ref[span, :] = (n * g2v + b2v).astype(BF)
            return 0

        lax.fori_loop(0, patches // 10, project, 0)
        tick(step, 4)
        for n in range(ff // TILE):
            cols = slice(n * TILE, n * TILE + TILE)
            act = gelu_exact(dot(h_ref[...], wup[:, cols]) + bupv[:, cols])
            act_ref[caps, cols] = jnp.sum(act.reshape(patches, group, TILE), axis=0)
            if n == ff // TILE // 2:
                tick(step, 5)
        return 0

    lax.fori_loop(0, steps, chunk_step, 0)
    loads[4].wait()
    both = jnp.concatenate(split(act_ref[...] * (1.0 / patches)), axis=0)
    for n in range(width // TILE):
        cols = slice(n * TILE, n * TILE + TILE)
        o = dot(both, wdown[:, cols])
        aim_ref[:, cols] = (
            o[:cap] + o[cap:] + xm_ref[:, cols] * (1.0 / patches) + bdownv[:, cols] + t_ref[:, cols].astype(F32)
        )
    if comm:
        column = lax.broadcasted_iota(jnp.int32, (cap, 128), 0)
        mine = jnp.zeros((cap, 128), jnp.int32)
        for i in range(cap):
            mine = jnp.where(column == i, gid[i], mine)
        total = jnp.zeros((cap, 128), F32)
        for dx in range(2):
            for o in range(OWNERS):
                line = ids[dx, o // 4, o // 2 % 2, o % 2][0:1]
                total = total + jnp.where(mine == line, 1.0, 0.0)
        members = jnp.sum(total, axis=1, keepdims=True)
        wgt = jnp.where(column < count[0], 1.0 / jnp.maximum(members, 1.0), 0.0)
        wgt_ref[...] = wgt
        vec_ref[...] = vecs[...]
        gather.finish()
        for stage in stages:
            for copy in stage:
                copy.wait_send()


def image_call(patches, targets, weights, extra=(), group=16):
    comm = bool(extra)
    g1, b1, wqkv, bqv, wout, bout, g2, b2, wup, bup, wdown, bdown = weights
    count, cap, width = patches.shape
    ff = wup.shape[1]
    anys = pl.BlockSpec(memory_space=pl.ANY)
    vmem = pl.BlockSpec(memory_space=pltpu.VMEM)
    smem = pl.BlockSpec(memory_space=pltpu.SMEM)
    rows = count * group
    sds = jax.ShapeDtypeStruct
    out_shape = [sds((cap, width), F32)]
    out_specs = [vmem]
    in_specs = [anys] + [vmem] * 9 + [anys] * 4
    scratch = [
        pltpu.VMEM(patches.shape, BF),
        pltpu.VMEM(wqkv.shape, BF),
        pltpu.VMEM(wout.shape, BF),
        pltpu.VMEM(wup.shape, BF),
        pltpu.VMEM(wdown.shape, BF),
        pltpu.VMEM((rows, width), BF),
        pltpu.VMEM((3 * width // 128, rows, 128), F32),
        pltpu.VMEM((width // 128, rows, 128), F32),
        pltpu.VMEM((cap, ff), F32),
        pltpu.VMEM((cap, width), F32),
        pltpu.SemaphoreType.DMA((5,)),
    ]
    params = dict(vmem_limit_bytes=VMEM_LIMIT)
    if comm:
        chunks = 12
        piece = extra[1].shape
        in_specs += [anys] * 4 + [vmem] * 8 + [smem] * 2
        out_shape += [
            sds((chunks, NZ, NY, NC) + piece, BF),
            sds((NZ, NY, NC, 16, 128), BF),
            sds((cap, 128), F32),
        ]
        out_specs += [anys, vmem, vmem]
        scratch += [
            pltpu.VMEM((2, NZ, NY, NC, 8, 128), jnp.int32),
            pltpu.VMEM((NZ, NY, NC, 16, 128), BF),
            pltpu.VMEM((chunks,) + piece, BF),
            pltpu.SemaphoreType.DMA((chunks,)),
            pltpu.SemaphoreType.DMA((chunks, 13)),
            pltpu.SemaphoreType.DMA((chunks, 13)),
            pltpu.SemaphoreType.DMA((11,)),
            pltpu.SemaphoreType.DMA((11,)),
        ]
        params.update(collective_id=0, has_side_effects=True)
    return pl.pallas_call(
        functools.partial(image_body, comm, group),
        out_shape=out_shape,
        in_specs=in_specs,
        out_specs=out_specs,
        scratch_shapes=scratch,
        compiler_params=pltpu.CompilerParams(**params),
    )(patches, targets, g1, b1, bqv, bout, g2, b2, bup, bdown, wqkv, wout, wup, wdown, *extra)


class Reduce:
    def __init__(self, landing, split_bufs, whole_bufs, sems):
        self.landing, self.split_bufs, self.whole_bufs = landing, split_bufs, whole_bufs
        self.send, self.recv = sems
        self.x, self.z, self.y, self.c = place()
        self.far_z = [device(self.x, (self.z + j) % NZ, self.y, self.c) for j in range(1, NZ)]
        self.near_y = device(self.x, self.z, 1 - self.y, self.c)
        self.near_x = device(1 - self.x, self.z, self.y, self.c)
        self.twin = device(self.x, self.z, self.y, 1 - self.c)
        self.peers = self.far_z + [self.near_y, self.near_x, self.twin]
        self.plans = {}

    def add(self, k, grad, out):
        z, y, c = self.z, self.y, self.c
        full = slice(None)

        def copy(slot, src, dst, peer):
            return remote(src, dst, self.send.at[k, slot], self.recv.at[k, slot], peer)

        def start(items):
            for item in items:
                item.start()

        def wait(items):
            for item in items:
                item.wait()

        def add_into(target, value):
            target[...] = target[...] + value

        landed = self.landing(k)
        c0 = [copy(0, grad(full, full, 1 - c, full), landed, self.twin)]
        if k in WHOLE:
            n = WHOLE.index(k)
            in_y, in_z, mine, other = (buf.at[n] for buf in self.whole_bufs)
            c1 = [copy(1, grad(full, 1 - y, c, full), in_y, self.near_y)]
            c2 = [
                copy(1 + j, grad((z + j) % NZ, y, c, full), in_z.at[j - 1], self.far_z[j - 1]) for j in range(1, NZ)
            ]
            c3 = [copy(5, mine, other, self.near_x)]

            def s1():
                wait(c0)
                add_into(grad(full, full, c, full), landed[...])
                start(c1)

            def s2():
                wait(c1)
                add_into(grad(full, y, c, full), in_y[...])
                start(c2)

            def s3():
                wait(c2)
                total = grad(z, y, c, full)[...].astype(F32)
                for j in range(NZ - 1):
                    total = total + in_z[j].astype(F32)
                mine[...] = total.astype(BF)
                start(c3)

            def s4():
                wait(c3)
                out(pl.ds(0, mine.shape[-1]))[...] = mine[...].astype(F32) + other[...].astype(F32)

            self.plans[k] = [lambda: start(c0), s1, s2, s3, s4]
            return
        n = SPLIT.index(k)
        in_x, in_y, in_z, sum_x, other = (buf.at[n] for buf in self.split_bufs)
        half = sum_x.shape[-1]
        mine = pl.ds(pl.multiple_of(self.x * half, 128), half)
        theirs = pl.ds(pl.multiple_of((1 - self.x) * half, 128), half)
        c1 = [copy(1, grad(full, full, c, theirs), in_x, self.near_x)]
        c2 = [copy(2, grad(full, 1 - y, c, mine), in_y, self.near_y)]
        c3 = [copy(2 + j, grad((z + j) % NZ, y, c, mine), in_z.at[j - 1], self.far_z[j - 1]) for j in range(1, NZ)]
        c4 = [copy(6, sum_x, other, self.near_x)]

        def s1():
            wait(c0)
            add_into(grad(full, full, c, full), landed[...])
            start(c1)

        def s2():
            wait(c1)
            add_into(grad(full, full, c, mine), in_x[...])
            start(c2)

        def s3():
            wait(c2)
            add_into(grad(full, y, c, mine), in_y[...])
            start(c3)

        def s4():
            wait(c3)
            total = grad(z, y, c, mine)[...].astype(F32)
            for j in range(NZ - 1):
                total = total + in_z[j].astype(F32)
            rounded = total.astype(BF)
            sum_x[...] = rounded
            out(mine)[...] = rounded.astype(F32)
            start(c4)

        def s5():
            wait(c4)
            out(theirs)[...] = other[...].astype(F32)

        self.plans[k] = [lambda: start(c0), s1, s2, s3, s4, s5]

    def run(self, k, stage):
        self.plans[k][stage]()


def one_hot(rows, start, width, limit):
    i = lax.broadcasted_iota(jnp.int32, (rows, width), 0)
    j = lax.broadcasted_iota(jnp.int32, (rows, width), 1)
    return jnp.where((j == i + start) & (i < limit), 1.0, 0.0).astype(BF)


def spread_rows(all_small, vec_ref, bup_ref):
    width = vec_ref.shape[1]
    part = width // OWNERS
    tile = lambda o: all_small[o // 4, o // 2 % 2, o % 2]
    plain = jnp.zeros((16, width), F32)
    for o in range(OWNERS):
        plain = plain + dot(tile(o), one_hot(128, o * part, width, part))
    halves = []
    for h in range(2):
        total = jnp.zeros((16, width), F32)
        for m in range(8):
            total = total + dot(tile(8 * h + m), one_hot(128, 2 * m * part, width, 2 * part))
        halves.append(total[2:3])
    zero = jnp.zeros((1, width), F32)
    order = [plain[0:1], plain[1:2], halves[0], zero, halves[1], plain[3:4], plain[4:5], plain[5:6], plain[8:9]]
    vec_ref[...] = jnp.concatenate(order + [jnp.zeros((7, width), F32)], axis=0)
    first = [one_hot(128, 4 * m * part, width, 128) for m in range(4)]
    rest = [one_hot(128, 4 * m * part + 128, width, 4 * part - 128) for m in range(4)]
    for q in range(4):
        total = jnp.zeros((1, width), F32)
        for m in range(4):
            t = tile(4 * q + m)
            total = total + dot(t, first[m])[6:7] + dot(t, rest[m])[7:8]
        bup_ref[:, q * width : (q + 1) * width] = total


def own_rows(gvec, own_ref):
    width = gvec.shape[1]
    part = width // OWNERS
    me = lax.axis_index("fsdp")
    high = gvec.astype(BF)
    left = gvec - high.astype(F32)
    mid = left.astype(BF)
    low = (left - mid.astype(F32)).astype(BF)

    def pick(start, lanes):
        i = lax.broadcasted_iota(jnp.int32, (width, lanes), 0)
        j = lax.broadcasted_iota(jnp.int32, (width, lanes), 1)
        hot = jnp.where(i == j + start, 1.0, 0.0).astype(BF)
        return dot(high, hot) + dot(mid, hot) + dot(low, hot)

    plain = pick(me * part, 256)
    pair = pick(me % 8 * (2 * part), 256)
    four = pick(me % 4 * (4 * part), 256)
    qv = jnp.where(me < 8, pair[2:3], pair[4:5])
    q = me // 4
    bup = jnp.where(q == 0, four[12:13], jnp.where(q == 1, four[13:14], jnp.where(q == 2, four[14:15], four[15:16])))
    loss = jnp.broadcast_to(gvec[9:10, :1], (1, 256))
    rows = [plain[0:1], plain[1:2], qv, plain[5:6], plain[6:7], plain[7:8], plain[8:9], loss, bup]
    own_ref[...] = jnp.concatenate(rows + [jnp.zeros((7, 256), F32)], axis=0)


def text_body(comm, *refs):
    if comm:
        (x_ref, all_small, aim_ref, wgt_ref, len_ref, w_hbm), refs = refs[:6], refs[6:]
    else:
        (x_ref, vec_ref, bup_ref, aim_ref, wgt_ref, len_ref, w_hbm), refs = refs[:7], refs[7:]
    if comm:
        (y_hbm, dx_hbm, own_out, gqkv, gout, gup, gdown), refs = refs[:7], refs[7:]
    else:
        (y_hbm, dx_hbm, gvec_ref, grad_hbm), refs = refs[:4], refs[4:]
    (w_ref, wd_ref, h1_ref, qkv_ref, p_ref, ctx_ref, x1_ref, h2_ref, act_ref, slope_ref, asum_ref, lcol_ref, e_ref, et_ref,
     dy_ref, d_ref, da_ref, dmw_ref, sems), refs = refs[:19], refs[19:]
    tok, width = x_ref.shape
    cap = aim_ref.shape[0]
    seq = tok // cap
    ff = 4 * width
    blocks = tok // BLK
    pairs = width // 128
    tiles = width // TILE
    piece = w_ref.shape[-2]

    def chunk(k):
        return w_ref.at[k] if k < 8 else wd_ref.at[:, :, :, (k - 8) * piece : (k - 7) * piece]

    loads = [pltpu.make_async_copy(w_hbm.at[k], chunk(k), sems.at[k]) for k in range(12)]
    for load in loads:
        load.start()
    if comm:
        vec_ref, bup_ref, gvec_ref, *bufs, vecs, vec_in, vec_z, as0, as1, as2, as3, dms, down_mine, down_in, r_send, r_recv, v_send, v_recv, f_send, f_recv, free = refs
        split_bufs, whole_bufs = bufs[:5], bufs[5:]
        red = Reduce(
            lambda k: slope_ref.at[LANDING[k] // 2, LANDING[k] % 2], split_bufs, whole_bufs, (r_send, r_recv)
        )
        outs = [gqkv, gqkv, gqkv, gout, gup, gup, gup, gup]

        def view(k):
            if k >= 4:
                rows = slice((k - 4) * piece, (k - 3) * piece)
                return lambda a, b, d, lanes: wd_ref.at[a, b, d, rows, lanes]
            n = 3 if k == 3 else 4 + k
            return lambda a, b, d, lanes: w_ref.at[n, a, b, d, :, lanes]

        def result(k):
            base = (0, 1, 2, 0, 0, 1, 2, 3)[k] * width
            return lambda lanes: outs[k].at[:, pl.ds(pl.multiple_of(base + lanes.start, 128), lanes.size)]

        for k in range(8):
            red.add(k, view(k), result(k))
        z, y_at, c = red.z, red.y, red.c

        def side(slot, src, dst, peer):
            return remote(src, dst, f_send.at[slot], f_recv.at[slot], peer)

        to_twin = [side(0, as0.at[:, :, 1 - c], as1.at[:, :, c], red.twin)]
        to_y = [side(1, as1.at[:, 1 - y_at], as2.at[:, y_at], red.near_y)]
        to_z = [side(2 + j, as2.at[(z + 1 + j) % NZ], as3.at[z], peer) for j, peer in enumerate(red.far_z)]
        dm_z = [side(5 + j, dms.at[z, y_at, c], dms.at[z, y_at, c], peer) for j, peer in enumerate(red.far_z)]
        dm_y = [side(8, dms.at[:, y_at, c], dms.at[:, y_at, c], red.near_y)]
        dm_twin = [side(9, dms.at[:, :, c], dms.at[:, :, c], red.twin)]
        down_x = [side(10, down_mine, down_in, red.near_x)]

        def begin(copies):
            for item in copies:
                item.start()

        def end(copies):
            for item in copies:
                item.wait()

        greet(red.peers)
        run = red.run
        spread_rows(all_small, vec_ref, bup_ref)
    else:

        def run(k, stage):
            pass

    vec = lambda i: vec_ref[i : i + 1, :]
    rows_at = lambda b: pl.ds(pl.multiple_of(b * BLK, BLK), BLK)

    for i in range(cap):
        lcol_ref[i : i + 1, :] = jnp.full((1, 128), len_ref[i], jnp.int32)
    lcol = lcol_ref[:, :1]
    t_lane = lax.broadcasted_iota(jnp.int32, (cap, tok), 1)
    c_row = lax.broadcasted_iota(jnp.int32, (cap, tok), 0)
    pool = jnp.where((t_lane // seq == c_row) & (t_lane % seq < lcol), 1.0, 0.0)
    e_ref[...] = pool.astype(BF)
    et_ref[...] = jnp.concatenate([pool, pool, jnp.zeros((128 - 2 * cap, tok), F32)], axis=0).T.astype(BF)
    d_ref[2 * cap :, :] = jnp.zeros_like(d_ref[2 * cap :, :])

    def norm_one(b, _):
        n, _r = norm_rows(x_ref[rows_at(b), :].astype(F32))
        h1_ref[rows_at(b), :] = (n * vec(0) + vec(1)).astype(BF)
        return 0

    lax.fori_loop(0, blocks, norm_one, 0)

    def weight(k, cols):
        return w_ref[k, :, :, :, :, cols].reshape(width, -1)

    for part in range(3):
        loads[part].wait()
        for n in range(tiles):
            cols = slice(n * TILE, n * TILE + TILE)
            value = dot(h1_ref[...], weight(part, cols)) + vec_ref[2 + part : 3 + part, cols]
            qkv_ref[:, part * width + n * TILE : part * width + n * TILE + TILE] = value.astype(BF)

    lane = lax.broadcasted_iota(jnp.int32, (BLK, 128), 1)
    low_half = lane < HEAD
    live_lane = jnp.sum(pool, axis=0, keepdims=True)

    def both_heads(v):
        zero = jnp.zeros_like(v)
        return jnp.concatenate([jnp.where(low_half, v, zero), jnp.where(low_half, zero, v)], axis=0)

    def pick(v):
        return jnp.where(low_half, v[:BLK], v[BLK:])

    same = (lax.broadcasted_iota(jnp.int32, (2 * BLK, BLK), 0) % BLK) // seq == lax.broadcasted_iota(
        jnp.int32, (2 * BLK, BLK), 1
    ) // seq
    for b in range(blocks):
        key_ok = same & (live_lane[:, b * BLK : b * BLK + BLK] > 0.5)
        rows = slice(b * BLK, b * BLK + BLK)
        heads = range(pairs)
        part = lambda n, h: qkv_ref[rows, n * width + h * 128 : n * width + h * 128 + 128]
        ss = [jnp.where(key_ok, dot_nt(both_heads(part(0, h)), part(1, h)), DEAD) for h in heads]
        tops = [jnp.max(s, axis=-1, keepdims=True) for s in ss]
        es = [jnp.exp((s - top) * 0.125) for s, top in zip(ss, tops)]
        sums = [jnp.sum(e, axis=-1, keepdims=True) for e in es]
        ps = [e / total for e, total in zip(es, sums)]
        for h in heads:
            p_ref[b * pairs + h] = ps[h]
        os = [dot(ps[h].astype(BF), part(2, h)) for h in heads]
        for h in heads:
            ctx_ref[rows, h * 128 : h * 128 + 128] = pick(os[h]).astype(BF)

    loads[3].wait()
    for n in range(tiles):
        cols = slice(n * TILE, n * TILE + TILE)
        x1_ref[:, cols] = x_ref[:, cols].astype(F32) + dot(ctx_ref[...], weight(3, cols)) + vec_ref[5:6, cols]

    def norm_two(b, _):
        n, _r = norm_rows(x1_ref[rows_at(b), :])
        h2_ref[rows_at(b), :] = (n * vec(6) + vec(7)).astype(BF)
        return 0

    lax.fori_loop(0, blocks, norm_two, 0)
    for n in range(ff // TILE):
        k, off = divmod(n * TILE, width)
        if off == 0:
            loads[4 + k].wait()
        cols = slice(n * TILE, n * TILE + TILE)
        inner = slice(off, off + TILE)
        pre = dot(h2_ref[...], weight(4 + k, inner)) + bup_ref[:, cols]
        half_slope = 0.5 * (1.0 + lax.erf(pre * ROOT_HALF))
        act = (pre * half_slope).astype(BF)
        slope = (half_slope + pre * jnp.exp(-0.5 * pre * pre) * INV_ROOT_TAU).astype(BF)
        slope_ref[k, :, :, :, :, inner] = slope.reshape(slope_ref.shape[1:-1] + (TILE,))
        act_ref[:, cols] = act

    for k in range(4):
        total = dot(e_ref[...], act_ref[:, k * width : (k + 1) * width])
        if comm:
            for o in range(4):
                own = total[:, o * 4 * piece : (o + 1) * 4 * piece]
                own = jnp.concatenate([own, jnp.zeros((cap, 256 - 4 * piece), F32)], axis=1)
                as0[k, o // 2, o % 2] = own.astype(BF)
        else:
            hi, lo = split(total)
            asum_ref[:cap, k * width : (k + 1) * width] = hi
            asum_ref[cap:, k * width : (k + 1) * width] = lo
    if comm:
        begin(to_twin)
        as1[:, :, c] = as0[:, :, c]
    h2_ref[...] = h2_ref[...].T
    for load in loads[8:]:
        load.wait()
    lens = lcol.astype(F32)
    wgt = wgt_ref[:, :1]
    loss = jnp.zeros((1, TILE), F32)
    for n in range(tiles):
        cols = slice(n * TILE, n * TILE + TILE)
        y = x1_ref[:, cols] + vec_ref[8:9, cols]
        for k in range(NZ):
            y = y + dot(act_ref[:, k * width : k * width + width], wd_ref[k, :, :, :, cols].reshape(width, TILE))
        hi, lo = split(y)
        da_ref[:, cols] = hi
        error = (dot(e_ref[...], hi) + dot(e_ref[...], lo)) / lens - aim_ref[:, cols]
        loss = loss + jnp.sum(wgt * error * error, axis=0, keepdims=True)
        dpool = 2.0 * wgt * error / lens
        dy_hi, dy_lo = split(dpool)
        d_ref[:cap, cols] = dy_hi
        d_ref[cap : 2 * cap, cols] = dy_lo
        gvec_ref[8:9, cols] = jnp.sum(dy_hi.astype(F32) * lens, axis=0, keepdims=True)
        if comm:
            dms[z, y_at, c, :, cols] = dy_hi
            if n == 1:
                end(to_twin)
                begin(to_y)
                as2[:, y_at] = as1[:, y_at]
            elif n == tiles - 1:
                begin(dm_z)
    y_out = pltpu.make_async_copy(da_ref, y_hbm, sems.at[12])
    y_out.start()
    gvec_ref[3:4, :] = jnp.zeros((1, width), F32)
    gvec_ref[9:10, :] = jnp.broadcast_to(jnp.sum(loss, axis=1, keepdims=True), (1, width))
    gvec_ref[10:12, :] = jnp.zeros((2, width), F32)

    dm = d_ref[:cap, :]
    span = ff // 8
    pad = jnp.zeros((128 - 2 * cap, span), BF)
    for n in range(8):
        hi, lo = split(dot_nt(dm, wd_ref[n // 2, n % 2].reshape(span, width)))
        dmw_ref[:cap, n * span : (n + 1) * span] = hi
        dmw_ref[cap : 2 * cap, n * span : (n + 1) * span] = lo
        dmw_ref[2 * cap :, n * span : (n + 1) * span] = pad
    for k in range(4):
        for n in range(tiles):
            at = k * width + n * TILE
            cols = slice(n * TILE, n * TILE + TILE)
            slope = slope_ref[k, :, :, :, :, cols].reshape(tok, TILE)
            dpre = (dot(et_ref[...], dmw_ref[:, at : at + TILE]) * slope.astype(F32)).astype(BF)
            gvec_ref[12 + k : 13 + k, cols] = jnp.sum(dpre.astype(F32), axis=0, keepdims=True)
            act_ref[:, at : at + TILE] = dpre
            wd_ref[:, :, :, k * piece : (k + 1) * piece, cols] = (
                dot(h2_ref[...], dpre).astype(BF).reshape(NZ, NY, NC, piece, TILE)
            )
        if comm:
            pl.semaphore_signal(free, inc=1, device_id=red.twin, device_id_type=MESH)
            if k == 0:
                end(to_y)
                begin(to_z)
                as3[z] = as2[z]
            if k == 1:
                end(dm_z)
                begin(dm_y)
            if k % 2 == 0:
                pl.semaphore_wait(free, 1)
        run(4 + k, 0)
        if k > 0:
            run(3 + k, 1)
    for n in range(tiles):
        total = jnp.zeros((tok, TILE), F32)
        for k in range(4):
            w_rows = w_ref[4 + k].reshape(width, width)[n * TILE : n * TILE + TILE]
            total = total + dot_nt(act_ref[:, k * width : k * width + width], w_rows)
        dy_ref[:, n * TILE : n * TILE + TILE] = total
        if n == 0:
            run(7, 1)
        elif n == 2:
            run(4, 2)
    if not comm:
        dm2 = jnp.concatenate([dm, dm], axis=0)
        per = ff // OWNERS
        for o in range(OWNERS):
            lo, hi = o * per // 128 * 128, (o * per + per + 127) // 128 * 128
            g = dot_tn(asum_ref[:, lo:hi], dm2)[o * per - lo : o * per - lo + per].astype(BF)
            for k in range(4):
                slope_ref[k, o % 2, o // 4, o // 2 % 2] = g[k * piece : (k + 1) * piece]
    y_out.wait()

    def two_back(b, sums):
        g_gain, g_bias, g_out = sums
        dh = dy_ref[rows_at(b), :]
        n2, r2 = norm_rows(x1_ref[rows_at(b), :])
        dx1 = dot(et_ref[rows_at(b), :], d_ref[...]) + norm_back(dh * vec(6), n2, r2)
        dy_ref[rows_at(b), :] = dx1
        da = dx1.astype(BF)
        da_ref[rows_at(b), :] = da
        return (
            g_gain + jnp.sum(dh * n2, axis=0, keepdims=True),
            g_bias + jnp.sum(dh, axis=0, keepdims=True),
            g_out + jnp.sum(da.astype(F32), axis=0, keepdims=True),
        )

    zero_row = jnp.zeros((1, width), F32)
    sums = lax.fori_loop(0, blocks, two_back, (zero_row,) * 3)
    gvec_ref[6:7, :] = sums[0]
    gvec_ref[7:8, :] = sums[1]
    gvec_ref[5:6, :] = sums[2]
    run(5, 2)
    if comm:
        end(dm_y)
        begin(dm_twin)
    for n in range(tiles):
        w_rows = w_ref[3].reshape(width, width)[n * TILE : n * TILE + TILE]
        h2_ref[:, n * TILE : n * TILE + TILE] = dot_nt(da_ref[...], w_rows).astype(BF)
    ctx_ref[...] = ctx_ref[...].T
    for n in range(tiles):
        cols = slice(n * TILE, n * TILE + TILE)
        w_ref[3, :, :, :, :, cols] = dot(ctx_ref[...], da_ref[:, cols]).astype(BF).reshape(w_ref.shape[1:-1] + (TILE,))
    if comm:
        pl.semaphore_wait(free, 1)
    run(3, 0)
    for b in range(blocks):
        rows = slice(b * BLK, b * BLK + BLK)
        heads = range(pairs)
        at = lambda n, h: slice(n * width + h * 128, n * width + h * 128 + 128)
        ps = [p_ref[b * pairs + h] for h in heads]
        dcs = [both_heads(h2_ref[rows, at(0, h)]) for h in heads]
        dps = [dot_nt(dcs[h], qkv_ref[rows, at(2, h)]) for h in heads]
        sums = [jnp.sum(ps[h] * dps[h], axis=-1, keepdims=True) for h in heads]
        dss = [(ps[h] * (dps[h] - sums[h])).astype(BF) for h in heads]
        dqs = [pick(dot(dss[h], qkv_ref[rows, at(1, h)])) * 0.125 for h in heads]
        dks = [dot_tn(dss[h], both_heads(qkv_ref[rows, at(0, h)])) * 0.125 for h in heads]
        dvs = [dot_tn(ps[h].astype(BF), dcs[h]) for h in heads]
        for h in heads:
            qkv_ref[rows, at(0, h)] = dqs[h].astype(BF)
            qkv_ref[rows, at(1, h)] = dks[h].astype(BF)
            qkv_ref[rows, at(2, h)] = dvs[h].astype(BF)
        for k, stage in BACK_STEPS[b]:
            run(k, stage)
        if comm and b == 2:
            end(dm_twin)
            end(to_z)
            g = dot_tn(as3[...].reshape(OWNERS * cap, 256), dms[...].reshape(OWNERS * cap, width))
            down_mine[...] = g[: 4 * piece].astype(BF)
            begin(down_x)
    h1_ref[...] = h1_ref[...].T
    for k in range(3):
        for n in range(tiles):
            cols = slice(n * TILE, n * TILE + TILE)
            d = qkv_ref[:, k * width + n * TILE : k * width + n * TILE + TILE]
            gvec_ref[2 + k : 3 + k, cols] = jnp.sum(d.astype(F32), axis=0, keepdims=True)
            w_ref[4 + k, :, :, :, :, cols] = dot(h1_ref[...], d).astype(BF).reshape(w_ref.shape[1:-1] + (TILE,))
        if comm and k == 1:
            pl.semaphore_wait(free, 1)
        run(k, 0)
        if k > 0:
            run(k - 1, 1)
    for n in range(tiles):
        total = jnp.zeros((tok, TILE), F32)
        for k in range(3):
            w_rows = w_ref[k].reshape(width, width)[n * TILE : n * TILE + TILE]
            total = total + dot_nt(qkv_ref[:, k * width : k * width + width], w_rows)
        x1_ref[:, n * TILE : n * TILE + TILE] = total
        for k, stage in (((2, 1),), ((3, 3), (4, 4)), ((5, 4), (6, 4)))[n]:
            run(k, stage)

    def one_back(b, sums):
        g_gain, g_bias = sums
        dh = x1_ref[rows_at(b), :]
        n1, r1 = norm_rows(x_ref[rows_at(b), :].astype(F32))
        dy_ref[rows_at(b), :] = dy_ref[rows_at(b), :] + norm_back(dh * vec(0), n1, r1)
        return (g_gain + jnp.sum(dh * n1, axis=0, keepdims=True), g_bias + jnp.sum(dh, axis=0, keepdims=True))

    sums = lax.fori_loop(0, blocks, one_back, (zero_row,) * 2)
    gvec_ref[0:1, :] = sums[0]
    gvec_ref[1:2, :] = sums[1]
    dx_out = pltpu.make_async_copy(dy_ref, dx_hbm, sems.at[13])
    dx_out.start()
    if comm:

        def small(slot, src, dst, peer):
            return remote(src, dst, v_send.at[slot], v_recv.at[slot], peer)

        steps = [
            small(0, vecs.at[0], vec_in.at[0], red.twin),
            small(1, vecs.at[1], vec_in.at[1], red.near_y),
            small(2, vecs.at[2], vec_in.at[2], red.near_x),
        ]
        spread = [small(3 + j, vec_z.at[red.z], vec_z.at[red.z], peer) for j, peer in enumerate(red.far_z)]
        vecs[0] = gvec_ref[...]
        steps[0].start()
        run(0, 2)
        run(1, 2)
        steps[0].wait()
        vecs[1] = vecs[0] + vec_in[0]
        steps[1].start()
        for k, stage in ((3, 4), (7, 4), (4, 5), (6, 5), (2, 2)):
            run(k, stage)
        steps[1].wait()
        vecs[2] = vecs[1] + vec_in[1]
        steps[2].start()
        run(0, 3)
        run(1, 3)
        end(down_x)
        gdown[...] = down_mine[...].astype(F32) + down_in[...].astype(F32)
        steps[2].wait()
        vec_z[red.z] = vecs[2] + vec_in[2]
        for item in spread:
            item.start()
        run(2, 3)
        run(3, 5)
        run(1, 4)
        run(0, 4)
        for item in spread:
            item.wait()
        own_rows(vec_z[0] + vec_z[1] + vec_z[2] + vec_z[3], own_out)
        run(2, 4)
        run(0, 5)
    else:
        copies = [pltpu.make_async_copy(w_ref.at[3 if k == 3 else 4 + k], grad_hbm.at[k], sems.at[k]) for k in range(4)]
        for k in range(4):
            rows = slice(k * piece, (k + 1) * piece)
            copies.append(pltpu.make_async_copy(wd_ref.at[:, :, :, rows], grad_hbm.at[4 + k], sems.at[4 + k]))
            for c in range(NC):
                copies.append(
                    pltpu.make_async_copy(slope_ref.at[k, c], grad_hbm.at[8 + k, :, :, c], sems.at[14 + 2 * k + c])
                )
        for copy in copies:
            copy.start()
        for copy in copies:
            copy.wait()
    dx_out.wait()


def text_call(comm, x, smalls, aim, wgt, lens, packed):
    tok, width = x.shape
    cap = aim.shape[0]
    ff = 4 * width
    piece = packed.shape[-2]
    anys = pl.BlockSpec(memory_space=pl.ANY)
    vmem = pl.BlockSpec(memory_space=pltpu.VMEM)
    smem = pl.BlockSpec(memory_space=pltpu.SMEM)
    sds = jax.ShapeDtypeStruct
    out_shape = [sds((tok, width), BF), sds((tok, width), F32), sds((16, 256 if comm else width), F32)]
    out_specs = [anys, anys, vmem]
    eight = (8, NZ, NY, NC, piece, width)
    scratch = [
        pltpu.VMEM(eight, BF),
        pltpu.VMEM((NZ, NY, NC, 4 * piece, width), BF),
        pltpu.VMEM((tok, width), BF),
        pltpu.VMEM((tok, 3 * width), BF),
        pltpu.VMEM((tok // BLK * (width // 128), 2 * BLK, BLK), F32),
        pltpu.VMEM((tok, width), BF),
        pltpu.VMEM((tok, width), F32),
        pltpu.VMEM((tok, width), BF),
        pltpu.VMEM((tok, ff), BF),
        pltpu.VMEM((ff // width, 2, NZ, NY, tok // 16, width), BF),
        pltpu.VMEM((2 * cap, ff), BF),
        pltpu.VMEM((cap, 128), jnp.int32),
        pltpu.VMEM((cap, tok), BF),
        pltpu.VMEM((tok, 128), BF),
        pltpu.VMEM((tok, width), F32),
        pltpu.VMEM((128, width), BF),
        pltpu.VMEM((tok, width), BF),
        pltpu.VMEM((128, ff), BF),
        pltpu.SemaphoreType.DMA((22,)),
    ]
    params = dict(vmem_limit_bytes=VMEM_LIMIT)
    if comm:
        out_shape += [
            sds((piece, 3 * width), F32), sds((piece, width), F32), sds((piece, ff), F32), sds((4 * piece, width), F32),
        ]
        out_specs += [vmem] * 4
        scratch += [
            pltpu.VMEM((16, width), F32),
            pltpu.VMEM((1, ff), F32),
            pltpu.VMEM((16, width), F32),
            pltpu.VMEM((4, NZ, NY, piece, width // 2), BF),
            pltpu.VMEM((4, NZ, piece, width // 2), BF),
            pltpu.VMEM((4, NZ - 1, piece, width // 2), BF),
            pltpu.VMEM((4, piece, width // 2), BF),
            pltpu.VMEM((4, piece, width // 2), BF),
            pltpu.VMEM((4, NZ, piece, width), BF),
            pltpu.VMEM((4, NZ - 1, piece, width), BF),
            pltpu.VMEM((4, piece, width), BF),
            pltpu.VMEM((4, piece, width), BF),
            pltpu.VMEM((3, 16, width), F32),
            pltpu.VMEM((3, 16, width), F32),
            pltpu.VMEM((NZ, 16, width), F32),
            *[pltpu.VMEM((NZ, NY, NC, cap, 256), BF)] * 4,
            pltpu.VMEM((NZ, NY, NC, cap, width), BF),
            pltpu.VMEM((4 * piece, width), BF),
            pltpu.VMEM((4 * piece, width), BF),
            pltpu.SemaphoreType.DMA((8, 7)),
            pltpu.SemaphoreType.DMA((8, 7)),
            pltpu.SemaphoreType.DMA((6,)),
            pltpu.SemaphoreType.DMA((6,)),
            pltpu.SemaphoreType.DMA((11,)),
            pltpu.SemaphoreType.DMA((11,)),
            pltpu.SemaphoreType.REGULAR,
        ]
        params.update(collective_id=1, has_side_effects=True)
    else:
        out_shape += [sds(packed.shape, BF)]
        out_specs += [anys]
    return pl.pallas_call(
        functools.partial(text_body, comm),
        out_shape=out_shape,
        in_specs=[vmem] * (3 + len(smalls)) + [smem, anys],
        out_specs=out_specs,
        scratch_shapes=scratch,
        compiler_params=pltpu.CompilerParams(**params),
    )(x, *smalls, aim, wgt, lens, packed)


def pack(wqkv, wout, wup, wdown):
    width = wout.shape[1]
    parts = [wqkv[:, k * width : (k + 1) * width] for k in range(3)] + [wout]
    parts += [wup[:, k * width : (k + 1) * width] for k in range(4)]
    down = wdown.reshape(OWNERS, 4, width // OWNERS, width)
    parts += [down[:, k].reshape(width, width) for k in range(4)]
    return jnp.stack(parts).reshape(12, NZ, NY, NC, width // OWNERS, width)


def unpack(packed):
    width = packed.shape[-1]
    flat = packed.reshape(12, width, width)
    wqkv = jnp.concatenate([flat[k] for k in range(3)], axis=1)
    wup = jnp.concatenate([flat[4 + k] for k in range(4)], axis=1)
    down = flat[8:].reshape(4, OWNERS, width // OWNERS, width)
    return wqkv, flat[3], wup, jnp.swapaxes(down, 0, 1).reshape(4 * width, width)


def vectors(g1, b1, bqv, bout, g2, b2, bup, bdown):
    width = g1.shape[0]
    zero = jnp.zeros((width,), BF)
    rows = [g1, b1, bqv[:width], zero, bqv[width:], bout, g2, b2, bdown] + [zero] * 7
    return jnp.stack(rows).astype(F32), bup.astype(F32).reshape(1, -1)


def hand_out_body(part, *refs):
    big, own, outs, bufs, sem_in, sem_out = refs[:6], refs[6], refs[7:22], refs[22:28], refs[28], refs[29]
    loss, y, dx, g1, b1, gqkv, qv, gout, bout, g2, b2, gup, bup, gdown, bdown = outs
    pairs = list(zip(big, bufs, (y, dx, gqkv, gout, gup, gdown)))
    ins, backs = [], []
    for i, (src, buf, dst) in enumerate(pairs):
        pieces = 4 if i < 2 else 1
        n = src.shape[0] // pieces
        for p in range(pieces):
            rows = pl.ds(p * n, n)
            slot = 4 * i + p
            ins.append(pltpu.make_async_copy(src.at[rows], buf.at[rows], sem_in.at[slot]))
            backs.append(pltpu.make_async_copy(buf.at[rows], dst.at[rows], sem_out.at[slot]))
    for copy in ins:
        copy.start()
    for ref, at, lanes in (
        (g1, 0, part), (b1, 1, part), (qv, 2, 2 * part), (bout, 3, part), (g2, 4, part), (b2, 5, part), (bdown, 6, part),
        (bup, 8, 4 * part),
    ):
        ref[...] = own[at : at + 1, :lanes].reshape(lanes)
    loss[...] = own[7:8, :1]
    for copy, back in zip(ins, backs):
        copy.wait()
        back.start()
    for back in backs:
        back.wait()


def hand_out(big, own, part):
    sds = jax.ShapeDtypeStruct
    anys = pl.BlockSpec(memory_space=pl.ANY)
    vmem = pl.BlockSpec(memory_space=pltpu.VMEM)
    like = lambda v: sds(v.shape, v.dtype)
    line = lambda n: sds((n * part,), F32)
    y, dx, gqkv, gout, gup, gdown = big
    return pl.pallas_call(
        functools.partial(hand_out_body, part),
        out_shape=[
            sds((1, 1), F32), like(y), like(dx), line(1), line(1), like(gqkv), line(2), like(gout), line(1), line(1),
            line(1), like(gup), line(4), like(gdown), line(1),
        ],
        in_specs=[anys] * 6 + [vmem],
        out_specs=[vmem, anys, anys, vmem, vmem, anys, vmem, anys, vmem, vmem, vmem, anys, vmem, anys, vmem],
        scratch_shapes=[pltpu.VMEM(v.shape, v.dtype) for v in big]
        + [pltpu.SemaphoreType.DMA((24,)), pltpu.SemaphoreType.DMA((24,))],
        compiler_params=pltpu.CompilerParams(vmem_limit_bytes=VMEM_LIMIT),
    )(*big, own)


def group_weight(group_ids, live):
    match = group_ids[:, None] == jnp.arange(1024, dtype=jnp.int32)[None, :]
    local = jnp.sum(jnp.where(match & live[:, None], 1.0, 0.0).astype(F32), axis=0)
    size = lax.psum(local, ("dp", "fsdp"))
    members = jnp.sum(jnp.where(match, size[None, :], 0.0), axis=1)
    return jnp.where(live, 1.0 / jnp.maximum(members, 1.0), 0.0)


def any_mesh(text, weights, image_weights, patches, targets, group_ids, cap_len, slot_counts):
    cap = targets.shape[0]
    gathered = [lax.all_gather(w, "fsdp", axis=0, tiled=True) for w in weights]
    g1, b1, wqkv, bqv, wout, bout, g2, b2, wup, bup, wdown, bdown = gathered
    live = jnp.arange(cap, dtype=jnp.int32) < slot_counts[0]
    wgt = group_weight(group_ids, live)
    (aim,) = image_call(patches, targets, image_weights)
    vec, bup_row = vectors(g1, b1, bqv, bout, g2, b2, bup, bdown)
    y, dx, gvec, packed = text_call(
        False, text, (vec, bup_row), aim, jnp.broadcast_to(wgt[:, None], (cap, 128)), cap_len, pack(wqkv, wout, wup, wdown)
    )
    gqkv, gout, gup, gdown = unpack(packed)
    grads = [
        gvec[0], gvec[1], gqkv, jnp.concatenate([gvec[2], gvec[4]]), gout, gvec[5], gvec[6], gvec[7], gup,
        gvec[12:16].reshape(-1), gdown, gvec[8],
    ]
    owned = [lax.psum_scatter(g.astype(F32), "fsdp", scatter_dimension=0, tiled=True) for g in grads]
    return (lax.psum(gvec[9, 0], ("dp", "fsdp")), y, dx, *[lax.psum(g, "dp") for g in owned])


def block_mesh(text, weights, image_weights, patches, targets, group_ids, cap_len, slot_counts):
    g1, b1, wqkv, bqv, wout, bout, g2, b2, wup, bup, wdown, bdown = weights
    width = wout.shape[1]
    aim, packed, all_small, wgt = image_call(
        patches, targets, image_weights, (wqkv, wout, wup, wdown, g1, b1, bqv, bout, g2, b2, bup, bdown, group_ids, slot_counts)
    )
    y, dx, gvec, gqkv, gout, gup, gdown = text_call(True, text, (all_small,), aim, wgt, cap_len, packed)
    part = width // OWNERS
    loss, y, dx, g1, b1, gqkv, qv, gout, bout, g2, b2, gup, bup, gdown, bdown = hand_out(
        (y, dx, gqkv, gout, gup, gdown), gvec, part
    )
    return loss[0, 0], y, dx, g1, b1, gqkv, qv, gout, bout, g2, b2, gup, bup, gdown, bdown


def solution(mesh):
    shape = dict(mesh.shape)
    inner = block_mesh if (shape["dp"], shape["fsdp"]) == (2, OWNERS) else any_mesh

    def per_device(text_in, *rest):
        weights, image_weights = rest[:12], rest[12:24]
        patches, targets, group_ids, cap_len, slot_counts = rest[24:]
        return inner(
            text_in, weights, image_weights, jnp.transpose(patches, (1, 0, 2)), targets, group_ids, cap_len, slot_counts
        )

    both = ("dp", "fsdp")
    owned, table = P("fsdp"), P("fsdp", None)
    text_specs = (owned, owned, table, owned, table, owned, owned, owned, table, owned, table, owned)
    return jax.shard_map(
        per_device,
        mesh=mesh,
        in_specs=(P(both, None), *text_specs, *([P()] * 12), P(both, None, None), P(both, None), P(both), P(both), P(both)),
        out_specs=(P(), P(both, None), P(both, None), *text_specs),
        check_vma=False,
    )
```

```python
import functools

import jax
import jax.numpy as jnp
from jax import lax
from jax.experimental import pallas as pl
from jax.experimental.pallas import tpu as pltpu
from jax.sharding import PartitionSpec as P

HEAD = 64
EPS = 1e-06
ROOT_HALF = 0.7071067811865476
INV_ROOT_TAU = 0.3989422804014327
DEAD = -8e9
BF = jnp.bfloat16
F32 = jnp.float32
BLK = 128
TILE = 256
NZ, NY, NC = 4, 2, 2
OWNERS = NZ * NY * NC
MESH = pl.DeviceIdType.MESH
VMEM_LIMIT = 63 * 2**20
LAGS = (-2, 1, 2, 3)
SPLIT = (0, 3, 4, 6)
WHOLE = (1, 2, 5, 7)
LANDING = {4: 0, 5: 1, 6: 2, 7: 3, 3: 4, 0: 5, 1: 6, 2: 7}
BACK_STEPS = (
    ((3, 1),),
    ((6, 2), (7, 2)),
    ((4, 3),),
    ((5, 3),),
    ((3, 2),),
    ((6, 3), (7, 3)),
)
SMALL = ((0, 0), (0, 4), (1, 2), (2, 0), (2, 4))


def norm_rows(values):
    centered = values - jnp.mean(values, axis=-1, keepdims=True)
    inv_std = lax.rsqrt(jnp.mean(centered * centered, axis=-1, keepdims=True) + EPS)
    return centered * inv_std, inv_std


def norm_back(u, n, r):
    return r * (u - jnp.mean(u, axis=-1, keepdims=True) - n * jnp.mean(u * n, axis=-1, keepdims=True))


def gelu_exact(v):
    return 0.5 * v * (1.0 + lax.erf(v * ROOT_HALF))


def dot(a, b):
    return jnp.dot(a, b, preferred_element_type=F32)


def dot_nt(a, b):
    return lax.dot_general(a, b, (((1,), (1,)), ((), ())), preferred_element_type=F32)


def dot_tn(a, b):
    return lax.dot_general(a, b, (((0,), (0,)), ((), ())), preferred_element_type=F32)


def split(v):
    high = v.astype(BF)
    return high, (v - high.astype(F32)).astype(BF)


def row(ref, start=0, size=None):
    size = ref.shape[0] if size is None else size
    return ref[pl.ds(start, size)].astype(F32).reshape(1, size)


def place():
    f = lax.axis_index("fsdp")
    return lax.axis_index("dp"), f // (NY * NC), (f // NC) % NY, f % NC


def device(x, z, y, c):
    return (x, (z * NY + y) * NC + c)


def greet(peers):
    barrier = pltpu.get_barrier_semaphore()
    for peer in peers:
        pl.semaphore_signal(barrier, inc=1, device_id=peer, device_id_type=MESH)
    pl.semaphore_wait(barrier, len(peers))


def remote(src, dst, send, recv, peer):
    return pltpu.make_async_remote_copy(
        src_ref=src, dst_ref=dst, send_sem=send, recv_sem=recv, device_id=peer, device_id_type=MESH
    )


class Gather:
    def __init__(self, g_ref, send, recv):
        self.g, self.send, self.recv = g_ref, send, recv
        self.chunks = g_ref.shape[0]
        half = g_ref.shape[-1] // 2
        self.x, self.z, self.y, self.c = place()
        self.mine = pl.ds(pl.multiple_of(self.x * half, 128), half)
        self.far_z = [device(self.x, (self.z + j) % NZ, self.y, self.c) for j in range(1, NZ)]
        self.near_y = device(self.x, self.z, 1 - self.y, self.c)
        self.near_x = device(1 - self.x, self.z, self.y, self.c)
        self.twin = device(self.x, self.z, self.y, 1 - self.c)
        self.peers = self.far_z + [self.near_y, self.near_x, self.twin]

    def copy(self, k, slot, ref, peer):
        return remote(ref, ref, self.send.at[k, slot], self.recv.at[k, slot], peer)

    def along_z(self, k):
        ref = self.g.at[k, self.z, self.y, self.c, :, self.mine]
        return [self.copy(k, j, ref, peer) for j, peer in enumerate(self.far_z)]

    def first(self, k):
        top, rest = pl.ds(0, 32), pl.ds(32, 16)
        return [self.copy(k, 3, self.g.at[k, :, self.y, self.c, top, self.mine], self.near_y)] + [
            self.copy(k, 4 + j, self.g.at[k, (self.z + 1 + j) % NZ, self.y, self.c, rest, self.mine], self.near_x)
            for j in range(3)
        ]

    def second(self, k):
        top, rest = pl.ds(0, 32), pl.ds(32, 16)
        return (
            [
                self.copy(k, 7 + j, self.g.at[k, (self.z + 1 + j) % NZ, :, self.c, top, self.mine], self.near_x)
                for j in range(3)
            ]
            + [self.copy(k, 10, self.g.at[k, self.z, 1 - self.y, self.c, top, self.mine], self.near_x)]
            + [self.copy(k, 11, self.g.at[k, :, self.y, self.c, rest], self.near_y)]
        )

    def last(self, k):
        return [self.copy(k, 12, self.g.at[k, :, :, self.c], self.twin)]

    def tick(self, t):
        def start(copies):
            for copy in copies:
                copy.start()

        def arrive(copies):
            for copy in copies:
                copy.wait_recv()

        def stage(lag, action):
            @pl.when(jnp.logical_and(t - lag >= 0, t - lag < self.chunks))
            def _():
                action(t - lag)

        def one(k):
            start(self.along_z(k))

        def two(k):
            arrive(self.along_z(k))
            start(self.first(k))

        def three(k):
            arrive(self.first(k))
            start(self.second(k))

        def four(k):
            arrive(self.second(k))
            start(self.last(k))

        stage(LAGS[0], one)
        stage(LAGS[1], two)
        stage(LAGS[2], three)
        stage(LAGS[3], four)

    def finish(self):
        def end(k, _):
            for copy in self.last(k):
                copy.wait()
            for copy in self.along_z(k) + self.first(k) + self.second(k):
                copy.wait_send()
            return 0

        lax.fori_loop(0, self.chunks, end, 0)


def image_body(comm, group, *refs):
    (x_hbm, t_ref, g1, b1, bqv, bout, g2, b2, bup, bdown, wqkv_hbm, wout_hbm, wup_hbm, wdown_hbm), refs = refs[:14], refs[14:]
    if comm:
        (oqkv, oout, oup, odown, *smalls, gid, count), refs = refs[:14], refs[14:]
        (aim_ref, gath, vec_ref, wgt_ref), refs = refs[:4], refs[4:]
    else:
        (aim_ref,), refs = refs[:1], refs[1:]
    (x_ref, wqkv, wout, wup, wdown, h_ref, qkv_ref, ctx_ref, act_ref, xm_ref, sems), refs = refs[:11], refs[11:]
    patches, cap, width = x_hbm.shape
    ff = wup.shape[1]
    steps = cap // group
    rows = patches * group
    loads = [
        pltpu.make_async_copy(src, dst, sems.at[i])
        for i, (src, dst) in enumerate(
            [(x_hbm, x_ref), (wqkv_hbm, wqkv), (wout_hbm, wout), (wup_hbm, wup), (wdown_hbm, wdown)]
        )
    ]
    if comm:
        ids, vecs, own_ref, own_sem, g_send, g_recv, s_send, s_recv = refs
        gather = Gather(gath, g_send, g_recv)
        x, z, y, c = gather.x, gather.z, gather.y, gather.c
        own = []
        for k in range(gath.shape[0]):
            if k < 3:
                src = oqkv.at[:, k * width : k * width + width]
            elif k < 4:
                src = oout
            elif k < 8:
                src = oup.at[:, (k - 4) * width : (k - 3) * width]
            else:
                src = odown.at[(k - 8) * oout.shape[0] : (k - 7) * oout.shape[0]]
            own.append((pltpu.make_async_copy(src, own_ref.at[k], own_sem.at[k]), pltpu.make_async_copy(own_ref.at[k], gath.at[k, z, y, c], own_sem.at[k])))
        for copy, _out in own:
            copy.start()
        for load in loads:
            load.start()
        lines = []
        for ref in smalls:
            n = ref.shape[0]
            for at in range(0, n, 128):
                take = min(128, n - at)
                line = row(ref)[:, at : at + take]
                lines.append(jnp.concatenate([line, jnp.zeros((1, 128 - take), F32)], axis=1) if take < 128 else line)
        lines.append(jnp.zeros((16 - len(lines), 128), F32))
        vecs[z, y, c] = jnp.concatenate(lines, axis=0).astype(BF)
        lane = lax.broadcasted_iota(jnp.int32, (8, 128), 1)
        line = jnp.full((8, 128), -1, jnp.int32)
        for i in range(cap):
            line = jnp.where(lane == i, jnp.where(i < count[0], gid[i], -1), line)
        ids[x, z, y, c] = line
        greet(gather.peers)

        def small(slot, ref, peer):
            return remote(ref, ref, s_send.at[slot], s_recv.at[slot], peer)

        small_z = [small(j, ids.at[x, z, y, c], peer) for j, peer in enumerate(gather.far_z)]
        small_z += [small(3 + j, vecs.at[z, y, c], peer) for j, peer in enumerate(gather.far_z)]
        small_y = [small(6, ids.at[x, :, y, c], gather.near_y), small(7, vecs.at[:, y, c], gather.near_y)]
        small_x = [small(8, ids.at[x, :, :, c], gather.near_x), small(9, vecs.at[:, :, c], gather.twin)]
        small_c = [small(10, ids.at[:, :, :, c], gather.twin)]
        stages = [small_z, small_y, small_x, small_c]
        for copy, out in own:
            copy.wait()
            out.start()
        for _copy, out in own:
            out.wait()
        for k in range(-LAGS[0]):
            for copy in gather.along_z(k):
                copy.start()

        def tick(step, t):
            gather.tick(step * 6 + t)
            for i, (at_step, at) in enumerate(SMALL):
                if at == t:

                    @pl.when(step == at_step)
                    def _():
                        if i > 0:
                            for copy in stages[i - 1]:
                                copy.wait_recv()
                        if i < 4:
                            for copy in stages[i]:
                                copy.start()

    else:
        for load in loads:
            load.start()

        def tick(step, t):
            pass

    lane_q = lax.broadcasted_iota(jnp.int32, (112, 128), 1)
    low_half = lane_q < HEAD
    key = lax.broadcasted_iota(jnp.int32, (224, 128), 1)
    second = lax.broadcasted_iota(jnp.int32, (224, 128), 0) % 112 >= 56
    first_key = jnp.where(second, 64, 0)
    key_ok = (key >= first_key) & (key < first_key + patches)
    ones = jnp.ones((128, 128), BF)
    g1v, b1v, g2v, b2v = row(g1), row(b1), row(g2), row(b2)
    bias = [row(bqv, 0, width), jnp.zeros((1, width), F32), row(bqv, width, width)]
    boutv, bupv, bdownv = row(bout), row(bup), row(bdown)
    xm_ref[...] = jnp.zeros_like(xm_ref)
    for load in loads[:4]:
        load.wait()

    def chunk_step(step, _):
        c0 = pl.multiple_of(step * group, group)
        caps = pl.ds(c0, group)
        tick(step, 0)

        def norm_one(p, _):
            value = x_ref[pl.ds(p * 5, 5), caps, :].astype(F32).reshape(5 * group, width)
            n, _inv = norm_rows(value)
            h_ref[pl.ds(pl.multiple_of(p * 5 * group, 16), 5 * group), :] = (n * g1v + b1v).astype(BF)
            return 0

        lax.fori_loop(0, patches // 5, norm_one, 0)
        for n in range(3 * width // TILE):
            cols = slice(n * TILE, n * TILE + TILE)
            part, off = divmod(n * TILE, width)
            value = dot(h_ref[...], wqkv[:, cols]) + bias[part][:, off : off + TILE]
            qkv_ref[2 * n] = value[:, :128]
            qkv_ref[2 * n + 1] = value[:, 128:]
        tick(step, 1)

        def attend(p, _):
            def load(col, tall):
                parts = []
                for k in range(2):
                    v = qkv_ref[col // 128, pl.ds(2 * p + k, patches, stride=group), :]
                    parts.append(jnp.concatenate([v, jnp.zeros((tall - patches, 128), F32)], axis=0))
                return jnp.concatenate(parts, axis=0).astype(BF)

            def scores(h):
                q = load(h * 128, 56)
                zero = jnp.zeros_like(q)
                q2 = jnp.concatenate([jnp.where(low_half, q, zero), jnp.where(low_half, zero, q)], axis=0)
                return jnp.where(key_ok, dot_nt(q2, load(width + h * 128, 64)), DEAD)

            for first in range(0, width // 128, 6):
                heads = range(first, first + 6)
                ss = [scores(h) for h in heads]
                tops = [jnp.max(s, axis=-1, keepdims=True) for s in ss]
                es = [jnp.exp((s - top) * 0.125).astype(BF) for s, top in zip(ss, tops)]
                os = [dot(e, jnp.concatenate([load(2 * width + h * 128, 64), ones], axis=1)) for e, h in zip(es, heads)]
                for o, h in zip(os, heads):
                    num = jnp.where(low_half, o[:112, :128], o[112:, :128])
                    den = jnp.where(low_half, o[:112, 128:], o[112:, 128:])
                    out = num / den
                    for k in range(2):
                        ctx_ref[h, pl.ds(2 * p + k, patches, stride=group), :] = out[56 * k : 56 * k + patches]
            return 0

        lax.fori_loop(0, group // 4, attend, 0)
        tick(step, 2)
        lax.fori_loop(group // 4, group // 2, attend, 0)
        tick(step, 3)

        def project(p, _):
            span = pl.ds(pl.multiple_of(p * 10 * group, 16), 10 * group)
            ctx = jnp.concatenate([ctx_ref[h, span, :] for h in range(width // 128)], axis=1).astype(BF)
            x1 = x_ref[pl.ds(p * 10, 10), caps, :].astype(F32).reshape(10 * group, width) + dot(ctx, wout[...]) + boutv
            xm_ref[caps, :] += jnp.sum(x1.reshape(10, group, width), axis=0)
            n, _inv = norm_rows(x1)
            h_ref[span, :] = (n * g2v + b2v).astype(BF)
            return 0

        lax.fori_loop(0, patches // 10, project, 0)
        tick(step, 4)
        for n in range(ff // TILE):
            cols = slice(n * TILE, n * TILE + TILE)
            act = gelu_exact(dot(h_ref[...], wup[:, cols]) + bupv[:, cols])
            act_ref[caps, cols] = jnp.sum(act.reshape(patches, group, TILE), axis=0)
            if n == ff // TILE // 2:
                tick(step, 5)
        return 0

    lax.fori_loop(0, steps, chunk_step, 0)
    loads[4].wait()
    both = jnp.concatenate(split(act_ref[...] * (1.0 / patches)), axis=0)
    for n in range(width // TILE):
        cols = slice(n * TILE, n * TILE + TILE)
        o = dot(both, wdown[:, cols])
        aim_ref[:, cols] = (
            o[:cap] + o[cap:] + xm_ref[:, cols] * (1.0 / patches) + bdownv[:, cols] + t_ref[:, cols].astype(F32)
        )
    if comm:
        column = lax.broadcasted_iota(jnp.int32, (cap, 128), 0)
        mine = jnp.zeros((cap, 128), jnp.int32)
        for i in range(cap):
            mine = jnp.where(column == i, gid[i], mine)
        total = jnp.zeros((cap, 128), F32)
        for dx in range(2):
            for o in range(OWNERS):
                line = ids[dx, o // 4, o // 2 % 2, o % 2][0:1]
                total = total + jnp.where(mine == line, 1.0, 0.0)
        members = jnp.sum(total, axis=1, keepdims=True)
        wgt = jnp.where(column < count[0], 1.0 / jnp.maximum(members, 1.0), 0.0)
        wgt_ref[...] = wgt
        vec_ref[...] = vecs[...]
        gather.finish()
        for stage in stages:
            for copy in stage:
                copy.wait_send()


def image_call(patches, targets, weights, extra=(), group=16):
    comm = bool(extra)
    g1, b1, wqkv, bqv, wout, bout, g2, b2, wup, bup, wdown, bdown = weights
    count, cap, width = patches.shape
    ff = wup.shape[1]
    anys = pl.BlockSpec(memory_space=pl.ANY)
    vmem = pl.BlockSpec(memory_space=pltpu.VMEM)
    smem = pl.BlockSpec(memory_space=pltpu.SMEM)
    rows = count * group
    sds = jax.ShapeDtypeStruct
    out_shape = [sds((cap, width), F32)]
    out_specs = [vmem]
    in_specs = [anys] + [vmem] * 9 + [anys] * 4
    scratch = [
        pltpu.VMEM(patches.shape, BF),
        pltpu.VMEM(wqkv.shape, BF),
        pltpu.VMEM(wout.shape, BF),
        pltpu.VMEM(wup.shape, BF),
        pltpu.VMEM(wdown.shape, BF),
        pltpu.VMEM((rows, width), BF),
        pltpu.VMEM((3 * width // 128, rows, 128), F32),
        pltpu.VMEM((width // 128, rows, 128), F32),
        pltpu.VMEM((cap, ff), F32),
        pltpu.VMEM((cap, width), F32),
        pltpu.SemaphoreType.DMA((5,)),
    ]
    params = dict(vmem_limit_bytes=VMEM_LIMIT)
    if comm:
        chunks = 12
        piece = extra[1].shape
        in_specs += [anys] * 4 + [vmem] * 8 + [smem] * 2
        out_shape += [
            sds((chunks, NZ, NY, NC) + piece, BF),
            sds((NZ, NY, NC, 16, 128), BF),
            sds((cap, 128), F32),
        ]
        out_specs += [anys, vmem, vmem]
        scratch += [
            pltpu.VMEM((2, NZ, NY, NC, 8, 128), jnp.int32),
            pltpu.VMEM((NZ, NY, NC, 16, 128), BF),
            pltpu.VMEM((chunks,) + piece, BF),
            pltpu.SemaphoreType.DMA((chunks,)),
            pltpu.SemaphoreType.DMA((chunks, 13)),
            pltpu.SemaphoreType.DMA((chunks, 13)),
            pltpu.SemaphoreType.DMA((11,)),
            pltpu.SemaphoreType.DMA((11,)),
        ]
        params.update(collective_id=0, has_side_effects=True)
    return pl.pallas_call(
        functools.partial(image_body, comm, group),
        out_shape=out_shape,
        in_specs=in_specs,
        out_specs=out_specs,
        scratch_shapes=scratch,
        compiler_params=pltpu.CompilerParams(**params),
    )(patches, targets, g1, b1, bqv, bout, g2, b2, bup, bdown, wqkv, wout, wup, wdown, *extra)


class Reduce:
    def __init__(self, landing, split_bufs, whole_bufs, sems):
        self.landing, self.split_bufs, self.whole_bufs = landing, split_bufs, whole_bufs
        self.send, self.recv = sems
        self.x, self.z, self.y, self.c = place()
        self.far_z = [device(self.x, (self.z + j) % NZ, self.y, self.c) for j in range(1, NZ)]
        self.near_y = device(self.x, self.z, 1 - self.y, self.c)
        self.near_x = device(1 - self.x, self.z, self.y, self.c)
        self.twin = device(self.x, self.z, self.y, 1 - self.c)
        self.peers = self.far_z + [self.near_y, self.near_x, self.twin]
        self.plans = {}

    def add(self, k, grad, out):
        z, y, c = self.z, self.y, self.c
        full = slice(None)

        def copy(slot, src, dst, peer):
            return remote(src, dst, self.send.at[k, slot], self.recv.at[k, slot], peer)

        def start(items):
            for item in items:
                item.start()

        def wait(items):
            for item in items:
                item.wait()

        def add_into(target, value):
            target[...] = target[...] + value

        landed = self.landing(k)
        c0 = [copy(0, grad(full, full, 1 - c, full), landed, self.twin)]
        if k in WHOLE:
            n = WHOLE.index(k)
            in_y, in_z, mine, other = (buf.at[n] for buf in self.whole_bufs)
            c1 = [copy(1, grad(full, 1 - y, c, full), in_y, self.near_y)]
            c2 = [
                copy(1 + j, grad((z + j) % NZ, y, c, full), in_z.at[j - 1], self.far_z[j - 1]) for j in range(1, NZ)
            ]
            c3 = [copy(5, mine, other, self.near_x)]

            def s1():
                wait(c0)
                add_into(grad(full, full, c, full), landed[...])
                start(c1)

            def s2():
                wait(c1)
                add_into(grad(full, y, c, full), in_y[...])
                start(c2)

            def s3():
                wait(c2)
                total = grad(z, y, c, full)[...].astype(F32)
                for j in range(NZ - 1):
                    total = total + in_z[j].astype(F32)
                mine[...] = total.astype(BF)
                start(c3)

            def s4():
                wait(c3)
                out(pl.ds(0, mine.shape[-1]))[...] = mine[...].astype(F32) + other[...].astype(F32)

            self.plans[k] = [lambda: start(c0), s1, s2, s3, s4]
            return
        n = SPLIT.index(k)
        in_x, in_y, in_z, sum_x, other = (buf.at[n] for buf in self.split_bufs)
        half = sum_x.shape[-1]
        mine = pl.ds(pl.multiple_of(self.x * half, 128), half)
        theirs = pl.ds(pl.multiple_of((1 - self.x) * half, 128), half)
        c1 = [copy(1, grad(full, full, c, theirs), in_x, self.near_x)]
        c2 = [copy(2, grad(full, 1 - y, c, mine), in_y, self.near_y)]
        c3 = [copy(2 + j, grad((z + j) % NZ, y, c, mine), in_z.at[j - 1], self.far_z[j - 1]) for j in range(1, NZ)]
        c4 = [copy(6, sum_x, other, self.near_x)]

        def s1():
            wait(c0)
            add_into(grad(full, full, c, full), landed[...])
            start(c1)

        def s2():
            wait(c1)
            add_into(grad(full, full, c, mine), in_x[...])
            start(c2)

        def s3():
            wait(c2)
            add_into(grad(full, y, c, mine), in_y[...])
            start(c3)

        def s4():
            wait(c3)
            total = grad(z, y, c, mine)[...].astype(F32)
            for j in range(NZ - 1):
                total = total + in_z[j].astype(F32)
            rounded = total.astype(BF)
            sum_x[...] = rounded
            out(mine)[...] = rounded.astype(F32)
            start(c4)

        def s5():
            wait(c4)
            out(theirs)[...] = other[...].astype(F32)

        self.plans[k] = [lambda: start(c0), s1, s2, s3, s4, s5]

    def run(self, k, stage):
        self.plans[k][stage]()


def one_hot(rows, start, width, limit):
    i = lax.broadcasted_iota(jnp.int32, (rows, width), 0)
    j = lax.broadcasted_iota(jnp.int32, (rows, width), 1)
    return jnp.where((j == i + start) & (i < limit), 1.0, 0.0).astype(BF)


def spread_rows(all_small, vec_ref, bup_ref):
    width = vec_ref.shape[1]
    part = width // OWNERS
    tile = lambda o: all_small[o // 4, o // 2 % 2, o % 2]
    plain = jnp.zeros((16, width), F32)
    for o in range(OWNERS):
        plain = plain + dot(tile(o), one_hot(128, o * part, width, part))
    halves = []
    for h in range(2):
        total = jnp.zeros((16, width), F32)
        for m in range(8):
            total = total + dot(tile(8 * h + m), one_hot(128, 2 * m * part, width, 2 * part))
        halves.append(total[2:3])
    zero = jnp.zeros((1, width), F32)
    order = [plain[0:1], plain[1:2], halves[0], zero, halves[1], plain[3:4], plain[4:5], plain[5:6], plain[8:9]]
    vec_ref[...] = jnp.concatenate(order + [jnp.zeros((7, width), F32)], axis=0)
    first = [one_hot(128, 4 * m * part, width, 128) for m in range(4)]
    rest = [one_hot(128, 4 * m * part + 128, width, 4 * part - 128) for m in range(4)]
    for q in range(4):
        total = jnp.zeros((1, width), F32)
        for m in range(4):
            t = tile(4 * q + m)
            total = total + dot(t, first[m])[6:7] + dot(t, rest[m])[7:8]
        bup_ref[:, q * width : (q + 1) * width] = total


def own_rows(gvec, own_ref):
    width = gvec.shape[1]
    part = width // OWNERS
    me = lax.axis_index("fsdp")
    high = gvec.astype(BF)
    left = gvec - high.astype(F32)
    mid = left.astype(BF)
    low = (left - mid.astype(F32)).astype(BF)

    def pick(start, lanes):
        i = lax.broadcasted_iota(jnp.int32, (width, lanes), 0)
        j = lax.broadcasted_iota(jnp.int32, (width, lanes), 1)
        hot = jnp.where(i == j + start, 1.0, 0.0).astype(BF)
        return dot(high, hot) + dot(mid, hot) + dot(low, hot)

    plain = pick(me * part, 256)
    pair = pick(me % 8 * (2 * part), 256)
    four = pick(me % 4 * (4 * part), 256)
    qv = jnp.where(me < 8, pair[2:3], pair[4:5])
    q = me // 4
    bup = jnp.where(q == 0, four[12:13], jnp.where(q == 1, four[13:14], jnp.where(q == 2, four[14:15], four[15:16])))
    loss = jnp.broadcast_to(gvec[9:10, :1], (1, 256))
    rows = [plain[0:1], plain[1:2], qv, plain[5:6], plain[6:7], plain[7:8], plain[8:9], loss, bup]
    own_ref[...] = jnp.concatenate(rows + [jnp.zeros((7, 256), F32)], axis=0)


def text_body(comm, *refs):
    if comm:
        (x_ref, all_small, aim_ref, wgt_ref, len_ref, w_hbm), refs = refs[:6], refs[6:]
    else:
        (x_ref, vec_ref, bup_ref, aim_ref, wgt_ref, len_ref, w_hbm), refs = refs[:7], refs[7:]
    if comm:
        (y_hbm, dx_hbm, own_out, gqkv, gout, gup, gdown), refs = refs[:7], refs[7:]
    else:
        (y_hbm, dx_hbm, gvec_ref, grad_hbm), refs = refs[:4], refs[4:]
    (w_ref, wd_ref, h1_ref, qkv_ref, p_ref, ctx_ref, x1_ref, h2_ref, act_ref, slope_ref, asum_ref, lcol_ref, e_ref, et_ref,
     dy_ref, d_ref, da_ref, dmw_ref, sems), refs = refs[:19], refs[19:]
    tok, width = x_ref.shape
    cap = aim_ref.shape[0]
    seq = tok // cap
    ff = 4 * width
    blocks = tok // BLK
    pairs = width // 128
    tiles = width // TILE
    piece = w_ref.shape[-2]

    def chunk(k):
        return w_ref.at[k] if k < 8 else wd_ref.at[:, :, :, (k - 8) * piece : (k - 7) * piece]

    loads = [pltpu.make_async_copy(w_hbm.at[k], chunk(k), sems.at[k]) for k in range(12)]
    for load in loads:
        load.start()
    if comm:
        vec_ref, bup_ref, gvec_ref, *bufs, vecs, vec_in, vec_z, as0, as1, as2, as3, dms, down_mine, down_in, r_send, r_recv, v_send, v_recv, f_send, f_recv, free = refs
        split_bufs, whole_bufs = bufs[:5], bufs[5:]
        red = Reduce(
            lambda k: slope_ref.at[LANDING[k] // 2, LANDING[k] % 2], split_bufs, whole_bufs, (r_send, r_recv)
        )
        outs = [gqkv, gqkv, gqkv, gout, gup, gup, gup, gup]

        def view(k):
            if k >= 4:
                rows = slice((k - 4) * piece, (k - 3) * piece)
                return lambda a, b, d, lanes: wd_ref.at[a, b, d, rows, lanes]
            n = 3 if k == 3 else 4 + k
            return lambda a, b, d, lanes: w_ref.at[n, a, b, d, :, lanes]

        def result(k):
            base = (0, 1, 2, 0, 0, 1, 2, 3)[k] * width
            return lambda lanes: outs[k].at[:, pl.ds(pl.multiple_of(base + lanes.start, 128), lanes.size)]

        for k in range(8):
            red.add(k, view(k), result(k))
        z, y_at, c = red.z, red.y, red.c

        def side(slot, src, dst, peer):
            return remote(src, dst, f_send.at[slot], f_recv.at[slot], peer)

        to_twin = [side(0, as0.at[:, :, 1 - c], as1.at[:, :, c], red.twin)]
        to_y = [side(1, as1.at[:, 1 - y_at], as2.at[:, y_at], red.near_y)]
        to_z = [side(2 + j, as2.at[(z + 1 + j) % NZ], as3.at[z], peer) for j, peer in enumerate(red.far_z)]
        dm_z = [side(5 + j, dms.at[z, y_at, c], dms.at[z, y_at, c], peer) for j, peer in enumerate(red.far_z)]
        dm_y = [side(8, dms.at[:, y_at, c], dms.at[:, y_at, c], red.near_y)]
        dm_twin = [side(9, dms.at[:, :, c], dms.at[:, :, c], red.twin)]
        down_x = [side(10, down_mine, down_in, red.near_x)]

        def begin(copies):
            for item in copies:
                item.start()

        def end(copies):
            for item in copies:
                item.wait()

        greet(red.peers)
        run = red.run
        spread_rows(all_small, vec_ref, bup_ref)
    else:

        def run(k, stage):
            pass

    vec = lambda i: vec_ref[i : i + 1, :]
    rows_at = lambda b: pl.ds(pl.multiple_of(b * BLK, BLK), BLK)

    for i in range(cap):
        lcol_ref[i : i + 1, :] = jnp.full((1, 128), len_ref[i], jnp.int32)
    lcol = lcol_ref[:, :1]
    t_lane = lax.broadcasted_iota(jnp.int32, (cap, tok), 1)
    c_row = lax.broadcasted_iota(jnp.int32, (cap, tok), 0)
    pool = jnp.where((t_lane // seq == c_row) & (t_lane % seq < lcol), 1.0, 0.0)
    e_ref[...] = pool.astype(BF)
    et_ref[...] = jnp.concatenate([pool, pool, jnp.zeros((128 - 2 * cap, tok), F32)], axis=0).T.astype(BF)
    d_ref[2 * cap :, :] = jnp.zeros_like(d_ref[2 * cap :, :])

    def norm_one(b, _):
        n, _r = norm_rows(x_ref[rows_at(b), :].astype(F32))
        h1_ref[rows_at(b), :] = (n * vec(0) + vec(1)).astype(BF)
        return 0

    lax.fori_loop(0, blocks, norm_one, 0)

    def weight(k, cols):
        return w_ref[k, :, :, :, :, cols].reshape(width, -1)

    for part in range(3):
        loads[part].wait()
        for n in range(tiles):
            cols = slice(n * TILE, n * TILE + TILE)
            value = dot(h1_ref[...], weight(part, cols)) + vec_ref[2 + part : 3 + part, cols]
            qkv_ref[:, part * width + n * TILE : part * width + n * TILE + TILE] = value.astype(BF)

    lane = lax.broadcasted_iota(jnp.int32, (BLK, 128), 1)
    low_half = lane < HEAD
    live_lane = jnp.sum(pool, axis=0, keepdims=True)

    def both_heads(v):
        zero = jnp.zeros_like(v)
        return jnp.concatenate([jnp.where(low_half, v, zero), jnp.where(low_half, zero, v)], axis=0)

    def pick(v):
        return jnp.where(low_half, v[:BLK], v[BLK:])

    same = (lax.broadcasted_iota(jnp.int32, (2 * BLK, BLK), 0) % BLK) // seq == lax.broadcasted_iota(
        jnp.int32, (2 * BLK, BLK), 1
    ) // seq
    for b in range(blocks):
        key_ok = same & (live_lane[:, b * BLK : b * BLK + BLK] > 0.5)
        rows = slice(b * BLK, b * BLK + BLK)
        heads = range(pairs)
        part = lambda n, h: qkv_ref[rows, n * width + h * 128 : n * width + h * 128 + 128]
        ss = [jnp.where(key_ok, dot_nt(both_heads(part(0, h)), part(1, h)), DEAD) for h in heads]
        tops = [jnp.max(s, axis=-1, keepdims=True) for s in ss]
        es = [jnp.exp((s - top) * 0.125) for s, top in zip(ss, tops)]
        sums = [jnp.sum(e, axis=-1, keepdims=True) for e in es]
        ps = [e / total for e, total in zip(es, sums)]
        for h in heads:
            p_ref[b * pairs + h] = ps[h]
        os = [dot(ps[h].astype(BF), part(2, h)) for h in heads]
        for h in heads:
            ctx_ref[rows, h * 128 : h * 128 + 128] = pick(os[h]).astype(BF)

    loads[3].wait()
    for n in range(tiles):
        cols = slice(n * TILE, n * TILE + TILE)
        x1_ref[:, cols] = x_ref[:, cols].astype(F32) + dot(ctx_ref[...], weight(3, cols)) + vec_ref[5:6, cols]

    def norm_two(b, _):
        n, _r = norm_rows(x1_ref[rows_at(b), :])
        h2_ref[rows_at(b), :] = (n * vec(6) + vec(7)).astype(BF)
        return 0

    lax.fori_loop(0, blocks, norm_two, 0)
    for n in range(ff // TILE):
        k, off = divmod(n * TILE, width)
        if off == 0:
            loads[4 + k].wait()
        cols = slice(n * TILE, n * TILE + TILE)
        inner = slice(off, off + TILE)
        pre = dot(h2_ref[...], weight(4 + k, inner)) + bup_ref[:, cols]
        half_slope = 0.5 * (1.0 + lax.erf(pre * ROOT_HALF))
        act = (pre * half_slope).astype(BF)
        slope = (half_slope + pre * jnp.exp(-0.5 * pre * pre) * INV_ROOT_TAU).astype(BF)
        slope_ref[k, :, :, :, :, inner] = slope.reshape(slope_ref.shape[1:-1] + (TILE,))
        act_ref[:, cols] = act

    for k in range(4):
        total = dot(e_ref[...], act_ref[:, k * width : (k + 1) * width])
        if comm:
            for o in range(4):
                own = total[:, o * 4 * piece : (o + 1) * 4 * piece]
                own = jnp.concatenate([own, jnp.zeros((cap, 256 - 4 * piece), F32)], axis=1)
                as0[k, o // 2, o % 2] = own.astype(BF)
        else:
            hi, lo = split(total)
            asum_ref[:cap, k * width : (k + 1) * width] = hi
            asum_ref[cap:, k * width : (k + 1) * width] = lo
    if comm:
        begin(to_twin)
        as1[:, :, c] = as0[:, :, c]
    h2_ref[...] = h2_ref[...].T
    for load in loads[8:]:
        load.wait()
    lens = lcol.astype(F32)
    wgt = wgt_ref[:, :1]
    loss = jnp.zeros((1, TILE), F32)
    for n in range(tiles):
        cols = slice(n * TILE, n * TILE + TILE)
        y = x1_ref[:, cols] + vec_ref[8:9, cols]
        for k in range(NZ):
            y = y + dot(act_ref[:, k * width : k * width + width], wd_ref[k, :, :, :, cols].reshape(width, TILE))
        hi, lo = split(y)
        da_ref[:, cols] = hi
        error = (dot(e_ref[...], hi) + dot(e_ref[...], lo)) / lens - aim_ref[:, cols]
        loss = loss + jnp.sum(wgt * error * error, axis=0, keepdims=True)
        dpool = 2.0 * wgt * error / lens
        dy_hi, dy_lo = split(dpool)
        d_ref[:cap, cols] = dy_hi
        d_ref[cap : 2 * cap, cols] = dy_lo
        gvec_ref[8:9, cols] = jnp.sum(dy_hi.astype(F32) * lens, axis=0, keepdims=True)
        if comm:
            dms[z, y_at, c, :, cols] = dy_hi
            if n == 1:
                end(to_twin)
                begin(to_y)
                as2[:, y_at] = as1[:, y_at]
            elif n == tiles - 1:
                begin(dm_z)
    y_out = pltpu.make_async_copy(da_ref, y_hbm, sems.at[12])
    y_out.start()
    gvec_ref[3:4, :] = jnp.zeros((1, width), F32)
    gvec_ref[9:10, :] = jnp.broadcast_to(jnp.sum(loss, axis=1, keepdims=True), (1, width))
    gvec_ref[10:12, :] = jnp.zeros((2, width), F32)

    dm = d_ref[:cap, :]
    span = ff // 8
    pad = jnp.zeros((128 - 2 * cap, span), BF)
    for n in range(8):
        hi, lo = split(dot_nt(dm, wd_ref[n // 2, n % 2].reshape(span, width)))
        dmw_ref[:cap, n * span : (n + 1) * span] = hi
        dmw_ref[cap : 2 * cap, n * span : (n + 1) * span] = lo
        dmw_ref[2 * cap :, n * span : (n + 1) * span] = pad
    for k in range(4):
        for n in range(tiles):
            at = k * width + n * TILE
            cols = slice(n * TILE, n * TILE + TILE)
            slope = slope_ref[k, :, :, :, :, cols].reshape(tok, TILE)
            dpre = (dot(et_ref[...], dmw_ref[:, at : at + TILE]) * slope.astype(F32)).astype(BF)
            gvec_ref[12 + k : 13 + k, cols] = jnp.sum(dpre.astype(F32), axis=0, keepdims=True)
            act_ref[:, at : at + TILE] = dpre
            wd_ref[:, :, :, k * piece : (k + 1) * piece, cols] = (
                dot(h2_ref[...], dpre).astype(BF).reshape(NZ, NY, NC, piece, TILE)
            )
        if comm:
            pl.semaphore_signal(free, inc=1, device_id=red.twin, device_id_type=MESH)
            if k == 0:
                end(to_y)
                begin(to_z)
                as3[z] = as2[z]
            if k == 1:
                end(dm_z)
                begin(dm_y)
            if k % 2 == 0:
                pl.semaphore_wait(free, 1)
        run(4 + k, 0)
        if k > 0:
            run(3 + k, 1)
    for n in range(tiles):
        total = jnp.zeros((tok, TILE), F32)
        for k in range(4):
            w_rows = w_ref[4 + k].reshape(width, width)[n * TILE : n * TILE + TILE]
            total = total + dot_nt(act_ref[:, k * width : k * width + width], w_rows)
        dy_ref[:, n * TILE : n * TILE + TILE] = total
        if n == 0:
            run(7, 1)
        elif n == 2:
            run(4, 2)
    if not comm:
        dm2 = jnp.concatenate([dm, dm], axis=0)
        per = ff // OWNERS
        for o in range(OWNERS):
            lo, hi = o * per // 128 * 128, (o * per + per + 127) // 128 * 128
            g = dot_tn(asum_ref[:, lo:hi], dm2)[o * per - lo : o * per - lo + per].astype(BF)
            for k in range(4):
                slope_ref[k, o % 2, o // 4, o // 2 % 2] = g[k * piece : (k + 1) * piece]
    y_out.wait()

    def two_back(b, sums):
        g_gain, g_bias, g_out = sums
        dh = dy_ref[rows_at(b), :]
        n2, r2 = norm_rows(x1_ref[rows_at(b), :])
        dx1 = dot(et_ref[rows_at(b), :], d_ref[...]) + norm_back(dh * vec(6), n2, r2)
        dy_ref[rows_at(b), :] = dx1
        da = dx1.astype(BF)
        da_ref[rows_at(b), :] = da
        return (
            g_gain + jnp.sum(dh * n2, axis=0, keepdims=True),
            g_bias + jnp.sum(dh, axis=0, keepdims=True),
            g_out + jnp.sum(da.astype(F32), axis=0, keepdims=True),
        )

    zero_row = jnp.zeros((1, width), F32)
    sums = lax.fori_loop(0, blocks, two_back, (zero_row,) * 3)
    gvec_ref[6:7, :] = sums[0]
    gvec_ref[7:8, :] = sums[1]
    gvec_ref[5:6, :] = sums[2]
    run(5, 2)
    if comm:
        end(dm_y)
        begin(dm_twin)
    for n in range(tiles):
        w_rows = w_ref[3].reshape(width, width)[n * TILE : n * TILE + TILE]
        h2_ref[:, n * TILE : n * TILE + TILE] = dot_nt(da_ref[...], w_rows).astype(BF)
    ctx_ref[...] = ctx_ref[...].T
    for n in range(tiles):
        cols = slice(n * TILE, n * TILE + TILE)
        w_ref[3, :, :, :, :, cols] = dot(ctx_ref[...], da_ref[:, cols]).astype(BF).reshape(w_ref.shape[1:-1] + (TILE,))
    if comm:
        pl.semaphore_wait(free, 1)
    run(3, 0)
    for b in range(blocks):
        rows = slice(b * BLK, b * BLK + BLK)
        heads = range(pairs)
        at = lambda n, h: slice(n * width + h * 128, n * width + h * 128 + 128)
        ps = [p_ref[b * pairs + h] for h in heads]
        dcs = [both_heads(h2_ref[rows, at(0, h)]) for h in heads]
        dps = [dot_nt(dcs[h], qkv_ref[rows, at(2, h)]) for h in heads]
        sums = [jnp.sum(ps[h] * dps[h], axis=-1, keepdims=True) for h in heads]
        dss = [(ps[h] * (dps[h] - sums[h])).astype(BF) for h in heads]
        dqs = [pick(dot(dss[h], qkv_ref[rows, at(1, h)])) * 0.125 for h in heads]
        dks = [dot_tn(dss[h], both_heads(qkv_ref[rows, at(0, h)])) * 0.125 for h in heads]
        dvs = [dot_tn(ps[h].astype(BF), dcs[h]) for h in heads]
        for h in heads:
            qkv_ref[rows, at(0, h)] = dqs[h].astype(BF)
            qkv_ref[rows, at(1, h)] = dks[h].astype(BF)
            qkv_ref[rows, at(2, h)] = dvs[h].astype(BF)
        for k, stage in BACK_STEPS[b]:
            run(k, stage)
        if comm and b == 2:
            end(dm_twin)
            end(to_z)
            g = dot_tn(as3[...].reshape(OWNERS * cap, 256), dms[...].reshape(OWNERS * cap, width))
            down_mine[...] = g[: 4 * piece].astype(BF)
            begin(down_x)
    h1_ref[...] = h1_ref[...].T
    for k in range(3):
        for n in range(tiles):
            cols = slice(n * TILE, n * TILE + TILE)
            d = qkv_ref[:, k * width + n * TILE : k * width + n * TILE + TILE]
            gvec_ref[2 + k : 3 + k, cols] = jnp.sum(d.astype(F32), axis=0, keepdims=True)
            w_ref[4 + k, :, :, :, :, cols] = dot(h1_ref[...], d).astype(BF).reshape(w_ref.shape[1:-1] + (TILE,))
        if comm and k == 1:
            pl.semaphore_wait(free, 1)
        run(k, 0)
        if k > 0:
            run(k - 1, 1)
    for n in range(tiles):
        total = jnp.zeros((tok, TILE), F32)
        for k in range(3):
            w_rows = w_ref[k].reshape(width, width)[n * TILE : n * TILE + TILE]
            total = total + dot_nt(qkv_ref[:, k * width : k * width + width], w_rows)
        x1_ref[:, n * TILE : n * TILE + TILE] = total
        for k, stage in (((2, 1),), ((3, 3), (4, 4)), ((5, 4), (6, 4)))[n]:
            run(k, stage)

    def one_back(b, sums):
        g_gain, g_bias = sums
        dh = x1_ref[rows_at(b), :]
        n1, r1 = norm_rows(x_ref[rows_at(b), :].astype(F32))
        dy_ref[rows_at(b), :] = dy_ref[rows_at(b), :] + norm_back(dh * vec(0), n1, r1)
        return (g_gain + jnp.sum(dh * n1, axis=0, keepdims=True), g_bias + jnp.sum(dh, axis=0, keepdims=True))

    sums = lax.fori_loop(0, blocks, one_back, (zero_row,) * 2)
    gvec_ref[0:1, :] = sums[0]
    gvec_ref[1:2, :] = sums[1]
    dx_out = pltpu.make_async_copy(dy_ref, dx_hbm, sems.at[13])
    dx_out.start()
    if comm:

        def small(slot, src, dst, peer):
            return remote(src, dst, v_send.at[slot], v_recv.at[slot], peer)

        steps = [
            small(0, vecs.at[0], vec_in.at[0], red.twin),
            small(1, vecs.at[1], vec_in.at[1], red.near_y),
            small(2, vecs.at[2], vec_in.at[2], red.near_x),
        ]
        spread = [small(3 + j, vec_z.at[red.z], vec_z.at[red.z], peer) for j, peer in enumerate(red.far_z)]
        vecs[0] = gvec_ref[...]
        steps[0].start()
        run(0, 2)
        run(1, 2)
        steps[0].wait()
        vecs[1] = vecs[0] + vec_in[0]
        steps[1].start()
        for k, stage in ((3, 4), (7, 4), (4, 5), (6, 5), (2, 2)):
            run(k, stage)
        steps[1].wait()
        vecs[2] = vecs[1] + vec_in[1]
        steps[2].start()
        run(0, 3)
        run(1, 3)
        end(down_x)
        gdown[...] = down_mine[...].astype(F32) + down_in[...].astype(F32)
        steps[2].wait()
        vec_z[red.z] = vecs[2] + vec_in[2]
        for item in spread:
            item.start()
        run(2, 3)
        run(3, 5)
        run(1, 4)
        run(0, 4)
        for item in spread:
            item.wait()
        own_rows(vec_z[0] + vec_z[1] + vec_z[2] + vec_z[3], own_out)
        run(2, 4)
        run(0, 5)
    else:
        copies = [pltpu.make_async_copy(w_ref.at[3 if k == 3 else 4 + k], grad_hbm.at[k], sems.at[k]) for k in range(4)]
        for k in range(4):
            rows = slice(k * piece, (k + 1) * piece)
            copies.append(pltpu.make_async_copy(wd_ref.at[:, :, :, rows], grad_hbm.at[4 + k], sems.at[4 + k]))
            for c in range(NC):
                copies.append(
                    pltpu.make_async_copy(slope_ref.at[k, c], grad_hbm.at[8 + k, :, :, c], sems.at[14 + 2 * k + c])
                )
        for copy in copies:
            copy.start()
        for copy in copies:
            copy.wait()
    dx_out.wait()


def text_call(comm, x, smalls, aim, wgt, lens, packed):
    tok, width = x.shape
    cap = aim.shape[0]
    ff = 4 * width
    piece = packed.shape[-2]
    anys = pl.BlockSpec(memory_space=pl.ANY)
    vmem = pl.BlockSpec(memory_space=pltpu.VMEM)
    smem = pl.BlockSpec(memory_space=pltpu.SMEM)
    sds = jax.ShapeDtypeStruct
    out_shape = [sds((tok, width), BF), sds((tok, width), F32), sds((16, 256 if comm else width), F32)]
    out_specs = [anys, anys, vmem]
    eight = (8, NZ, NY, NC, piece, width)
    scratch = [
        pltpu.VMEM(eight, BF),
        pltpu.VMEM((NZ, NY, NC, 4 * piece, width), BF),
        pltpu.VMEM((tok, width), BF),
        pltpu.VMEM((tok, 3 * width), BF),
        pltpu.VMEM((tok // BLK * (width // 128), 2 * BLK, BLK), F32),
        pltpu.VMEM((tok, width), BF),
        pltpu.VMEM((tok, width), F32),
        pltpu.VMEM((tok, width), BF),
        pltpu.VMEM((tok, ff), BF),
        pltpu.VMEM((ff // width, 2, NZ, NY, tok // 16, width), BF),
        pltpu.VMEM((2 * cap, ff), BF),
        pltpu.VMEM((cap, 128), jnp.int32),
        pltpu.VMEM((cap, tok), BF),
        pltpu.VMEM((tok, 128), BF),
        pltpu.VMEM((tok, width), F32),
        pltpu.VMEM((128, width), BF),
        pltpu.VMEM((tok, width), BF),
        pltpu.VMEM((128, ff), BF),
        pltpu.SemaphoreType.DMA((22,)),
    ]
    params = dict(vmem_limit_bytes=VMEM_LIMIT)
    if comm:
        out_shape += [
            sds((piece, 3 * width), F32), sds((piece, width), F32), sds((piece, ff), F32), sds((4 * piece, width), F32),
        ]
        out_specs += [vmem] * 4
        scratch += [
            pltpu.VMEM((16, width), F32),
            pltpu.VMEM((1, ff), F32),
            pltpu.VMEM((16, width), F32),
            pltpu.VMEM((4, NZ, NY, piece, width // 2), BF),
            pltpu.VMEM((4, NZ, piece, width // 2), BF),
            pltpu.VMEM((4, NZ - 1, piece, width // 2), BF),
            pltpu.VMEM((4, piece, width // 2), BF),
            pltpu.VMEM((4, piece, width // 2), BF),
            pltpu.VMEM((4, NZ, piece, width), BF),
            pltpu.VMEM((4, NZ - 1, piece, width), BF),
            pltpu.VMEM((4, piece, width), BF),
            pltpu.VMEM((4, piece, width), BF),
            pltpu.VMEM((3, 16, width), F32),
            pltpu.VMEM((3, 16, width), F32),
            pltpu.VMEM((NZ, 16, width), F32),
            *[pltpu.VMEM((NZ, NY, NC, cap, 256), BF)] * 4,
            pltpu.VMEM((NZ, NY, NC, cap, width), BF),
            pltpu.VMEM((4 * piece, width), BF),
            pltpu.VMEM((4 * piece, width), BF),
            pltpu.SemaphoreType.DMA((8, 7)),
            pltpu.SemaphoreType.DMA((8, 7)),
            pltpu.SemaphoreType.DMA((6,)),
            pltpu.SemaphoreType.DMA((6,)),
            pltpu.SemaphoreType.DMA((11,)),
            pltpu.SemaphoreType.DMA((11,)),
            pltpu.SemaphoreType.REGULAR,
        ]
        params.update(collective_id=1, has_side_effects=True)
    else:
        out_shape += [sds(packed.shape, BF)]
        out_specs += [anys]
    return pl.pallas_call(
        functools.partial(text_body, comm),
        out_shape=out_shape,
        in_specs=[vmem] * (3 + len(smalls)) + [smem, anys],
        out_specs=out_specs,
        scratch_shapes=scratch,
        compiler_params=pltpu.CompilerParams(**params),
    )(x, *smalls, aim, wgt, lens, packed)


def pack(wqkv, wout, wup, wdown):
    width = wout.shape[1]
    parts = [wqkv[:, k * width : (k + 1) * width] for k in range(3)] + [wout]
    parts += [wup[:, k * width : (k + 1) * width] for k in range(4)]
    down = wdown.reshape(OWNERS, 4, width // OWNERS, width)
    parts += [down[:, k].reshape(width, width) for k in range(4)]
    return jnp.stack(parts).reshape(12, NZ, NY, NC, width // OWNERS, width)


def unpack(packed):
    width = packed.shape[-1]
    flat = packed.reshape(12, width, width)
    wqkv = jnp.concatenate([flat[k] for k in range(3)], axis=1)
    wup = jnp.concatenate([flat[4 + k] for k in range(4)], axis=1)
    down = flat[8:].reshape(4, OWNERS, width // OWNERS, width)
    return wqkv, flat[3], wup, jnp.swapaxes(down, 0, 1).reshape(4 * width, width)


def vectors(g1, b1, bqv, bout, g2, b2, bup, bdown):
    width = g1.shape[0]
    zero = jnp.zeros((width,), BF)
    rows = [g1, b1, bqv[:width], zero, bqv[width:], bout, g2, b2, bdown] + [zero] * 7
    return jnp.stack(rows).astype(F32), bup.astype(F32).reshape(1, -1)


def hand_out_body(part, *refs):
    big, own, outs, bufs, sem_in, sem_out = refs[:6], refs[6], refs[7:22], refs[22:28], refs[28], refs[29]
    loss, y, dx, g1, b1, gqkv, qv, gout, bout, g2, b2, gup, bup, gdown, bdown = outs
    pairs = list(zip(big, bufs, (y, dx, gqkv, gout, gup, gdown)))
    ins, backs = [], []
    for i, (src, buf, dst) in enumerate(pairs):
        pieces = 4 if i < 2 else 1
        n = src.shape[0] // pieces
        for p in range(pieces):
            rows = pl.ds(p * n, n)
            slot = 4 * i + p
            ins.append(pltpu.make_async_copy(src.at[rows], buf.at[rows], sem_in.at[slot]))
            backs.append(pltpu.make_async_copy(buf.at[rows], dst.at[rows], sem_out.at[slot]))
    for copy in ins:
        copy.start()
    for ref, at, lanes in (
        (g1, 0, part), (b1, 1, part), (qv, 2, 2 * part), (bout, 3, part), (g2, 4, part), (b2, 5, part), (bdown, 6, part),
        (bup, 8, 4 * part),
    ):
        ref[...] = own[at : at + 1, :lanes].reshape(lanes)
    loss[...] = own[7:8, :1]
    for copy, back in zip(ins, backs):
        copy.wait()
        back.start()
    for back in backs:
        back.wait()


def hand_out(big, own, part):
    sds = jax.ShapeDtypeStruct
    anys = pl.BlockSpec(memory_space=pl.ANY)
    vmem = pl.BlockSpec(memory_space=pltpu.VMEM)
    like = lambda v: sds(v.shape, v.dtype)
    line = lambda n: sds((n * part,), F32)
    y, dx, gqkv, gout, gup, gdown = big
    return pl.pallas_call(
        functools.partial(hand_out_body, part),
        out_shape=[
            sds((1, 1), F32), like(y), like(dx), line(1), line(1), like(gqkv), line(2), like(gout), line(1), line(1),
            line(1), like(gup), line(4), like(gdown), line(1),
        ],
        in_specs=[anys] * 6 + [vmem],
        out_specs=[vmem, anys, anys, vmem, vmem, anys, vmem, anys, vmem, vmem, vmem, anys, vmem, anys, vmem],
        scratch_shapes=[pltpu.VMEM(v.shape, v.dtype) for v in big]
        + [pltpu.SemaphoreType.DMA((24,)), pltpu.SemaphoreType.DMA((24,))],
        compiler_params=pltpu.CompilerParams(vmem_limit_bytes=VMEM_LIMIT),
    )(*big, own)


def group_weight(group_ids, live):
    match = group_ids[:, None] == jnp.arange(1024, dtype=jnp.int32)[None, :]
    local = jnp.sum(jnp.where(match & live[:, None], 1.0, 0.0).astype(F32), axis=0)
    size = lax.psum(local, ("dp", "fsdp"))
    members = jnp.sum(jnp.where(match, size[None, :], 0.0), axis=1)
    return jnp.where(live, 1.0 / jnp.maximum(members, 1.0), 0.0)


def any_mesh(text, weights, image_weights, patches, targets, group_ids, cap_len, slot_counts):
    cap = targets.shape[0]
    gathered = [lax.all_gather(w, "fsdp", axis=0, tiled=True) for w in weights]
    g1, b1, wqkv, bqv, wout, bout, g2, b2, wup, bup, wdown, bdown = gathered
    live = jnp.arange(cap, dtype=jnp.int32) < slot_counts[0]
    wgt = group_weight(group_ids, live)
    (aim,) = image_call(patches, targets, image_weights)
    vec, bup_row = vectors(g1, b1, bqv, bout, g2, b2, bup, bdown)
    y, dx, gvec, packed = text_call(
        False, text, (vec, bup_row), aim, jnp.broadcast_to(wgt[:, None], (cap, 128)), cap_len, pack(wqkv, wout, wup, wdown)
    )
    gqkv, gout, gup, gdown = unpack(packed)
    grads = [
        gvec[0], gvec[1], gqkv, jnp.concatenate([gvec[2], gvec[4]]), gout, gvec[5], gvec[6], gvec[7], gup,
        gvec[12:16].reshape(-1), gdown, gvec[8],
    ]
    owned = [lax.psum_scatter(g.astype(F32), "fsdp", scatter_dimension=0, tiled=True) for g in grads]
    return (lax.psum(gvec[9, 0], ("dp", "fsdp")), y, dx, *[lax.psum(g, "dp") for g in owned])


def block_mesh(text, weights, image_weights, patches, targets, group_ids, cap_len, slot_counts):
    g1, b1, wqkv, bqv, wout, bout, g2, b2, wup, bup, wdown, bdown = weights
    width = wout.shape[1]
    aim, packed, all_small, wgt = image_call(
        patches, targets, image_weights, (wqkv, wout, wup, wdown, g1, b1, bqv, bout, g2, b2, bup, bdown, group_ids, slot_counts)
    )
    y, dx, gvec, gqkv, gout, gup, gdown = text_call(True, text, (all_small,), aim, wgt, cap_len, packed)
    part = width // OWNERS
    loss, y, dx, g1, b1, gqkv, qv, gout, bout, g2, b2, gup, bup, gdown, bdown = hand_out(
        (y, dx, gqkv, gout, gup, gdown), gvec, part
    )
    return loss[0, 0], y, dx, g1, b1, gqkv, qv, gout, bout, g2, b2, gup, bup, gdown, bdown


def solution(mesh):
    shape = dict(mesh.shape)
    inner = block_mesh if (shape["dp"], shape["fsdp"]) == (2, OWNERS) else any_mesh

    def per_device(text_in, *rest):
        weights, image_weights = rest[:12], rest[12:24]
        patches, targets, group_ids, cap_len, slot_counts = rest[24:]
        return inner(
            text_in, weights, image_weights, jnp.transpose(patches, (1, 0, 2)), targets, group_ids, cap_len, slot_counts
        )

    both = ("dp", "fsdp")
    owned, table = P("fsdp"), P("fsdp", None)
    text_specs = (owned, owned, table, owned, table, owned, owned, owned, table, owned, table, owned)
    return jax.shard_map(
        per_device,
        mesh=mesh,
        in_specs=(P(both, None), *text_specs, *([P()] * 12), P(both, None, None), P(both, None), P(both), P(both), P(both)),
        out_specs=(P(), P(both, None), P(both, None), *text_specs),
        check_vma=False,
    )
```

```python
import functools

import jax
import jax.numpy as jnp
from jax import lax
from jax.experimental import pallas as pl
from jax.experimental.pallas import tpu as pltpu
from jax.sharding import PartitionSpec as P

HEAD = 64
EPS = 1e-06
ROOT_HALF = 0.7071067811865476
INV_ROOT_TAU = 0.3989422804014327
DEAD = -8e9
BF = jnp.bfloat16
F32 = jnp.float32
BLK = 128
TILE = 256
NZ, NY, NC = 4, 2, 2
OWNERS = NZ * NY * NC
MESH = pl.DeviceIdType.MESH
VMEM_LIMIT = 63 * 2**20
LAGS = (-2, 1, 3, 6)
SPLIT = (0, 3, 4, 6)
WHOLE = (1, 2, 5, 7)
LANDING = {4: 0, 5: 1, 6: 2, 7: 3, 3: 4, 0: 5, 1: 6, 2: 7}
BACK_STEPS = (
    ((3, 1),),
    ((6, 2), (7, 2)),
    ((4, 3),),
    ((5, 3),),
    ((3, 2),),
    ((6, 3), (7, 3)),
)
SMALL = ((0, 0), (0, 4), (1, 2), (2, 0), (2, 4))


def norm_rows(values):
    centered = values - jnp.mean(values, axis=-1, keepdims=True)
    inv_std = lax.rsqrt(jnp.mean(centered * centered, axis=-1, keepdims=True) + EPS)
    return centered * inv_std, inv_std


def norm_back(u, n, r):
    return r * (u - jnp.mean(u, axis=-1, keepdims=True) - n * jnp.mean(u * n, axis=-1, keepdims=True))


def gelu_exact(v):
    return 0.5 * v * (1.0 + lax.erf(v * ROOT_HALF))


def dot(a, b):
    return jnp.dot(a, b, preferred_element_type=F32)


def dot_nt(a, b):
    return lax.dot_general(a, b, (((1,), (1,)), ((), ())), preferred_element_type=F32)


def dot_tn(a, b):
    return lax.dot_general(a, b, (((0,), (0,)), ((), ())), preferred_element_type=F32)


def split(v):
    high = v.astype(BF)
    return high, (v - high.astype(F32)).astype(BF)


def row(ref, start=0, size=None):
    size = ref.shape[0] if size is None else size
    return ref[pl.ds(start, size)].astype(F32).reshape(1, size)


def place():
    f = lax.axis_index("fsdp")
    return lax.axis_index("dp"), f // (NY * NC), (f // NC) % NY, f % NC


def device(x, z, y, c):
    return (x, (z * NY + y) * NC + c)


def greet(peers):
    barrier = pltpu.get_barrier_semaphore()
    for peer in peers:
        pl.semaphore_signal(barrier, inc=1, device_id=peer, device_id_type=MESH)
    pl.semaphore_wait(barrier, len(peers))


def remote(src, dst, send, recv, peer):
    return pltpu.make_async_remote_copy(
        src_ref=src, dst_ref=dst, send_sem=send, recv_sem=recv, device_id=peer, device_id_type=MESH
    )


class Gather:
    def __init__(self, g_ref, send, recv):
        self.g, self.send, self.recv = g_ref, send, recv
        self.chunks = g_ref.shape[0]
        half = g_ref.shape[-1] // 2
        self.x, self.z, self.y, self.c = place()
        self.mine = pl.ds(pl.multiple_of(self.x * half, 128), half)
        self.far_z = [device(self.x, (self.z + j) % NZ, self.y, self.c) for j in range(1, NZ)]
        self.near_y = device(self.x, self.z, 1 - self.y, self.c)
        self.near_x = device(1 - self.x, self.z, self.y, self.c)
        self.twin = device(self.x, self.z, self.y, 1 - self.c)
        self.peers = self.far_z + [self.near_y, self.near_x, self.twin]

    def copy(self, k, slot, ref, peer):
        return remote(ref, ref, self.send.at[k, slot], self.recv.at[k, slot], peer)

    def along_z(self, k):
        ref = self.g.at[k, self.z, self.y, self.c, :, self.mine]
        return [self.copy(k, j, ref, peer) for j, peer in enumerate(self.far_z)]

    def first(self, k):
        top, rest = pl.ds(0, 32), pl.ds(32, 16)
        return [self.copy(k, 3, self.g.at[k, :, self.y, self.c, top, self.mine], self.near_y)] + [
            self.copy(k, 4 + j, self.g.at[k, (self.z + 1 + j) % NZ, self.y, self.c, rest, self.mine], self.near_x)
            for j in range(3)
        ]

    def second(self, k):
        top, rest = pl.ds(0, 32), pl.ds(32, 16)
        return (
            [
                self.copy(k, 7 + j, self.g.at[k, (self.z + 1 + j) % NZ, :, self.c, top, self.mine], self.near_x)
                for j in range(3)
            ]
            + [self.copy(k, 10, self.g.at[k, self.z, 1 - self.y, self.c, top, self.mine], self.near_x)]
            + [self.copy(k, 11, self.g.at[k, :, self.y, self.c, rest], self.near_y)]
        )

    def last(self, k):
        return [self.copy(k, 12, self.g.at[k, :, :, self.c], self.twin)]

    def tick(self, t):
        def start(copies):
            for copy in copies:
                copy.start()

        def arrive(copies):
            for copy in copies:
                copy.wait_recv()

        def stage(lag, action):
            @pl.when(jnp.logical_and(t - lag >= 0, t - lag < self.chunks))
            def _():
                action(t - lag)

        def one(k):
            start(self.along_z(k))

        def two(k):
            arrive(self.along_z(k))
            start(self.first(k))

        def three(k):
            arrive(self.first(k))
            start(self.second(k))

        def four(k):
            arrive(self.second(k))
            start(self.last(k))

        stage(LAGS[0], one)
        stage(LAGS[1], two)
        stage(LAGS[2], three)
        stage(LAGS[3], four)

    def finish(self):
        def end(k, _):
            for copy in self.last(k):
                copy.wait()
            for copy in self.along_z(k) + self.first(k) + self.second(k):
                copy.wait_send()
            return 0

        lax.fori_loop(0, self.chunks, end, 0)


def image_body(comm, group, *refs):
    (x_hbm, t_ref, g1, b1, bqv, bout, g2, b2, bup, bdown, wqkv_hbm, wout_hbm, wup_hbm, wdown_hbm), refs = refs[:14], refs[14:]
    if comm:
        (oqkv, oout, oup, odown, *smalls, gid, count), refs = refs[:14], refs[14:]
        (aim_ref, gath, vec_ref, wgt_ref), refs = refs[:4], refs[4:]
    else:
        (aim_ref,), refs = refs[:1], refs[1:]
    (x_ref, wqkv, wout, wup, wdown, h_ref, qkv_ref, ctx_ref, act_ref, xm_ref, sems), refs = refs[:11], refs[11:]
    patches, cap, width = x_hbm.shape
    ff = wup.shape[1]
    steps = cap // group
    rows = patches * group
    loads = [
        pltpu.make_async_copy(src, dst, sems.at[i])
        for i, (src, dst) in enumerate(
            [(x_hbm, x_ref), (wqkv_hbm, wqkv), (wout_hbm, wout), (wup_hbm, wup), (wdown_hbm, wdown)]
        )
    ]
    if comm:
        ids, vecs, own_ref, own_sem, g_send, g_recv, s_send, s_recv = refs
        gather = Gather(gath, g_send, g_recv)
        x, z, y, c = gather.x, gather.z, gather.y, gather.c
        own = []
        for k in range(gath.shape[0]):
            if k < 3:
                src = oqkv.at[:, k * width : k * width + width]
            elif k < 4:
                src = oout
            elif k < 8:
                src = oup.at[:, (k - 4) * width : (k - 3) * width]
            else:
                src = odown.at[(k - 8) * oout.shape[0] : (k - 7) * oout.shape[0]]
            own.append((pltpu.make_async_copy(src, own_ref.at[k], own_sem.at[k]), pltpu.make_async_copy(own_ref.at[k], gath.at[k, z, y, c], own_sem.at[k])))
        for copy, _out in own:
            copy.start()
        for load in loads:
            load.start()
        lines = []
        for ref in smalls:
            n = ref.shape[0]
            for at in range(0, n, 128):
                take = min(128, n - at)
                line = row(ref)[:, at : at + take]
                lines.append(jnp.concatenate([line, jnp.zeros((1, 128 - take), F32)], axis=1) if take < 128 else line)
        lines.append(jnp.zeros((16 - len(lines), 128), F32))
        vecs[z, y, c] = jnp.concatenate(lines, axis=0).astype(BF)
        lane = lax.broadcasted_iota(jnp.int32, (8, 128), 1)
        line = jnp.full((8, 128), -1, jnp.int32)
        for i in range(cap):
            line = jnp.where(lane == i, jnp.where(i < count[0], gid[i], -1), line)
        ids[x, z, y, c] = line
        greet(gather.peers)

        def small(slot, ref, peer):
            return remote(ref, ref, s_send.at[slot], s_recv.at[slot], peer)

        small_z = [small(j, ids.at[x, z, y, c], peer) for j, peer in enumerate(gather.far_z)]
        small_z += [small(3 + j, vecs.at[z, y, c], peer) for j, peer in enumerate(gather.far_z)]
        small_y = [small(6, ids.at[x, :, y, c], gather.near_y), small(7, vecs.at[:, y, c], gather.near_y)]
        small_x = [small(8, ids.at[x, :, :, c], gather.near_x), small(9, vecs.at[:, :, c], gather.twin)]
        small_c = [small(10, ids.at[:, :, :, c], gather.twin)]
        stages = [small_z, small_y, small_x, small_c]
        for copy, out in own:
            copy.wait()
            out.start()
        for _copy, out in own:
            out.wait()
        for k in range(-LAGS[0]):
            for copy in gather.along_z(k):
                copy.start()

        def tick(step, t):
            gather.tick(step * 6 + t)
            for i, (at_step, at) in enumerate(SMALL):
                if at == t:

                    @pl.when(step == at_step)
                    def _():
                        if i > 0:
                            for copy in stages[i - 1]:
                                copy.wait_recv()
                        if i < 4:
                            for copy in stages[i]:
                                copy.start()

    else:
        for load in loads:
            load.start()

        def tick(step, t):
            pass

    lane_q = lax.broadcasted_iota(jnp.int32, (112, 128), 1)
    low_half = lane_q < HEAD
    key = lax.broadcasted_iota(jnp.int32, (224, 128), 1)
    second = lax.broadcasted_iota(jnp.int32, (224, 128), 0) % 112 >= 56
    first_key = jnp.where(second, 64, 0)
    key_ok = (key >= first_key) & (key < first_key + patches)
    ones = jnp.ones((128, 128), BF)
    g1v, b1v, g2v, b2v = row(g1), row(b1), row(g2), row(b2)
    bias = [row(bqv, 0, width), jnp.zeros((1, width), F32), row(bqv, width, width)]
    boutv, bupv, bdownv = row(bout), row(bup), row(bdown)
    xm_ref[...] = jnp.zeros_like(xm_ref)
    for load in loads[:4]:
        load.wait()

    def chunk_step(step, _):
        c0 = pl.multiple_of(step * group, group)
        caps = pl.ds(c0, group)
        tick(step, 0)

        def norm_one(p, _):
            value = x_ref[pl.ds(p * 5, 5), caps, :].astype(F32).reshape(5 * group, width)
            n, _inv = norm_rows(value)
            h_ref[pl.ds(pl.multiple_of(p * 5 * group, 16), 5 * group), :] = (n * g1v + b1v).astype(BF)
            return 0

        lax.fori_loop(0, patches // 5, norm_one, 0)
        for n in range(3 * width // TILE):
            cols = slice(n * TILE, n * TILE + TILE)
            part, off = divmod(n * TILE, width)
            value = dot(h_ref[...], wqkv[:, cols]) + bias[part][:, off : off + TILE]
            qkv_ref[2 * n] = value[:, :128]
            qkv_ref[2 * n + 1] = value[:, 128:]
        tick(step, 1)

        def attend(p, _):
            def load(col, tall):
                parts = []
                for k in range(2):
                    v = qkv_ref[col // 128, pl.ds(2 * p + k, patches, stride=group), :]
                    parts.append(jnp.concatenate([v, jnp.zeros((tall - patches, 128), F32)], axis=0))
                return jnp.concatenate(parts, axis=0).astype(BF)

            def scores(h):
                q = load(h * 128, 56)
                zero = jnp.zeros_like(q)
                q2 = jnp.concatenate([jnp.where(low_half, q, zero), jnp.where(low_half, zero, q)], axis=0)
                return jnp.where(key_ok, dot_nt(q2, load(width + h * 128, 64)), DEAD)

            for first in range(0, width // 128, 6):
                heads = range(first, first + 6)
                ss = [scores(h) for h in heads]
                tops = [jnp.max(s, axis=-1, keepdims=True) for s in ss]
                es = [jnp.exp((s - top) * 0.125).astype(BF) for s, top in zip(ss, tops)]
                os = [dot(e, jnp.concatenate([load(2 * width + h * 128, 64), ones], axis=1)) for e, h in zip(es, heads)]
                for o, h in zip(os, heads):
                    num = jnp.where(low_half, o[:112, :128], o[112:, :128])
                    den = jnp.where(low_half, o[:112, 128:], o[112:, 128:])
                    out = num / den
                    for k in range(2):
                        ctx_ref[h, pl.ds(2 * p + k, patches, stride=group), :] = out[56 * k : 56 * k + patches]
            return 0

        lax.fori_loop(0, group // 4, attend, 0)
        tick(step, 2)
        lax.fori_loop(group // 4, group // 2, attend, 0)
        tick(step, 3)

        def project(p, _):
            span = pl.ds(pl.multiple_of(p * 10 * group, 16), 10 * group)
            ctx = jnp.concatenate([ctx_ref[h, span, :] for h in range(width // 128)], axis=1).astype(BF)
            x1 = x_ref[pl.ds(p * 10, 10), caps, :].astype(F32).reshape(10 * group, width) + dot(ctx, wout[...]) + boutv
            xm_ref[caps, :] += jnp.sum(x1.reshape(10, group, width), axis=0)
            n, _inv = norm_rows(x1)
            h_ref[span, :] = (n * g2v + b2v).astype(BF)
            return 0

        lax.fori_loop(0, patches // 10, project, 0)
        tick(step, 4)
        for n in range(ff // TILE):
            cols = slice(n * TILE, n * TILE + TILE)
            act = gelu_exact(dot(h_ref[...], wup[:, cols]) + bupv[:, cols])
            act_ref[caps, cols] = jnp.sum(act.reshape(patches, group, TILE), axis=0)
            if n == ff // TILE // 2:
                tick(step, 5)
        return 0

    lax.fori_loop(0, steps, chunk_step, 0)
    loads[4].wait()
    both = jnp.concatenate(split(act_ref[...] * (1.0 / patches)), axis=0)
    for n in range(width // TILE):
        cols = slice(n * TILE, n * TILE + TILE)
        o = dot(both, wdown[:, cols])
        aim_ref[:, cols] = (
            o[:cap] + o[cap:] + xm_ref[:, cols] * (1.0 / patches) + bdownv[:, cols] + t_ref[:, cols].astype(F32)
        )
    if comm:
        column = lax.broadcasted_iota(jnp.int32, (cap, 128), 0)
        mine = jnp.zeros((cap, 128), jnp.int32)
        for i in range(cap):
            mine = jnp.where(column == i, gid[i], mine)
        total = jnp.zeros((cap, 128), F32)
        for dx in range(2):
            for o in range(OWNERS):
                line = ids[dx, o // 4, o // 2 % 2, o % 2][0:1]
                total = total + jnp.where(mine == line, 1.0, 0.0)
        members = jnp.sum(total, axis=1, keepdims=True)
        wgt = jnp.where(column < count[0], 1.0 / jnp.maximum(members, 1.0), 0.0)
        wgt_ref[...] = wgt
        vec_ref[...] = vecs[...]
        gather.finish()
        for stage in stages:
            for copy in stage:
                copy.wait_send()


def image_call(patches, targets, weights, extra=(), group=16):
    comm = bool(extra)
    g1, b1, wqkv, bqv, wout, bout, g2, b2, wup, bup, wdown, bdown = weights
    count, cap, width = patches.shape
    ff = wup.shape[1]
    anys = pl.BlockSpec(memory_space=pl.ANY)
    vmem = pl.BlockSpec(memory_space=pltpu.VMEM)
    smem = pl.BlockSpec(memory_space=pltpu.SMEM)
    rows = count * group
    sds = jax.ShapeDtypeStruct
    out_shape = [sds((cap, width), F32)]
    out_specs = [vmem]
    in_specs = [anys] + [vmem] * 9 + [anys] * 4
    scratch = [
        pltpu.VMEM(patches.shape, BF),
        pltpu.VMEM(wqkv.shape, BF),
        pltpu.VMEM(wout.shape, BF),
        pltpu.VMEM(wup.shape, BF),
        pltpu.VMEM(wdown.shape, BF),
        pltpu.VMEM((rows, width), BF),
        pltpu.VMEM((3 * width // 128, rows, 128), F32),
        pltpu.VMEM((width // 128, rows, 128), F32),
        pltpu.VMEM((cap, ff), F32),
        pltpu.VMEM((cap, width), F32),
        pltpu.SemaphoreType.DMA((5,)),
    ]
    params = dict(vmem_limit_bytes=VMEM_LIMIT)
    if comm:
        chunks = 12
        piece = extra[1].shape
        in_specs += [anys] * 4 + [vmem] * 8 + [smem] * 2
        out_shape += [
            sds((chunks, NZ, NY, NC) + piece, BF),
            sds((NZ, NY, NC, 16, 128), BF),
            sds((cap, 128), F32),
        ]
        out_specs += [anys, vmem, vmem]
        scratch += [
            pltpu.VMEM((2, NZ, NY, NC, 8, 128), jnp.int32),
            pltpu.VMEM((NZ, NY, NC, 16, 128), BF),
            pltpu.VMEM((chunks,) + piece, BF),
            pltpu.SemaphoreType.DMA((chunks,)),
            pltpu.SemaphoreType.DMA((chunks, 13)),
            pltpu.SemaphoreType.DMA((chunks, 13)),
            pltpu.SemaphoreType.DMA((11,)),
            pltpu.SemaphoreType.DMA((11,)),
        ]
        params.update(collective_id=0, has_side_effects=True)
    return pl.pallas_call(
        functools.partial(image_body, comm, group),
        out_shape=out_shape,
        in_specs=in_specs,
        out_specs=out_specs,
        scratch_shapes=scratch,
        compiler_params=pltpu.CompilerParams(**params),
    )(patches, targets, g1, b1, bqv, bout, g2, b2, bup, bdown, wqkv, wout, wup, wdown, *extra)


class Reduce:
    def __init__(self, landing, split_bufs, whole_bufs, sems):
        self.landing, self.split_bufs, self.whole_bufs = landing, split_bufs, whole_bufs
        self.send, self.recv = sems
        self.x, self.z, self.y, self.c = place()
        self.far_z = [device(self.x, (self.z + j) % NZ, self.y, self.c) for j in range(1, NZ)]
        self.near_y = device(self.x, self.z, 1 - self.y, self.c)
        self.near_x = device(1 - self.x, self.z, self.y, self.c)
        self.twin = device(self.x, self.z, self.y, 1 - self.c)
        self.peers = self.far_z + [self.near_y, self.near_x, self.twin]
        self.plans = {}

    def add(self, k, grad, out):
        z, y, c = self.z, self.y, self.c
        full = slice(None)

        def copy(slot, src, dst, peer):
            return remote(src, dst, self.send.at[k, slot], self.recv.at[k, slot], peer)

        def start(items):
            for item in items:
                item.start()

        def wait(items):
            for item in items:
                item.wait()

        def add_into(target, value):
            target[...] = target[...] + value

        landed = self.landing(k)
        c0 = [copy(0, grad(full, full, 1 - c, full), landed, self.twin)]
        if k in WHOLE:
            n = WHOLE.index(k)
            in_y, in_z, mine, other = (buf.at[n] for buf in self.whole_bufs)
            c1 = [copy(1, grad(full, 1 - y, c, full), in_y, self.near_y)]
            c2 = [
                copy(1 + j, grad((z + j) % NZ, y, c, full), in_z.at[j - 1], self.far_z[j - 1]) for j in range(1, NZ)
            ]
            c3 = [copy(5, mine, other, self.near_x)]

            def s1():
                wait(c0)
                add_into(grad(full, full, c, full), landed[...])
                start(c1)

            def s2():
                wait(c1)
                add_into(grad(full, y, c, full), in_y[...])
                start(c2)

            def s3():
                wait(c2)
                total = grad(z, y, c, full)[...].astype(F32)
                for j in range(NZ - 1):
                    total = total + in_z[j].astype(F32)
                mine[...] = total.astype(BF)
                start(c3)

            def s4():
                wait(c3)
                out(pl.ds(0, mine.shape[-1]))[...] = mine[...].astype(F32) + other[...].astype(F32)

            self.plans[k] = [lambda: start(c0), s1, s2, s3, s4]
            return
        n = SPLIT.index(k)
        in_x, in_y, in_z, sum_x, other = (buf.at[n] for buf in self.split_bufs)
        half = sum_x.shape[-1]
        mine = pl.ds(pl.multiple_of(self.x * half, 128), half)
        theirs = pl.ds(pl.multiple_of((1 - self.x) * half, 128), half)
        c1 = [copy(1, grad(full, full, c, theirs), in_x, self.near_x)]
        c2 = [copy(2, grad(full, 1 - y, c, mine), in_y, self.near_y)]
        c3 = [copy(2 + j, grad((z + j) % NZ, y, c, mine), in_z.at[j - 1], self.far_z[j - 1]) for j in range(1, NZ)]
        c4 = [copy(6, sum_x, other, self.near_x)]

        def s1():
            wait(c0)
            add_into(grad(full, full, c, full), landed[...])
            start(c1)

        def s2():
            wait(c1)
            add_into(grad(full, full, c, mine), in_x[...])
            start(c2)

        def s3():
            wait(c2)
            add_into(grad(full, y, c, mine), in_y[...])
            start(c3)

        def s4():
            wait(c3)
            total = grad(z, y, c, mine)[...].astype(F32)
            for j in range(NZ - 1):
                total = total + in_z[j].astype(F32)
            rounded = total.astype(BF)
            sum_x[...] = rounded
            out(mine)[...] = rounded.astype(F32)
            start(c4)

        def s5():
            wait(c4)
            out(theirs)[...] = other[...].astype(F32)

        self.plans[k] = [lambda: start(c0), s1, s2, s3, s4, s5]

    def run(self, k, stage):
        self.plans[k][stage]()


def one_hot(rows, start, width, limit):
    i = lax.broadcasted_iota(jnp.int32, (rows, width), 0)
    j = lax.broadcasted_iota(jnp.int32, (rows, width), 1)
    return jnp.where((j == i + start) & (i < limit), 1.0, 0.0).astype(BF)


def spread_rows(all_small, vec_ref, bup_ref):
    width = vec_ref.shape[1]
    part = width // OWNERS
    tile = lambda o: all_small[o // 4, o // 2 % 2, o % 2]
    plain = jnp.zeros((16, width), F32)
    for o in range(OWNERS):
        plain = plain + dot(tile(o), one_hot(128, o * part, width, part))
    halves = []
    for h in range(2):
        total = jnp.zeros((16, width), F32)
        for m in range(8):
            total = total + dot(tile(8 * h + m), one_hot(128, 2 * m * part, width, 2 * part))
        halves.append(total[2:3])
    zero = jnp.zeros((1, width), F32)
    order = [plain[0:1], plain[1:2], halves[0], zero, halves[1], plain[3:4], plain[4:5], plain[5:6], plain[8:9]]
    vec_ref[...] = jnp.concatenate(order + [jnp.zeros((7, width), F32)], axis=0)
    first = [one_hot(128, 4 * m * part, width, 128) for m in range(4)]
    rest = [one_hot(128, 4 * m * part + 128, width, 4 * part - 128) for m in range(4)]
    for q in range(4):
        total = jnp.zeros((1, width), F32)
        for m in range(4):
            t = tile(4 * q + m)
            total = total + dot(t, first[m])[6:7] + dot(t, rest[m])[7:8]
        bup_ref[:, q * width : (q + 1) * width] = total


def own_rows(gvec, own_ref):
    width = gvec.shape[1]
    part = width // OWNERS
    me = lax.axis_index("fsdp")
    high = gvec.astype(BF)
    left = gvec - high.astype(F32)
    mid = left.astype(BF)
    low = (left - mid.astype(F32)).astype(BF)

    def pick(start, lanes):
        i = lax.broadcasted_iota(jnp.int32, (width, lanes), 0)
        j = lax.broadcasted_iota(jnp.int32, (width, lanes), 1)
        hot = jnp.where(i == j + start, 1.0, 0.0).astype(BF)
        return dot(high, hot) + dot(mid, hot) + dot(low, hot)

    plain = pick(me * part, 256)
    pair = pick(me % 8 * (2 * part), 256)
    four = pick(me % 4 * (4 * part), 256)
    qv = jnp.where(me < 8, pair[2:3], pair[4:5])
    q = me // 4
    bup = jnp.where(q == 0, four[12:13], jnp.where(q == 1, four[13:14], jnp.where(q == 2, four[14:15], four[15:16])))
    loss = jnp.broadcast_to(gvec[9:10, :1], (1, 256))
    rows = [plain[0:1], plain[1:2], qv, plain[5:6], plain[6:7], plain[7:8], plain[8:9], loss, bup]
    own_ref[...] = jnp.concatenate(rows + [jnp.zeros((7, 256), F32)], axis=0)


def text_body(comm, *refs):
    if comm:
        (x_ref, all_small, aim_ref, wgt_ref, len_ref, w_hbm), refs = refs[:6], refs[6:]
    else:
        (x_ref, vec_ref, bup_ref, aim_ref, wgt_ref, len_ref, w_hbm), refs = refs[:7], refs[7:]
    if comm:
        (y_hbm, dx_hbm, own_out, gqkv, gout, gup, gdown), refs = refs[:7], refs[7:]
    else:
        (y_hbm, dx_hbm, gvec_ref, grad_hbm), refs = refs[:4], refs[4:]
    (w_ref, wd_ref, h1_ref, qkv_ref, p_ref, ctx_ref, x1_ref, h2_ref, act_ref, slope_ref, asum_ref, lcol_ref, e_ref, et_ref,
     dy_ref, d_ref, da_ref, dmw_ref, sems), refs = refs[:19], refs[19:]
    tok, width = x_ref.shape
    cap = aim_ref.shape[0]
    seq = tok // cap
    ff = 4 * width
    blocks = tok // BLK
    pairs = width // 128
    tiles = width // TILE
    piece = w_ref.shape[-2]

    def chunk(k):
        return w_ref.at[k] if k < 8 else wd_ref.at[:, :, :, (k - 8) * piece : (k - 7) * piece]

    loads = [pltpu.make_async_copy(w_hbm.at[k], chunk(k), sems.at[k]) for k in range(12)]
    for load in loads:
        load.start()
    if comm:
        vec_ref, bup_ref, gvec_ref, *bufs, vecs, vec_in, vec_z, as0, as1, as2, as3, dms, down_mine, down_in, r_send, r_recv, v_send, v_recv, f_send, f_recv, free = refs
        split_bufs, whole_bufs = bufs[:5], bufs[5:]
        red = Reduce(
            lambda k: slope_ref.at[LANDING[k] // 2, LANDING[k] % 2], split_bufs, whole_bufs, (r_send, r_recv)
        )
        outs = [gqkv, gqkv, gqkv, gout, gup, gup, gup, gup]

        def view(k):
            if k >= 4:
                rows = slice((k - 4) * piece, (k - 3) * piece)
                return lambda a, b, d, lanes: wd_ref.at[a, b, d, rows, lanes]
            n = 3 if k == 3 else 4 + k
            return lambda a, b, d, lanes: w_ref.at[n, a, b, d, :, lanes]

        def result(k):
            base = (0, 1, 2, 0, 0, 1, 2, 3)[k] * width
            return lambda lanes: outs[k].at[:, pl.ds(pl.multiple_of(base + lanes.start, 128), lanes.size)]

        for k in range(8):
            red.add(k, view(k), result(k))
        z, y_at, c = red.z, red.y, red.c

        def side(slot, src, dst, peer):
            return remote(src, dst, f_send.at[slot], f_recv.at[slot], peer)

        to_twin = [side(0, as0.at[:, :, 1 - c], as1.at[:, :, c], red.twin)]
        to_y = [side(1, as1.at[:, 1 - y_at], as2.at[:, y_at], red.near_y)]
        to_z = [side(2 + j, as2.at[(z + 1 + j) % NZ], as3.at[z], peer) for j, peer in enumerate(red.far_z)]
        dm_z = [side(5 + j, dms.at[z, y_at, c], dms.at[z, y_at, c], peer) for j, peer in enumerate(red.far_z)]
        dm_y = [side(8, dms.at[:, y_at, c], dms.at[:, y_at, c], red.near_y)]
        dm_twin = [side(9, dms.at[:, :, c], dms.at[:, :, c], red.twin)]
        down_x = [side(10, down_mine, down_in, red.near_x)]

        def begin(copies):
            for item in copies:
                item.start()

        def end(copies):
            for item in copies:
                item.wait()

        greet(red.peers)
        run = red.run
        spread_rows(all_small, vec_ref, bup_ref)
    else:

        def run(k, stage):
            pass

    vec = lambda i: vec_ref[i : i + 1, :]
    rows_at = lambda b: pl.ds(pl.multiple_of(b * BLK, BLK), BLK)

    for i in range(cap):
        lcol_ref[i : i + 1, :] = jnp.full((1, 128), len_ref[i], jnp.int32)
    lcol = lcol_ref[:, :1]
    t_lane = lax.broadcasted_iota(jnp.int32, (cap, tok), 1)
    c_row = lax.broadcasted_iota(jnp.int32, (cap, tok), 0)
    pool = jnp.where((t_lane // seq == c_row) & (t_lane % seq < lcol), 1.0, 0.0)
    e_ref[...] = pool.astype(BF)
    et_ref[...] = jnp.concatenate([pool, pool, jnp.zeros((128 - 2 * cap, tok), F32)], axis=0).T.astype(BF)
    d_ref[2 * cap :, :] = jnp.zeros_like(d_ref[2 * cap :, :])

    def norm_one(b, _):
        n, _r = norm_rows(x_ref[rows_at(b), :].astype(F32))
        h1_ref[rows_at(b), :] = (n * vec(0) + vec(1)).astype(BF)
        return 0

    lax.fori_loop(0, blocks, norm_one, 0)

    def weight(k, cols):
        return w_ref[k, :, :, :, :, cols].reshape(width, -1)

    for part in range(3):
        loads[part].wait()
        for n in range(tiles):
            cols = slice(n * TILE, n * TILE + TILE)
            value = dot(h1_ref[...], weight(part, cols)) + vec_ref[2 + part : 3 + part, cols]
            qkv_ref[:, part * width + n * TILE : part * width + n * TILE + TILE] = value.astype(BF)

    lane = lax.broadcasted_iota(jnp.int32, (BLK, 128), 1)
    low_half = lane < HEAD
    live_lane = jnp.sum(pool, axis=0, keepdims=True)

    def both_heads(v):
        zero = jnp.zeros_like(v)
        return jnp.concatenate([jnp.where(low_half, v, zero), jnp.where(low_half, zero, v)], axis=0)

    def pick(v):
        return jnp.where(low_half, v[:BLK], v[BLK:])

    same = (lax.broadcasted_iota(jnp.int32, (2 * BLK, BLK), 0) % BLK) // seq == lax.broadcasted_iota(
        jnp.int32, (2 * BLK, BLK), 1
    ) // seq
    for b in range(blocks):
        key_ok = same & (live_lane[:, b * BLK : b * BLK + BLK] > 0.5)
        rows = slice(b * BLK, b * BLK + BLK)
        heads = range(pairs)
        part = lambda n, h: qkv_ref[rows, n * width + h * 128 : n * width + h * 128 + 128]
        ss = [jnp.where(key_ok, dot_nt(both_heads(part(0, h)), part(1, h)), DEAD) for h in heads]
        tops = [jnp.max(s, axis=-1, keepdims=True) for s in ss]
        es = [jnp.exp((s - top) * 0.125) for s, top in zip(ss, tops)]
        sums = [jnp.sum(e, axis=-1, keepdims=True) for e in es]
        ps = [e / total for e, total in zip(es, sums)]
        for h in heads:
            p_ref[b * pairs + h] = ps[h]
        os = [dot(ps[h].astype(BF), part(2, h)) for h in heads]
        for h in heads:
            ctx_ref[rows, h * 128 : h * 128 + 128] = pick(os[h]).astype(BF)

    loads[3].wait()
    for n in range(tiles):
        cols = slice(n * TILE, n * TILE + TILE)
        x1_ref[:, cols] = x_ref[:, cols].astype(F32) + dot(ctx_ref[...], weight(3, cols)) + vec_ref[5:6, cols]

    def norm_two(b, _):
        n, _r = norm_rows(x1_ref[rows_at(b), :])
        h2_ref[rows_at(b), :] = (n * vec(6) + vec(7)).astype(BF)
        return 0

    lax.fori_loop(0, blocks, norm_two, 0)
    for n in range(ff // TILE):
        k, off = divmod(n * TILE, width)
        if off == 0:
            loads[4 + k].wait()
        cols = slice(n * TILE, n * TILE + TILE)
        inner = slice(off, off + TILE)
        pre = dot(h2_ref[...], weight(4 + k, inner)) + bup_ref[:, cols]
        half_slope = 0.5 * (1.0 + lax.erf(pre * ROOT_HALF))
        act = (pre * half_slope).astype(BF)
        slope = (half_slope + pre * jnp.exp(-0.5 * pre * pre) * INV_ROOT_TAU).astype(BF)
        slope_ref[k, :, :, :, :, inner] = slope.reshape(slope_ref.shape[1:-1] + (TILE,))
        act_ref[:, cols] = act

    for k in range(4):
        total = dot(e_ref[...], act_ref[:, k * width : (k + 1) * width])
        if comm:
            for o in range(4):
                own = total[:, o * 4 * piece : (o + 1) * 4 * piece]
                own = jnp.concatenate([own, jnp.zeros((cap, 256 - 4 * piece), F32)], axis=1)
                as0[k, o // 2, o % 2] = own.astype(BF)
        else:
            hi, lo = split(total)
            asum_ref[:cap, k * width : (k + 1) * width] = hi
            asum_ref[cap:, k * width : (k + 1) * width] = lo
    if comm:
        begin(to_twin)
        as1[:, :, c] = as0[:, :, c]
    h2_ref[...] = h2_ref[...].T
    for load in loads[8:]:
        load.wait()
    lens = lcol.astype(F32)
    wgt = wgt_ref[:, :1]
    loss = jnp.zeros((1, TILE), F32)
    for n in range(tiles):
        cols = slice(n * TILE, n * TILE + TILE)
        y = x1_ref[:, cols] + vec_ref[8:9, cols]
        for k in range(NZ):
            y = y + dot(act_ref[:, k * width : k * width + width], wd_ref[k, :, :, :, cols].reshape(width, TILE))
        hi, lo = split(y)
        da_ref[:, cols] = hi
        error = (dot(e_ref[...], hi) + dot(e_ref[...], lo)) / lens - aim_ref[:, cols]
        loss = loss + jnp.sum(wgt * error * error, axis=0, keepdims=True)
        dpool = 2.0 * wgt * error / lens
        dy_hi, dy_lo = split(dpool)
        d_ref[:cap, cols] = dy_hi
        d_ref[cap : 2 * cap, cols] = dy_lo
        gvec_ref[8:9, cols] = jnp.sum(dy_hi.astype(F32) * lens, axis=0, keepdims=True)
        if comm:
            dms[z, y_at, c, :, cols] = dy_hi
            if n == 1:
                end(to_twin)
                begin(to_y)
                as2[:, y_at] = as1[:, y_at]
            elif n == tiles - 1:
                begin(dm_z)
    y_out = pltpu.make_async_copy(da_ref, y_hbm, sems.at[12])
    y_out.start()
    gvec_ref[3:4, :] = jnp.zeros((1, width), F32)
    gvec_ref[9:10, :] = jnp.broadcast_to(jnp.sum(loss, axis=1, keepdims=True), (1, width))
    gvec_ref[10:12, :] = jnp.zeros((2, width), F32)

    dm = d_ref[:cap, :]
    span = ff // 8
    pad = jnp.zeros((128 - 2 * cap, span), BF)
    for n in range(8):
        hi, lo = split(dot_nt(dm, wd_ref[n // 2, n % 2].reshape(span, width)))
        dmw_ref[:cap, n * span : (n + 1) * span] = hi
        dmw_ref[cap : 2 * cap, n * span : (n + 1) * span] = lo
        dmw_ref[2 * cap :, n * span : (n + 1) * span] = pad
    for k in range(4):
        for n in range(tiles):
            at = k * width + n * TILE
            cols = slice(n * TILE, n * TILE + TILE)
            slope = slope_ref[k, :, :, :, :, cols].reshape(tok, TILE)
            dpre = (dot(et_ref[...], dmw_ref[:, at : at + TILE]) * slope.astype(F32)).astype(BF)
            gvec_ref[12 + k : 13 + k, cols] = jnp.sum(dpre.astype(F32), axis=0, keepdims=True)
            act_ref[:, at : at + TILE] = dpre
            wd_ref[:, :, :, k * piece : (k + 1) * piece, cols] = (
                dot(h2_ref[...], dpre).astype(BF).reshape(NZ, NY, NC, piece, TILE)
            )
        if comm:
            pl.semaphore_signal(free, inc=1, device_id=red.twin, device_id_type=MESH)
            if k == 0:
                end(to_y)
                begin(to_z)
                as3[z] = as2[z]
            if k == 1:
                end(dm_z)
                begin(dm_y)
            if k % 2 == 0:
                pl.semaphore_wait(free, 1)
        run(4 + k, 0)
        if k > 0:
            run(3 + k, 1)
    for n in range(tiles):
        total = jnp.zeros((tok, TILE), F32)
        for k in range(4):
            w_rows = w_ref[4 + k].reshape(width, width)[n * TILE : n * TILE + TILE]
            total = total + dot_nt(act_ref[:, k * width : k * width + width], w_rows)
        dy_ref[:, n * TILE : n * TILE + TILE] = total
        if n == 0:
            run(7, 1)
        elif n == 2:
            run(4, 2)
    if not comm:
        dm2 = jnp.concatenate([dm, dm], axis=0)
        per = ff // OWNERS
        for o in range(OWNERS):
            lo, hi = o * per // 128 * 128, (o * per + per + 127) // 128 * 128
            g = dot_tn(asum_ref[:, lo:hi], dm2)[o * per - lo : o * per - lo + per].astype(BF)
            for k in range(4):
                slope_ref[k, o % 2, o // 4, o // 2 % 2] = g[k * piece : (k + 1) * piece]
    y_out.wait()

    def two_back(b, sums):
        g_gain, g_bias, g_out = sums
        dh = dy_ref[rows_at(b), :]
        n2, r2 = norm_rows(x1_ref[rows_at(b), :])
        dx1 = dot(et_ref[rows_at(b), :], d_ref[...]) + norm_back(dh * vec(6), n2, r2)
        dy_ref[rows_at(b), :] = dx1
        da = dx1.astype(BF)
        da_ref[rows_at(b), :] = da
        return (
            g_gain + jnp.sum(dh * n2, axis=0, keepdims=True),
            g_bias + jnp.sum(dh, axis=0, keepdims=True),
            g_out + jnp.sum(da.astype(F32), axis=0, keepdims=True),
        )

    zero_row = jnp.zeros((1, width), F32)
    sums = lax.fori_loop(0, blocks, two_back, (zero_row,) * 3)
    gvec_ref[6:7, :] = sums[0]
    gvec_ref[7:8, :] = sums[1]
    gvec_ref[5:6, :] = sums[2]
    run(5, 2)
    if comm:
        end(dm_y)
        begin(dm_twin)
    for n in range(tiles):
        w_rows = w_ref[3].reshape(width, width)[n * TILE : n * TILE + TILE]
        h2_ref[:, n * TILE : n * TILE + TILE] = dot_nt(da_ref[...], w_rows).astype(BF)
    ctx_ref[...] = ctx_ref[...].T
    for n in range(tiles):
        cols = slice(n * TILE, n * TILE + TILE)
        w_ref[3, :, :, :, :, cols] = dot(ctx_ref[...], da_ref[:, cols]).astype(BF).reshape(w_ref.shape[1:-1] + (TILE,))
    if comm:
        pl.semaphore_wait(free, 1)
    run(3, 0)
    for b in range(blocks):
        rows = slice(b * BLK, b * BLK + BLK)
        heads = range(pairs)
        at = lambda n, h: slice(n * width + h * 128, n * width + h * 128 + 128)
        ps = [p_ref[b * pairs + h] for h in heads]
        dcs = [both_heads(h2_ref[rows, at(0, h)]) for h in heads]
        dps = [dot_nt(dcs[h], qkv_ref[rows, at(2, h)]) for h in heads]
        sums = [jnp.sum(ps[h] * dps[h], axis=-1, keepdims=True) for h in heads]
        dss = [(ps[h] * (dps[h] - sums[h])).astype(BF) for h in heads]
        dqs = [pick(dot(dss[h], qkv_ref[rows, at(1, h)])) * 0.125 for h in heads]
        dks = [dot_tn(dss[h], both_heads(qkv_ref[rows, at(0, h)])) * 0.125 for h in heads]
        dvs = [dot_tn(ps[h].astype(BF), dcs[h]) for h in heads]
        for h in heads:
            qkv_ref[rows, at(0, h)] = dqs[h].astype(BF)
            qkv_ref[rows, at(1, h)] = dks[h].astype(BF)
            qkv_ref[rows, at(2, h)] = dvs[h].astype(BF)
        for k, stage in BACK_STEPS[b]:
            run(k, stage)
        if comm and b == 2:
            end(dm_twin)
            end(to_z)
            g = dot_tn(as3[...].reshape(OWNERS * cap, 256), dms[...].reshape(OWNERS * cap, width))
            down_mine[...] = g[: 4 * piece].astype(BF)
            begin(down_x)
    h1_ref[...] = h1_ref[...].T
    for k in range(3):
        for n in range(tiles):
            cols = slice(n * TILE, n * TILE + TILE)
            d = qkv_ref[:, k * width + n * TILE : k * width + n * TILE + TILE]
            gvec_ref[2 + k : 3 + k, cols] = jnp.sum(d.astype(F32), axis=0, keepdims=True)
            w_ref[4 + k, :, :, :, :, cols] = dot(h1_ref[...], d).astype(BF).reshape(w_ref.shape[1:-1] + (TILE,))
        if comm and k == 1:
            pl.semaphore_wait(free, 1)
        run(k, 0)
        if k > 0:
            run(k - 1, 1)
    for n in range(tiles):
        total = jnp.zeros((tok, TILE), F32)
        for k in range(3):
            w_rows = w_ref[k].reshape(width, width)[n * TILE : n * TILE + TILE]
            total = total + dot_nt(qkv_ref[:, k * width : k * width + width], w_rows)
        x1_ref[:, n * TILE : n * TILE + TILE] = total
        for k, stage in (((2, 1),), ((3, 3), (4, 4)), ((5, 4), (6, 4)))[n]:
            run(k, stage)

    def one_back(b, sums):
        g_gain, g_bias = sums
        dh = x1_ref[rows_at(b), :]
        n1, r1 = norm_rows(x_ref[rows_at(b), :].astype(F32))
        dy_ref[rows_at(b), :] = dy_ref[rows_at(b), :] + norm_back(dh * vec(0), n1, r1)
        return (g_gain + jnp.sum(dh * n1, axis=0, keepdims=True), g_bias + jnp.sum(dh, axis=0, keepdims=True))

    sums = lax.fori_loop(0, blocks, one_back, (zero_row,) * 2)
    gvec_ref[0:1, :] = sums[0]
    gvec_ref[1:2, :] = sums[1]
    dx_out = pltpu.make_async_copy(dy_ref, dx_hbm, sems.at[13])
    dx_out.start()
    if comm:

        def small(slot, src, dst, peer):
            return remote(src, dst, v_send.at[slot], v_recv.at[slot], peer)

        steps = [
            small(0, vecs.at[0], vec_in.at[0], red.twin),
            small(1, vecs.at[1], vec_in.at[1], red.near_y),
            small(2, vecs.at[2], vec_in.at[2], red.near_x),
        ]
        spread = [small(3 + j, vec_z.at[red.z], vec_z.at[red.z], peer) for j, peer in enumerate(red.far_z)]
        vecs[0] = gvec_ref[...]
        steps[0].start()
        run(0, 2)
        run(1, 2)
        steps[0].wait()
        vecs[1] = vecs[0] + vec_in[0]
        steps[1].start()
        for k, stage in ((3, 4), (7, 4), (4, 5), (6, 5), (2, 2)):
            run(k, stage)
        steps[1].wait()
        vecs[2] = vecs[1] + vec_in[1]
        steps[2].start()
        run(0, 3)
        run(1, 3)
        end(down_x)
        gdown[...] = down_mine[...].astype(F32) + down_in[...].astype(F32)
        steps[2].wait()
        vec_z[red.z] = vecs[2] + vec_in[2]
        for item in spread:
            item.start()
        run(2, 3)
        run(3, 5)
        run(1, 4)
        run(0, 4)
        for item in spread:
            item.wait()
        own_rows(vec_z[0] + vec_z[1] + vec_z[2] + vec_z[3], own_out)
        run(2, 4)
        run(0, 5)
    else:
        copies = [pltpu.make_async_copy(w_ref.at[3 if k == 3 else 4 + k], grad_hbm.at[k], sems.at[k]) for k in range(4)]
        for k in range(4):
            rows = slice(k * piece, (k + 1) * piece)
            copies.append(pltpu.make_async_copy(wd_ref.at[:, :, :, rows], grad_hbm.at[4 + k], sems.at[4 + k]))
            for c in range(NC):
                copies.append(
                    pltpu.make_async_copy(slope_ref.at[k, c], grad_hbm.at[8 + k, :, :, c], sems.at[14 + 2 * k + c])
                )
        for copy in copies:
            copy.start()
        for copy in copies:
            copy.wait()
    dx_out.wait()


def text_call(comm, x, smalls, aim, wgt, lens, packed):
    tok, width = x.shape
    cap = aim.shape[0]
    ff = 4 * width
    piece = packed.shape[-2]
    anys = pl.BlockSpec(memory_space=pl.ANY)
    vmem = pl.BlockSpec(memory_space=pltpu.VMEM)
    smem = pl.BlockSpec(memory_space=pltpu.SMEM)
    sds = jax.ShapeDtypeStruct
    out_shape = [sds((tok, width), BF), sds((tok, width), F32), sds((16, 256 if comm else width), F32)]
    out_specs = [anys, anys, vmem]
    eight = (8, NZ, NY, NC, piece, width)
    scratch = [
        pltpu.VMEM(eight, BF),
        pltpu.VMEM((NZ, NY, NC, 4 * piece, width), BF),
        pltpu.VMEM((tok, width), BF),
        pltpu.VMEM((tok, 3 * width), BF),
        pltpu.VMEM((tok // BLK * (width // 128), 2 * BLK, BLK), F32),
        pltpu.VMEM((tok, width), BF),
        pltpu.VMEM((tok, width), F32),
        pltpu.VMEM((tok, width), BF),
        pltpu.VMEM((tok, ff), BF),
        pltpu.VMEM((ff // width, 2, NZ, NY, tok // 16, width), BF),
        pltpu.VMEM((2 * cap, ff), BF),
        pltpu.VMEM((cap, 128), jnp.int32),
        pltpu.VMEM((cap, tok), BF),
        pltpu.VMEM((tok, 128), BF),
        pltpu.VMEM((tok, width), F32),
        pltpu.VMEM((128, width), BF),
        pltpu.VMEM((tok, width), BF),
        pltpu.VMEM((128, ff), BF),
        pltpu.SemaphoreType.DMA((22,)),
    ]
    params = dict(vmem_limit_bytes=VMEM_LIMIT)
    if comm:
        out_shape += [
            sds((piece, 3 * width), F32), sds((piece, width), F32), sds((piece, ff), F32), sds((4 * piece, width), F32),
        ]
        out_specs += [vmem] * 4
        scratch += [
            pltpu.VMEM((16, width), F32),
            pltpu.VMEM((1, ff), F32),
            pltpu.VMEM((16, width), F32),
            pltpu.VMEM((4, NZ, NY, piece, width // 2), BF),
            pltpu.VMEM((4, NZ, piece, width // 2), BF),
            pltpu.VMEM((4, NZ - 1, piece, width // 2), BF),
            pltpu.VMEM((4, piece, width // 2), BF),
            pltpu.VMEM((4, piece, width // 2), BF),
            pltpu.VMEM((4, NZ, piece, width), BF),
            pltpu.VMEM((4, NZ - 1, piece, width), BF),
            pltpu.VMEM((4, piece, width), BF),
            pltpu.VMEM((4, piece, width), BF),
            pltpu.VMEM((3, 16, width), F32),
            pltpu.VMEM((3, 16, width), F32),
            pltpu.VMEM((NZ, 16, width), F32),
            *[pltpu.VMEM((NZ, NY, NC, cap, 256), BF)] * 4,
            pltpu.VMEM((NZ, NY, NC, cap, width), BF),
            pltpu.VMEM((4 * piece, width), BF),
            pltpu.VMEM((4 * piece, width), BF),
            pltpu.SemaphoreType.DMA((8, 7)),
            pltpu.SemaphoreType.DMA((8, 7)),
            pltpu.SemaphoreType.DMA((6,)),
            pltpu.SemaphoreType.DMA((6,)),
            pltpu.SemaphoreType.DMA((11,)),
            pltpu.SemaphoreType.DMA((11,)),
            pltpu.SemaphoreType.REGULAR,
        ]
        params.update(collective_id=1, has_side_effects=True)
    else:
        out_shape += [sds(packed.shape, BF)]
        out_specs += [anys]
    return pl.pallas_call(
        functools.partial(text_body, comm),
        out_shape=out_shape,
        in_specs=[vmem] * (3 + len(smalls)) + [smem, anys],
        out_specs=out_specs,
        scratch_shapes=scratch,
        compiler_params=pltpu.CompilerParams(**params),
    )(x, *smalls, aim, wgt, lens, packed)


def pack(wqkv, wout, wup, wdown):
    width = wout.shape[1]
    parts = [wqkv[:, k * width : (k + 1) * width] for k in range(3)] + [wout]
    parts += [wup[:, k * width : (k + 1) * width] for k in range(4)]
    down = wdown.reshape(OWNERS, 4, width // OWNERS, width)
    parts += [down[:, k].reshape(width, width) for k in range(4)]
    return jnp.stack(parts).reshape(12, NZ, NY, NC, width // OWNERS, width)


def unpack(packed):
    width = packed.shape[-1]
    flat = packed.reshape(12, width, width)
    wqkv = jnp.concatenate([flat[k] for k in range(3)], axis=1)
    wup = jnp.concatenate([flat[4 + k] for k in range(4)], axis=1)
    down = flat[8:].reshape(4, OWNERS, width // OWNERS, width)
    return wqkv, flat[3], wup, jnp.swapaxes(down, 0, 1).reshape(4 * width, width)


def vectors(g1, b1, bqv, bout, g2, b2, bup, bdown):
    width = g1.shape[0]
    zero = jnp.zeros((width,), BF)
    rows = [g1, b1, bqv[:width], zero, bqv[width:], bout, g2, b2, bdown] + [zero] * 7
    return jnp.stack(rows).astype(F32), bup.astype(F32).reshape(1, -1)


def hand_out_body(part, *refs):
    big, own, outs, bufs, sem_in, sem_out = refs[:6], refs[6], refs[7:22], refs[22:28], refs[28], refs[29]
    loss, y, dx, g1, b1, gqkv, qv, gout, bout, g2, b2, gup, bup, gdown, bdown = outs
    pairs = list(zip(big, bufs, (y, dx, gqkv, gout, gup, gdown)))
    ins, backs = [], []
    for i, (src, buf, dst) in enumerate(pairs):
        pieces = 4 if i < 2 else 1
        n = src.shape[0] // pieces
        for p in range(pieces):
            rows = pl.ds(p * n, n)
            slot = 4 * i + p
            ins.append(pltpu.make_async_copy(src.at[rows], buf.at[rows], sem_in.at[slot]))
            backs.append(pltpu.make_async_copy(buf.at[rows], dst.at[rows], sem_out.at[slot]))
    for copy in ins:
        copy.start()
    for ref, at, lanes in (
        (g1, 0, part), (b1, 1, part), (qv, 2, 2 * part), (bout, 3, part), (g2, 4, part), (b2, 5, part), (bdown, 6, part),
        (bup, 8, 4 * part),
    ):
        ref[...] = own[at : at + 1, :lanes].reshape(lanes)
    loss[...] = own[7:8, :1]
    for copy, back in zip(ins, backs):
        copy.wait()
        back.start()
    for back in backs:
        back.wait()


def hand_out(big, own, part):
    sds = jax.ShapeDtypeStruct
    anys = pl.BlockSpec(memory_space=pl.ANY)
    vmem = pl.BlockSpec(memory_space=pltpu.VMEM)
    like = lambda v: sds(v.shape, v.dtype)
    line = lambda n: sds((n * part,), F32)
    y, dx, gqkv, gout, gup, gdown = big
    return pl.pallas_call(
        functools.partial(hand_out_body, part),
        out_shape=[
            sds((1, 1), F32), like(y), like(dx), line(1), line(1), like(gqkv), line(2), like(gout), line(1), line(1),
            line(1), like(gup), line(4), like(gdown), line(1),
        ],
        in_specs=[anys] * 6 + [vmem],
        out_specs=[vmem, anys, anys, vmem, vmem, anys, vmem, anys, vmem, vmem, vmem, anys, vmem, anys, vmem],
        scratch_shapes=[pltpu.VMEM(v.shape, v.dtype) for v in big]
        + [pltpu.SemaphoreType.DMA((24,)), pltpu.SemaphoreType.DMA((24,))],
        compiler_params=pltpu.CompilerParams(vmem_limit_bytes=VMEM_LIMIT),
    )(*big, own)


def group_weight(group_ids, live):
    match = group_ids[:, None] == jnp.arange(1024, dtype=jnp.int32)[None, :]
    local = jnp.sum(jnp.where(match & live[:, None], 1.0, 0.0).astype(F32), axis=0)
    size = lax.psum(local, ("dp", "fsdp"))
    members = jnp.sum(jnp.where(match, size[None, :], 0.0), axis=1)
    return jnp.where(live, 1.0 / jnp.maximum(members, 1.0), 0.0)


def any_mesh(text, weights, image_weights, patches, targets, group_ids, cap_len, slot_counts):
    cap = targets.shape[0]
    gathered = [lax.all_gather(w, "fsdp", axis=0, tiled=True) for w in weights]
    g1, b1, wqkv, bqv, wout, bout, g2, b2, wup, bup, wdown, bdown = gathered
    live = jnp.arange(cap, dtype=jnp.int32) < slot_counts[0]
    wgt = group_weight(group_ids, live)
    (aim,) = image_call(patches, targets, image_weights)
    vec, bup_row = vectors(g1, b1, bqv, bout, g2, b2, bup, bdown)
    y, dx, gvec, packed = text_call(
        False, text, (vec, bup_row), aim, jnp.broadcast_to(wgt[:, None], (cap, 128)), cap_len, pack(wqkv, wout, wup, wdown)
    )
    gqkv, gout, gup, gdown = unpack(packed)
    grads = [
        gvec[0], gvec[1], gqkv, jnp.concatenate([gvec[2], gvec[4]]), gout, gvec[5], gvec[6], gvec[7], gup,
        gvec[12:16].reshape(-1), gdown, gvec[8],
    ]
    owned = [lax.psum_scatter(g.astype(F32), "fsdp", scatter_dimension=0, tiled=True) for g in grads]
    return (lax.psum(gvec[9, 0], ("dp", "fsdp")), y, dx, *[lax.psum(g, "dp") for g in owned])


def block_mesh(text, weights, image_weights, patches, targets, group_ids, cap_len, slot_counts):
    g1, b1, wqkv, bqv, wout, bout, g2, b2, wup, bup, wdown, bdown = weights
    width = wout.shape[1]
    aim, packed, all_small, wgt = image_call(
        patches, targets, image_weights, (wqkv, wout, wup, wdown, g1, b1, bqv, bout, g2, b2, bup, bdown, group_ids, slot_counts)
    )
    y, dx, gvec, gqkv, gout, gup, gdown = text_call(True, text, (all_small,), aim, wgt, cap_len, packed)
    part = width // OWNERS
    loss, y, dx, g1, b1, gqkv, qv, gout, bout, g2, b2, gup, bup, gdown, bdown = hand_out(
        (y, dx, gqkv, gout, gup, gdown), gvec, part
    )
    return loss[0, 0], y, dx, g1, b1, gqkv, qv, gout, bout, g2, b2, gup, bup, gdown, bdown


def solution(mesh):
    shape = dict(mesh.shape)
    inner = block_mesh if (shape["dp"], shape["fsdp"]) == (2, OWNERS) else any_mesh

    def per_device(text_in, *rest):
        weights, image_weights = rest[:12], rest[12:24]
        patches, targets, group_ids, cap_len, slot_counts = rest[24:]
        return inner(
            text_in, weights, image_weights, jnp.transpose(patches, (1, 0, 2)), targets, group_ids, cap_len, slot_counts
        )

    both = ("dp", "fsdp")
    owned, table = P("fsdp"), P("fsdp", None)
    text_specs = (owned, owned, table, owned, table, owned, owned, owned, table, owned, table, owned)
    return jax.shard_map(
        per_device,
        mesh=mesh,
        in_specs=(P(both, None), *text_specs, *([P()] * 12), P(both, None, None), P(both, None), P(both), P(both), P(both)),
        out_specs=(P(), P(both, None), P(both, None), *text_specs),
        check_vma=False,
    )
```
